32 devices in a mesh: seq: 16 (over z, y, x), row: 2 (over core).
Axes of the slice: x: 2, y: 2, z: 4, core: 2. Of those that a mesh axis runs over, the one named last changes fastest.
Arguments:
- block_input: bfloat16 [4, 2048, 2048], P('row', 'seq'), may hold values from -6 to 6
- out_grad: bfloat16 [4, 2048, 2048], P('row', 'seq'), may hold values from -6 to 6
- doc_starts: int32 [4, 4], P('row'), may hold values from 0 to 2047, as said below
- w_query: bfloat16 [2048, 2048], P(('seq', 'row')), may hold values from -0.125 to 0.125
- w_forget: bfloat16 [2048, 2048], P(('seq', 'row')), may hold values from -0.125 to 0.125
- w_input: bfloat16 [2048, 2048], P(('seq', 'row')), may hold values from -0.125 to 0.125
- w_outgate: bfloat16 [2048, 2048], P(('seq', 'row')), may hold values from -0.125 to 0.125
- w_out: bfloat16 [2048, 2048], P(('seq', 'row')), may hold values from -0.125 to 0.125
- w_gate: bfloat16 [2048, 5632], P('seq', 'row'), may hold values from -0.125 to 0.125
- w_up: bfloat16 [2048, 5632], P('seq', 'row'), may hold values from -0.125 to 0.125
- w_down: bfloat16 [5632, 2048], P('row', 'seq'), may hold values from -0.078125 to 0.078125
- norm_gain: bfloat16 [2048], P(('seq', 'row')), may hold values from 0.5 to 1.5
- mlp_gain: bfloat16 [2048], P(('seq', 'row')), may hold values from 0.5 to 1.5
- group_gain: bfloat16 [2048], P(('seq', 'row')), may hold values from 0.5 to 1.5
- forget_bias: bfloat16 [2048], P(('seq', 'row')), may hold values from -1.5 to 9.5
Outputs:
- block_output: bfloat16 [4, 2048, 2048], P('row', 'seq')
- input_grad: bfloat16 [4, 2048, 2048], P('row', 'seq')
- grad_query: float32 [2048, 2048], P(('seq', 'row'))
- grad_forget: float32 [2048, 2048], P(('seq', 'row'))
- grad_input: float32 [2048, 2048], P(('seq', 'row'))
- grad_outgate: float32 [2048, 2048], P(('seq', 'row'))
- grad_out: float32 [2048, 2048], P(('seq', 'row'))
- grad_gate: float32 [2048, 5632], P('seq', 'row')
- grad_up: float32 [2048, 5632], P('seq', 'row')
- grad_down: float32 [5632, 2048], P('row', 'seq')
- grad_norm_gain: float32 [2048], P(('seq', 'row'))
- grad_mlp_gain: float32 [2048], P(('seq', 'row'))
- grad_group_gain: float32 [2048], P(('seq', 'row'))
- grad_forget_bias: float32 [2048], P(('seq', 'row'))
The draws below stay inside these ranges and needn't reach their ends.
Inputs may be any that keep to these rules, and one draw needn't show every extreme that they name: `doc_starts`: the first entry of every row is 0 and entries may repeat; in every aligned block of 2 rows one row has all entries 0.
All inputs are finite; a program needn't handle non-finite values.
Results may differ from the reference program's by a relative error of at most 0.013.
Values may be sent and summed in bfloat16 or wider, within the bound.
No kernel may reach another device: no remote copies, remote signals or barrier semaphores. Data moves between devices by JAX's collectives and lax.ppermute only.
A program may use at most 512 MiB of HBM per device.

```python
import jax
import jax.numpy as jnp
from jax import lax

D = 2048
HEADS = 16
FF = 5632
SPAN = 128
ROWS_DEV = 2
NSTART = 4
ROWS = 4
LENGTH = 2048


def draw_doc_starts(key, part):
    key = jax.random.fold_in(key, 11)
    split_keys = jax.random.split(key, 2)
    later_starts = jax.random.randint(split_keys[0], (ROWS, NSTART - 1), 1, LENGTH, dtype=jnp.int32)
    starts = jnp.concatenate([jnp.zeros((ROWS, 1), jnp.int32), later_starts], axis=1)
    block_count = ROWS // ROWS_DEV
    picked = jax.random.randint(split_keys[1], (block_count,), 0, ROWS_DEV, dtype=jnp.int32)
    row_ids = jnp.arange(ROWS, dtype=jnp.int32)
    chosen = picked[row_ids // ROWS_DEV] == row_ids % ROWS_DEV
    starts = jnp.where(chosen[:, None], 0, starts)
    far_row = (picked[0] + 1) % ROWS_DEV
    starts = starts.at[far_row, 1].set(LENGTH - 1)
    return starts


def draw_forget_bias(key, part):
    key = jax.random.fold_in(key, 23)
    split_keys = jax.random.split(key, 3)
    slow_share = 0.5
    head_draws = jax.random.uniform(split_keys[0], (HEADS,), jnp.float32)
    slow_heads = (head_draws < slow_share) | (head_draws == jnp.min(head_draws))
    slow_heads = slow_heads & (head_draws != jnp.max(head_draws))
    per_channel = jnp.repeat(slow_heads, D // HEADS)
    fast_values = jax.random.uniform(split_keys[1], (D,), jnp.float32, -1.5, 1.5)
    slow_values = jax.random.uniform(split_keys[2], (D,), jnp.float32, 7.0, 9.5)
    return jnp.where(per_channel, slow_values, fast_values).astype(jnp.bfloat16)


def block_levels(rng, dims, cuts, smallest, high):
    loudness, own = 1.0, jax.random.fold_in(rng, 6)
    for axis_at, blocks in cuts:
        heights = jnp.exp(jax.random.uniform(jax.random.fold_in(own, axis_at), (blocks,), jnp.float32, smallest / len(cuts), high / len(cuts)))
        loudness = loudness * jnp.repeat(heights, dims[axis_at] // blocks).reshape([-1 if axis == axis_at else 1 for axis in range(len(dims))])
    return loudness


def bell_draw(stream_key, dims, spread, most, cuts=(), held_as=jnp.bfloat16):
    factor_of = block_levels(stream_key, dims, cuts, -0.22, 0.18) if cuts else 1.0
    values = jax.random.normal(stream_key, dims, jnp.float32) * spread * factor_of
    return jnp.minimum(jnp.maximum(values, -most), most).astype(held_as)


def setup_inputs(seed: int = 0) -> dict:
    arg_keys = jax.random.split(jax.random.key(seed), 16)
    return {
        "block_input": bell_draw(arg_keys[0], (ROWS, LENGTH, D), 1.0, 6.0, ((0, 2), (1, 16))),
        "out_grad": bell_draw(arg_keys[1], (ROWS, LENGTH, D), 1.0, 6.0, ((0, 2), (1, 16))),
        "doc_starts": draw_doc_starts(jax.random.fold_in(arg_keys[15], 71), 0),
        "w_query": bell_draw(arg_keys[3], (D, D), D ** -0.5, 0.125, ((0, 32),)),
        "w_forget": bell_draw(arg_keys[4], (D, D), D ** -0.5, 0.125, ((0, 32),)),
        "w_input": bell_draw(arg_keys[5], (D, D), D ** -0.5, 0.125, ((0, 32),)),
        "w_outgate": bell_draw(arg_keys[6], (D, D), D ** -0.5, 0.125, ((0, 32),)),
        "w_out": bell_draw(arg_keys[7], (D, D), D ** -0.5, 0.125, ((0, 32),)),
        "w_gate": bell_draw(arg_keys[8], (D, FF), D ** -0.5, 0.125, ((0, 16), (1, 2))),
        "w_up": bell_draw(arg_keys[9], (D, FF), D ** -0.5, 0.125, ((0, 16), (1, 2))),
        "w_down": bell_draw(arg_keys[10], (FF, D), FF ** -0.5, 0.078125, ((0, 2), (1, 16))),
        "norm_gain": jnp.clip(1.0 + 0.1 * jax.random.normal(arg_keys[11], (D,), jnp.float32), 0.5, 1.5).astype(jnp.bfloat16),
        "mlp_gain": jnp.clip(1.0 + 0.1 * jax.random.normal(arg_keys[12], (D,), jnp.float32), 0.5, 1.5).astype(jnp.bfloat16),
        "group_gain": jnp.clip(1.0 + 0.1 * jax.random.normal(arg_keys[13], (D,), jnp.float32), 0.5, 1.5).astype(jnp.bfloat16),
        "forget_bias": draw_forget_bias(jax.random.fold_in(arg_keys[15], 71), 0),
    }


lower_bound = 0.85
epsilon = 1e-06
highest = lax.Precision.HIGHEST

@jax.custom_vjp
def low(v):
    return lax.optimization_barrier(v.astype(jnp.bfloat16)).astype(jnp.float32)

@jax.custom_vjp
def low_back(v):
    return v

def low_keep(v):
    return (low(v), None)

def low_pass(kept, grad):
    return (grad,)

def back_keep(v):
    return (v, None)

def back_low(kept, grad):
    return (low(grad),)
low.defvjp(low_keep, low_pass)
low_back.defvjp(back_keep, back_low)

def rms_scale(values, gain_vec):
    return values * lax.rsqrt(lax.optimization_barrier(jnp.mean(values * values, axis=-1, keepdims=True)) + epsilon) * gain_vec

def gate_local(mixer_out, gate_raw, gain_vec):
    shaped = mixer_out.reshape(mixer_out.shape[:-1] + (HEADS, mixer_out.shape[-1] // HEADS))
    normed = shaped * lax.rsqrt(lax.optimization_barrier(jnp.mean(shaped * shaped, axis=-1, keepdims=True)) + epsilon)
    return normed.reshape(mixer_out.shape) * gain_vec * jax.nn.silu(gate_raw)

def split_heads(array_in):
    return array_in.reshape(array_in.shape[0], array_in.shape[1], HEADS, array_in.shape[2] // HEADS)

def head_view(span_decay):
    return span_decay.reshape(span_decay.shape[0], HEADS, -1)[..., None]

def forget_terms(forget_logit):
    forget_gate = lower_bound + (1.0 - lower_bound) * jax.nn.sigmoid(forget_logit)
    key_weight = (1.0 - lower_bound) * jax.nn.sigmoid(-forget_logit)
    log_decay = jnp.cumsum(jnp.log(forget_gate), axis=1)
    return (key_weight, log_decay)

def state_local(forget_logit, values, segment):
    key_weight, log_decay = forget_terms(forget_logit)
    last_decay = log_decay[:, -1, :]
    unbroken = (segment[:, -1] == 0).astype(jnp.float32)
    span_decay = jnp.exp(last_decay) * unbroken[:, None]
    tail_mask = (segment == segment[:, -1:]).astype(jnp.float32)
    weighted = key_weight * jnp.exp(last_decay[:, None, :] - log_decay) * tail_mask[:, :, None]
    span_state = jnp.einsum('rshc,rshe->rhce', split_heads(weighted), split_heads(values), precision=highest)
    return (span_decay, span_state)

def out_local(query_raw, forget_logit, values, segment, carried_state):
    key_weight, log_decay = forget_terms(forget_logit)
    query_act = jax.nn.silu(query_raw)
    lifted = split_heads(query_act * jnp.exp(log_decay))
    lowered = split_heads(key_weight * jnp.exp(-log_decay))
    scores = jnp.einsum('rthc,rshc->rhts', lifted, lowered, precision=highest)
    step_index = jnp.arange(segment.shape[1], dtype=jnp.int32)
    causal = step_index[:, None] >= step_index[None, :]
    same_doc = (segment[:, :, None] == segment[:, None, :]) & causal[None]
    scores = jnp.where(same_doc[:, None], scores, 0.0)
    within = jnp.einsum('rhts,rshe->rthe', scores, split_heads(values), precision=highest)
    open_rows = (segment == 0).astype(jnp.float32)
    carried = jnp.einsum('rthc,rhce->rthe', lifted, carried_state, precision=highest) * open_rows[:, :, None, None]
    combined = within + carried
    return combined.reshape(values.shape)

def recurrence(query_raw, forget_logit, values, reset_mask):
    row_count, length_n, feature_count = values.shape
    block_count = length_n // SPAN
    head_size = feature_count // HEADS

    def blocks(array_in):
        return jnp.swapaxes(array_in.reshape(row_count, block_count, SPAN, feature_count), 0, 1)
    segments = jnp.cumsum(reset_mask.reshape(row_count, block_count, SPAN), axis=2).astype(jnp.int32)
    segments = jnp.swapaxes(segments, 0, 1)

    def advance(carried_state, pieces):
        query_block, logit_block, value_block, segment_block = pieces
        span_decay, span_state = state_local(logit_block, value_block, segment_block)
        mixed_block = out_local(query_block, logit_block, value_block, segment_block, carried_state)
        return (head_view(span_decay) * carried_state + span_state, mixed_block)
    zero_state = jnp.zeros((row_count, HEADS, head_size, head_size), jnp.float32)
    final_state, outputs = lax.scan(jax.checkpoint(advance), zero_state, (blocks(query_raw), blocks(forget_logit), blocks(values), segments))
    return jnp.swapaxes(outputs, 0, 1).reshape(row_count, length_n, feature_count)

def project(left, weight):
    return jnp.matmul(left, weight, precision=highest)

def forward_block(reset_mask, inputs, w_query, w_forget, w_input, w_outgate, w_out, w_gate, w_up, w_down, norm_gain, mlp_gain, group_gain, forget_bias):
    normed_in = low(rms_scale(inputs, norm_gain))
    query_raw = low_back(project(normed_in, w_query))
    forget_raw = low_back(project(normed_in, w_forget))
    values = low_back(project(normed_in, w_input))
    gate_raw = low_back(project(normed_in, w_outgate))
    forget_logit = forget_raw + forget_bias
    mixer_out = recurrence(query_raw, forget_logit, values, reset_mask)
    mixed_out = low(gate_local(mixer_out, gate_raw, group_gain))
    hidden = inputs + low_back(project(mixed_out, w_out))
    normed_mid = low(rms_scale(hidden, mlp_gain))
    gate_a = low_back(project(normed_mid, w_gate))
    up_b = low_back(project(normed_mid, w_up))
    product = low(jax.nn.silu(gate_a) * up_b)
    return hidden + low_back(project(product, w_down))

def reference(block_input, out_grad, doc_starts, w_query, w_forget, w_input, w_outgate, w_out, w_gate, w_up, w_down, norm_gain, mlp_gain, group_gain, forget_bias):
    positions = jnp.arange(LENGTH, dtype=jnp.int32)
    reset_mask = jnp.any(doc_starts[:, :, None] == positions[None, None, :], axis=1).astype(jnp.int32)
    floats = [array_in.astype(jnp.float32) for array_in in (block_input, w_query, w_forget, w_input, w_outgate, w_out, w_gate, w_up, w_down, norm_gain, mlp_gain, group_gain, forget_bias)]

    def forward_fn(inputs, w_query, w_forget, w_input, w_outgate, w_out, w_gate, w_up, w_down, norm_gain, mlp_gain, group_gain, forget_bias):
        return forward_block(reset_mask, inputs, w_query, w_forget, w_input, w_outgate, w_out, w_gate, w_up, w_down, norm_gain, mlp_gain, group_gain, forget_bias)
    output, pullback = jax.vjp(forward_fn, *floats)
    gradients = pullback(out_grad.astype(jnp.float32))
    return (output.astype(jnp.bfloat16), gradients[0].astype(jnp.bfloat16), gradients[1], gradients[2], gradients[3], gradients[4], gradients[5], gradients[6], gradients[7], gradients[8], gradients[9], gradients[10], gradients[11], gradients[12])
```

```python
import functools

import jax
import jax.numpy as jnp
from jax import lax
from jax.experimental import pallas as pl
from jax.experimental.pallas import tpu as pltpu
from jax.sharding import Mesh, PartitionSpec as P

HEADS = 16

lower_bound = 0.85
span_bound = 1.0 - lower_bound
epsilon = 1e-06
f32 = jnp.float32
bf16 = jnp.bfloat16
swap = ((0, 1), (1, 0))
everywhere = ("z", "y", "x", "row")
group = ("y", "x", "row")
plane = ("y", "x")


def swap_x(a):
    return lax.ppermute(a, "x", swap)


def swap_y(a):
    return lax.ppermute(a, "y", swap)


def swap_row(a):
    return lax.ppermute(a, "row", swap)


def gather_group(a):
    half = a.shape[0] // 2
    from_x = swap_x(a)
    from_y = swap_y(a)
    low = swap_y(from_x[:half])
    high = swap_x(from_y[half:])
    near = (a, from_x, from_y, low, high)
    far = tuple(swap_row(piece) for piece in near)
    return jnp.concatenate(near + far, axis=0)


def scatter_group(near, far):
    rows, columns = near.shape
    tokens = rows // 4
    half = columns // 2
    mine = near.astype(f32) + swap_row(far.astype(bf16)).astype(f32)
    mine = mine.reshape(2, 2, tokens, columns)
    left, right = mine[..., :half], mine[..., half:]
    left = left[:, 0] + swap_x(left[:, 1].astype(bf16)).astype(f32)
    right = right[0] + swap_y(right[1].astype(bf16)).astype(f32)
    left = left[0] + swap_y(left[1].astype(bf16)).astype(f32)
    right = right[0] + swap_x(right[1].astype(bf16)).astype(f32)
    return jnp.concatenate([left, right], axis=-1)


def relay(parts, forward):
    count = lax.axis_size("z")
    if forward:
        pairs = [(i, i + 1) for i in range(count - 1)]
    else:
        pairs = [(i + 1, i) for i in range(count - 1)]
    got = []
    for _ in range(count - 1):
        parts = jax.tree.map(lambda a: lax.ppermute(a, "z", pairs), parts)
        got.append(parts)
    return got


def carry_from(got):
    carry = got[-1][0]
    for state, decay in got[-2::-1]:
        carry = state + decay * carry
    return carry


def mm(a, b, dims):
    return lax.dot_general(
        a.astype(bf16), b.astype(bf16), (dims, ((), ())), preferred_element_type=f32
    )


def split_sum(ones_matrix, values, dims):
    first = values.astype(bf16)
    rest = values - first.astype(f32)
    second = rest.astype(bf16)
    third = (rest - second.astype(f32)).astype(bf16)
    total = lax.dot_general(ones_matrix, first, (dims, ((), ())), preferred_element_type=f32)
    total += lax.dot_general(ones_matrix, second, (dims, ((), ())), preferred_element_type=f32)
    total += lax.dot_general(ones_matrix, third, (dims, ((), ())), preferred_element_type=f32)
    return total


NT = ((1,), (1,))
NN = ((1,), (0,))
TN = ((0,), (0,))


def chunk_masks(docs_ref, row_at, start, size):
    at_row = lax.broadcasted_iota(jnp.int32, (size, size), 0)
    at_col = lax.broadcasted_iota(jnp.int32, (size, size), 1)
    same = at_row >= at_col
    opened = at_row >= 0
    tail = at_row >= 0
    whole = jnp.bool_(True)
    for entry in range(docs_ref.shape[1]):
        place = docs_ref[row_at, entry] - start
        same = same & ~((at_col < place) & (place <= at_row))
        opened = opened & ~((0 <= place) & (place <= at_row))
        tail = tail & ~((at_row < place) & (place <= size - 1))
        whole = whole & ~((0 <= place) & (place <= size - 1))
    return same, opened, tail, whole


def decay_terms(logit, tri):
    forget = lower_bound + span_bound * jax.nn.sigmoid(logit)
    key = span_bound * jax.nn.sigmoid(-logit)
    log_sum = split_sum(tri, jnp.log(forget), NN)
    return forget, key, log_sum


def lower_ones(size):
    at_row = lax.broadcasted_iota(jnp.int32, (size, size), 0)
    at_col = lax.broadcasted_iota(jnp.int32, (size, size), 1)
    return (at_row >= at_col).astype(f32).astype(bf16)


def head_rows(ref, head, width):
    return ref[0, 0, :, head * width : (head + 1) * width]


def state_kernel(at_ref, docs_ref, logit_ref, value_ref, bias_ref, state_ref, decay_ref):
    size = logit_ref.shape[2]
    heads = state_ref.shape[1]
    width = state_ref.shape[2]
    outer, inner, chunk = pl.program_id(0), pl.program_id(1), pl.program_id(2)
    row_at = outer * pl.num_programs(1) + inner
    _, _, tail, whole = chunk_masks(docs_ref, row_at, at_ref[1] + chunk * size, size)
    tri = lower_ones(size)

    @pl.when(chunk == 0)
    def _():
        state_ref[...] = jnp.zeros_like(state_ref)
        decay_ref[...] = jnp.ones_like(decay_ref)

    for head in range(heads):
        cut = slice(head * width, (head + 1) * width)
        logit = logit_ref[0, 0, :, cut] + bias_ref[:, cut]
        _, key, log_sum = decay_terms(logit, tri)
        last = log_sum[size - 1 : size, :]
        passed = jnp.where(whole, jnp.exp(last), 0.0)
        weighted = jnp.where(tail, key * jnp.exp(last - log_sum), 0.0)
        state_ref[0, head] = state_ref[0, head] * passed + mm(
            value_ref[0, 0, :, cut], weighted, TN
        )
        decay_ref[0, :, cut] = decay_ref[0, :, cut] * passed


def forward_kernel(
    at_ref, docs_ref, proj_ref, bias_ref, carry_ref, out_ref, mixed_ref, starts_ref, state
):
    size = proj_ref.shape[2]
    heads = state.shape[0]
    width = state.shape[1]
    wide = heads * width
    outer, inner, chunk = pl.program_id(0), pl.program_id(1), pl.program_id(2)
    row_at = outer * pl.num_programs(1) + inner
    same, opened, tail, whole = chunk_masks(docs_ref, row_at, at_ref[1] + chunk * size, size)
    tri = lower_ones(size)

    @pl.when(chunk == 0)
    def _():
        state[...] = carry_ref[0]

    for head in range(heads):
        cut = slice(head * width, (head + 1) * width)
        query = head_rows(proj_ref, head, width)
        logit = head_rows(proj_ref, heads + head, width) + bias_ref[:, cut]
        value = head_rows(proj_ref, 2 * heads + head, width).astype(bf16)
        gate = head_rows(proj_ref, 3 * heads + head, width)
        _, key, log_sum = decay_terms(logit, tri)
        last = log_sum[size - 1 : size, :]
        lifted = (query * jax.nn.sigmoid(query) * jnp.exp(log_sum)).astype(bf16)
        lowered = (key * jnp.exp(-log_sum)).astype(bf16)
        scores = jnp.where(same, mm(lifted, lowered, NT), 0.0)
        begin = state[head]
        starts_ref[0, 0, head] = begin
        out = mm(scores, value, NN) + jnp.where(opened, mm(lifted, begin, NT), 0.0)
        passed = jnp.where(whole, jnp.exp(last), 0.0)
        weighted = jnp.where(tail, key * jnp.exp(last - log_sum), 0.0)
        state[head] = begin * passed + mm(value, weighted, TN)
        scale = lax.rsqrt(jnp.mean(out * out, axis=-1, keepdims=True) + epsilon)
        out_ref[0, 0, :, cut] = out
        mixed_ref[0, 0, :, cut] = (out * scale * (gate * jax.nn.sigmoid(gate))).astype(bf16)


def out_grad_terms(out, gate, grad_mixed):
    gate_on = jax.nn.sigmoid(gate)
    scale = lax.rsqrt(jnp.mean(out * out, axis=-1, keepdims=True) + epsilon)
    normed = out * scale
    grad_normed = grad_mixed * (gate * gate_on)
    grad_out = scale * (
        grad_normed - normed * jnp.mean(grad_normed * normed, axis=-1, keepdims=True)
    )
    return gate_on, normed, grad_out


def back_state_kernel(
    at_ref, docs_ref, query_ref, logit_ref, gate_ref, out_ref, grad_ref, bias_ref, state_ref
):
    size = query_ref.shape[2]
    heads = state_ref.shape[1]
    width = state_ref.shape[2]
    outer, inner, step = pl.program_id(0), pl.program_id(1), pl.program_id(2)
    chunk = pl.num_programs(2) - 1 - step
    row_at = outer * pl.num_programs(1) + inner
    _, opened, _, whole = chunk_masks(docs_ref, row_at, at_ref[1] + chunk * size, size)
    tri = lower_ones(size)

    @pl.when(step == 0)
    def _():
        state_ref[...] = jnp.zeros_like(state_ref)

    for head in range(heads):
        cut = slice(head * width, (head + 1) * width)
        query = query_ref[0, 0, :, cut]
        logit = logit_ref[0, 0, :, cut] + bias_ref[:, cut]
        _, _, log_sum = decay_terms(logit, tri)
        last = log_sum[size - 1 : size, :]
        lifted = jnp.where(opened, query * jax.nn.sigmoid(query) * jnp.exp(log_sum), 0.0)
        _, _, grad_out = out_grad_terms(
            out_ref[0, 0, :, cut], gate_ref[0, 0, :, cut], grad_ref[0, 0, :, cut]
        )
        passed = jnp.where(whole, jnp.exp(last), 0.0)
        state_ref[0, head] = state_ref[0, head] * passed + mm(grad_out, lifted, TN)


def backward_kernel(
    at_ref,
    docs_ref,
    proj_ref,
    out_ref,
    grad_ref,
    bias_ref,
    starts_ref,
    carry_ref,
    all_ref,
    bias_grad_ref,
    state,
):
    size = proj_ref.shape[2]
    heads = state.shape[0]
    width = state.shape[1]
    wide = heads * width
    outer, inner, step = pl.program_id(0), pl.program_id(1), pl.program_id(2)
    chunk = pl.num_programs(2) - 1 - step
    row_at = outer * pl.num_programs(1) + inner
    same, opened, tail, whole = chunk_masks(docs_ref, row_at, at_ref[1] + chunk * size, size)
    tri = lower_ones(size)

    @pl.when((step == 0) & (row_at == 0))
    def _():
        bias_grad_ref[...] = jnp.zeros_like(bias_grad_ref)

    @pl.when(step == 0)
    def _():
        state[...] = carry_ref[0]

    for head in range(heads):
        cut = slice(head * width, (head + 1) * width)
        query = head_rows(proj_ref, head, width)
        logit = head_rows(proj_ref, heads + head, width) + bias_ref[:, cut]
        value = head_rows(proj_ref, 2 * heads + head, width).astype(bf16)
        gate = head_rows(proj_ref, 3 * heads + head, width)
        grad_mixed = grad_ref[0, 0, :, cut]
        forget, key, log_sum = decay_terms(logit, tri)
        last = log_sum[size - 1 : size, :]
        rise = jnp.exp(log_sum)
        fall = jnp.exp(-log_sum)
        remain = jnp.where(tail, jnp.exp(last - log_sum), 0.0)
        query_on = jax.nn.sigmoid(query)
        lifted = (query * query_on * rise).astype(bf16)
        lowered = (key * fall).astype(bf16)
        weighted = (key * remain).astype(bf16)
        scores = jnp.where(same, mm(lifted, lowered, NT), 0.0)
        gate_on, normed, grad_out = out_grad_terms(out_ref[0, 0, :, cut], gate, grad_mixed)
        grad_low = grad_out.astype(bf16)
        begin = starts_ref[0, 0, head]
        later = state[head]
        later_low = later.astype(bf16)
        grad_scores = jnp.where(same, mm(grad_low, value, NT), 0.0).astype(bf16)
        grad_value = mm(scores, grad_low, TN) + mm(weighted, later_low, NT)
        grad_lifted = mm(grad_scores, lowered, NN) + jnp.where(
            opened, mm(grad_low, begin, NN), 0.0
        )
        grad_lowered = mm(grad_scores, lifted, TN)
        grad_weighted = mm(value, later_low, NN)
        passed = jnp.where(whole, jnp.exp(last), 0.0)
        open_lifted = jnp.where(opened, lifted.astype(f32), 0.0)
        state[head] = later * passed + mm(grad_low, open_lifted, TN)
        through = jnp.sum(begin * later, axis=0, keepdims=True) * passed
        weighted_part = grad_weighted * weighted.astype(f32)
        grad_log = (
            grad_lifted * lifted.astype(f32) - grad_lowered * lowered.astype(f32) - weighted_part
        )
        grad_last = through + jnp.sum(weighted_part, axis=0, keepdims=True)
        grad_step = split_sum(tri, grad_log, TN) + grad_last
        grad_key = grad_lowered * fall + grad_weighted * remain
        grad_logit = (
            span_bound
            * jax.nn.sigmoid(logit)
            * jax.nn.sigmoid(-logit)
            * (grad_step / forget - grad_key)
        )
        grad_query = grad_lifted * rise * query_on * (1.0 + query * (1.0 - query_on))
        grad_gate = grad_mixed * normed * gate_on * (1.0 + gate * (1.0 - gate_on))
        bias_grad_ref[:, cut] += jnp.sum(grad_logit, axis=0, keepdims=True)
        for place, part in enumerate((grad_query, grad_logit, grad_value, grad_gate)):
            low = place * wide + head * width
            all_ref[0, 0, :, low : low + width] = part.astype(bf16)


def local_call(kernel, at, docs, ins, in_specs, out_shapes, out_specs, grid, scratch=()):
    return pl.pallas_call(
        kernel,
        grid_spec=pltpu.PrefetchScalarGridSpec(
            num_scalar_prefetch=2,
            grid=grid,
            in_specs=in_specs,
            out_specs=out_specs,
            scratch_shapes=scratch,
        ),
        out_shape=out_shapes,
        compiler_params=pltpu.CompilerParams(
            dimension_semantics=("arbitrary",) * 3, vmem_limit_bytes=40 * 1024 * 1024
        ),
    )(at, docs, *ins)


def contract_rows(left, right):
    return lax.dot_general(left, right, (TN, ((), ())), preferred_element_type=f32)


def times_transpose(left, right):
    return lax.dot_general(left, right, (NT, ((), ())), preferred_element_type=f32)


def times(left, right):
    return jnp.dot(left, right, preferred_element_type=f32)


def rms_rate(values):
    return lax.rsqrt(jnp.mean(values * values, axis=-1, keepdims=True) + epsilon)


def rms_back(grad, values, rate):
    return rate * grad - values * (
        rate * rate * rate * jnp.mean(grad * values, axis=-1, keepdims=True)
    )


def on_device(
    block_input,
    out_grad,
    doc_starts,
    w_query,
    w_forget,
    w_input,
    w_outgate,
    w_out,
    w_gate,
    w_up,
    w_down,
    norm_gain,
    mlp_gain,
    group_gain,
    forget_bias,
):
    row_count, span, features = block_input.shape
    groups = lax.axis_size("z")
    own_row = lax.axis_index("row")
    own_spot = lax.axis_index("y") * 2 + lax.axis_index("x")
    spots, members = 4, 8
    tokens = row_count * span
    width = features // HEADS
    heads = HEADS // members
    wide = heads * width
    share = w_query.shape[0]
    units = w_gate.shape[1] // spots
    block = w_gate.shape[0]

    input_float = block_input.astype(f32).reshape(tokens, features)
    first_rate = rms_rate(input_float)
    normed_all = gather_group((input_float * first_rate).astype(bf16))

    first_gain = norm_gain.astype(f32)[:, None]
    mixer_weights = (w_query, w_forget, w_input, w_outgate)
    scaled = jnp.stack([(w.astype(f32) * first_gain).astype(bf16) for w in mixer_weights])
    scaled = scaled.reshape(4, share, 2, heads, spots, width).transpose(4, 2, 1, 0, 3, 5)
    scaled = scaled.reshape(members, share, 4 * wide)
    scaled = lax.all_to_all(scaled, group, 0, 0, tiled=True)
    mixer_all = lax.all_gather(
        scaled.reshape(members * share, 4 * wide), "z", axis=0, tiled=True
    )

    bias_sent = jnp.broadcast_to(forget_bias.astype(f32), (groups * members, share))
    bias_all = lax.all_to_all(bias_sent, everywhere, 0, 0, tiled=True)
    bias_all = bias_all.reshape(2, heads, spots, width)
    bias_here = lax.dynamic_index_in_dim(bias_all, own_row, 0, False)
    bias_here = lax.dynamic_index_in_dim(bias_here, own_spot, 1, False).reshape(1, wide)

    head_gain = group_gain.astype(f32)[:, None]
    out_scaled = (w_out.astype(f32) * head_gain).astype(bf16)
    by_chip = 2 * share == width and groups == 2 * heads
    if by_chip:
        held = lax.all_gather(out_scaled, "z", axis=0, tiled=False)
        held = held.reshape(2, heads, share, features)
        keep = lax.dynamic_index_in_dim(held, own_row, 0, False)
        give = lax.dynamic_index_in_dim(held, 1 - own_row, 0, False)
        take = swap_row(give)
        own_first = own_row == 0
        out_here = jnp.stack(
            [jnp.where(own_first, keep, take), jnp.where(own_first, take, keep)], axis=1
        ).reshape(wide, features)
    else:
        held = lax.all_gather(out_scaled, everywhere, axis=0, tiled=True)
        held = held.reshape(2, heads, spots, width, features)
        held = lax.dynamic_index_in_dim(held, own_row, 0, False)
        out_here = lax.dynamic_index_in_dim(held, own_spot, 1, False).reshape(wide, features)

    gain_pair = swap_row(mlp_gain)
    mid_gain = jnp.where(
        own_row == 0,
        jnp.concatenate([mlp_gain, gain_pair]),
        jnp.concatenate([gain_pair, mlp_gain]),
    ).astype(f32)[:, None]
    gate_scaled = (w_gate.astype(f32) * mid_gain).astype(bf16)
    up_scaled = (w_up.astype(f32) * mid_gain).astype(bf16)
    down_turned = w_down.T
    gate_cut = gate_scaled.reshape(block, spots, units)
    up_cut = up_scaled.reshape(block, spots, units)
    down_cut = down_turned.reshape(block, spots, units)
    pair_cut = jnp.concatenate([gate_cut, up_cut], axis=-1).transpose(1, 0, 2)
    pair_cut = lax.all_to_all(pair_cut, plane, 0, 0, tiled=True)
    down_cut = lax.all_to_all(down_cut.transpose(1, 0, 2), plane, 0, 0, tiled=True)
    pair_all = lax.all_gather(
        pair_cut.reshape(spots * block, 2 * units), "z", axis=0, tiled=True
    )
    down_all = lax.all_gather(down_cut.reshape(spots * block, units), "z", axis=0, tiled=True)
    gate_all, up_all = pair_all[:, :units], pair_all[:, units:]

    grad_low = out_grad.reshape(tokens, features)
    grad_all = gather_group(grad_low)

    docs = jnp.concatenate([doc_starts, swap_row(doc_starts)], axis=0)
    at = jnp.stack([own_spot, lax.axis_index("z") * (spots * span)]).astype(jnp.int32)
    proj = times(normed_all, mixer_all).reshape(members, row_count, span, 4 * wide)

    grid = (2, row_count, spots)

    def there(place):
        return lambda o, i, c, at_ref, docs_ref: (o * spots + (c ^ at_ref[0]), i, 0, place)

    def back(place):
        return lambda o, i, c, at_ref, docs_ref: (
            o * spots + ((spots - 1 - c) ^ at_ref[0]),
            i,
            0,
            place,
        )

    slab = (1, 1, span, wide)
    full_slab = (1, 1, span, 4 * wide)
    state_slab = (1, heads, width, width)
    rows_all = 2 * row_count
    bias_spec = pl.BlockSpec((1, wide), lambda o, i, c, at_ref, docs_ref: (0, 0))

    def by_row(o, i, c, at_ref, docs_ref):
        return (o * row_count + i, 0, 0, 0)

    state_spec = pl.BlockSpec(state_slab, by_row)
    state_shape = jax.ShapeDtypeStruct((rows_all, heads, width, width), f32)

    span_state, span_decay = local_call(
        state_kernel,
        at,
        docs,
        (proj, proj, bias_here),
        [pl.BlockSpec(slab, there(1)), pl.BlockSpec(slab, there(2)), bias_spec],
        (state_shape, jax.ShapeDtypeStruct((rows_all, 1, wide), f32)),
        (
            state_spec,
            pl.BlockSpec(
                (1, 1, wide), lambda o, i, c, at_ref, docs_ref: (o * row_count + i, 0, 0)
            ),
        ),
        grid,
    )
    span_decay = span_decay.reshape(rows_all, heads, 1, width)
    carried = carry_from(relay((span_state, span_decay), True))

    mixer_out, mixed, starts = local_call(
        forward_kernel,
        at,
        docs,
        (proj, bias_here, carried),
        [pl.BlockSpec(full_slab, there(0)), bias_spec, state_spec],
        (
            jax.ShapeDtypeStruct((members, row_count, span, wide), f32),
            jax.ShapeDtypeStruct((members, row_count, span, wide), bf16),
            jax.ShapeDtypeStruct((rows_all, spots, heads, width, width), f32),
        ),
        (
            pl.BlockSpec(slab, there(0)),
            pl.BlockSpec(slab, there(0)),
            pl.BlockSpec(
                (1, 1, heads, width, width),
                lambda o, i, c, at_ref, docs_ref: (o * row_count + i, c, 0, 0, 0),
            ),
        ),
        grid,
        (pltpu.VMEM((heads, width, width), f32),),
    )
    half = spots * tokens
    mixed_flat = mixed.reshape(2 * half, wide)
    far_part = times(mixed_flat[half:], out_here)
    near_part = times(mixed_flat[:half], out_here)
    hidden = input_float + scatter_group(near_part, far_part)

    mid_rate = rms_rate(hidden)
    mid_all = gather_group((hidden * mid_rate).astype(bf16))
    gate_a = times(mid_all, gate_all)
    up_b = times(mid_all, up_all)
    gate_on = jax.nn.sigmoid(gate_a)
    gate_act = gate_a * gate_on
    product = (gate_act * up_b).astype(bf16)
    grad_product = times(grad_all, down_all)
    grad_a = (grad_product * up_b * gate_on * (1.0 + gate_a * (1.0 - gate_on))).astype(bf16)
    grad_b = (grad_product * gate_act).astype(bf16)
    far_mid = times_transpose(grad_a[half:], gate_all) + times_transpose(grad_b[half:], up_all)
    near_mid = times_transpose(grad_a[:half], gate_all) + times_transpose(grad_b[:half], up_all)
    grad_mid = scatter_group(near_mid, far_mid)
    grad_float = out_grad.astype(f32).reshape(tokens, features)
    grad_hidden = grad_float + rms_back(grad_mid, hidden, mid_rate)
    far_down = times_transpose(product[half:], down_all)
    near_down = times_transpose(product[:half], down_all)
    block_output = (hidden + scatter_group(near_down, far_down)).astype(bf16)

    def spread(partial, axis_size):
        return lax.psum_scatter(partial.astype(bf16), "z", scatter_dimension=0, tiled=True)

    grad_down = spread(contract_rows(grad_all, product), groups)
    grad_pair = spread(
        jnp.concatenate([contract_rows(mid_all, grad_a), contract_rows(mid_all, grad_b)], axis=-1),
        groups,
    )

    gm_all = gather_group(grad_hidden.astype(bf16))
    grad_mixed = times_transpose(gm_all, out_here).reshape(members, row_count, span, wide)
    local_back = local_call(
        back_state_kernel,
        at,
        docs,
        (proj, proj, proj, mixer_out, grad_mixed, bias_here),
        [
            pl.BlockSpec(slab, back(0)),
            pl.BlockSpec(slab, back(1)),
            pl.BlockSpec(slab, back(3)),
            pl.BlockSpec(slab, back(0)),
            pl.BlockSpec(slab, back(0)),
            bias_spec,
        ],
        state_shape,
        state_spec,
        grid,
    )
    later = carry_from(relay((local_back, span_decay), False))
    grads_flat, bias_part = local_call(
        backward_kernel,
        at,
        docs,
        (proj, mixer_out, grad_mixed, bias_here, starts, later),
        [
            pl.BlockSpec(full_slab, back(0)),
            pl.BlockSpec(slab, back(0)),
            pl.BlockSpec(slab, back(0)),
            bias_spec,
            pl.BlockSpec(
                (1, 1, heads, width, width),
                lambda o, i, c, at_ref, docs_ref: (o * row_count + i, spots - 1 - c, 0, 0, 0),
            ),
            state_spec,
        ],
        (
            jax.ShapeDtypeStruct((members, row_count, span, 4 * wide), bf16),
            jax.ShapeDtypeStruct((1, wide), f32),
        ),
        (pl.BlockSpec(full_slab, back(0)), bias_spec),
        grid,
        (pltpu.VMEM((heads, width, width), f32),),
    )
    grads_flat = grads_flat.reshape(2 * half, 4 * wide)
    grad_mixer = spread(contract_rows(normed_all, grads_flat), groups)
    far_in = times_transpose(grads_flat[half:], mixer_all)
    near_in = times_transpose(grads_flat[:half], mixer_all)
    grad_normed = scatter_group(near_in, far_in)
    input_grad = grad_hidden + rms_back(grad_normed, input_float, first_rate)
    input_grad = input_grad.astype(bf16).reshape(block_input.shape)

    grad_out_rows = contract_rows(mixed_flat, gm_all).astype(bf16)
    if by_chip:
        cut = grad_out_rows.reshape(heads, 2, share, features)
        keep = lax.dynamic_index_in_dim(cut, own_row, 1, False)
        give = lax.dynamic_index_in_dim(cut, 1 - own_row, 1, False)
        take = swap_row(give)
        cut = jnp.concatenate(
            [jnp.where(own_first, keep, take), jnp.where(own_first, take, keep)], axis=0
        )
        grad_out = lax.psum_scatter(
            cut.reshape(groups * share, features), "z", scatter_dimension=0, tiled=True
        )
    else:
        placed = jnp.zeros((2, heads, spots, width, features), bf16)
        placed = lax.dynamic_update_slice(
            placed,
            grad_out_rows.reshape(1, heads, 1, width, features),
            (own_row, 0, own_spot, 0, 0),
        )
        grad_out = lax.psum_scatter(
            placed.reshape(features, features), everywhere, scatter_dimension=0, tiled=True
        )
    grad_out = grad_out.astype(f32)
    grad_head_gain = jnp.sum(grad_out * w_out.astype(f32), axis=1)

    pair_back = lax.all_to_all(
        grad_pair.reshape(spots, block, 2 * units), plane, 0, 0, tiled=True
    ).astype(f32)
    grad_gate = pair_back[..., :units].transpose(1, 0, 2).reshape(block, spots * units)
    grad_up = pair_back[..., units:].transpose(1, 0, 2).reshape(block, spots * units)
    down_back = lax.all_to_all(grad_down.reshape(spots, block, units), plane, 0, 0, tiled=True)
    grad_down = down_back.transpose(0, 2, 1).reshape(spots * units, block).astype(f32)
    mid_part = jnp.sum(grad_gate * w_gate.astype(f32) + grad_up * w_up.astype(f32), axis=1)
    mid_part = mid_part.reshape(2, share)
    mid_keep = lax.dynamic_index_in_dim(mid_part, own_row, 0, False)
    mid_give = lax.dynamic_index_in_dim(mid_part, 1 - own_row, 0, False)
    grad_mid_gain = mid_keep + swap_row(mid_give)

    mixer_back = lax.all_to_all(
        grad_mixer.reshape(members, share, 4 * wide), group, 0, 0, tiled=True
    ).astype(f32)
    mixer_back = mixer_back.reshape(spots, 2, share, 4, heads, width).transpose(3, 2, 1, 4, 0, 5)
    mixer_back = mixer_back.reshape(4, share, features)
    grad_first_gain = jnp.zeros((share,), f32)
    for place, weight in enumerate(mixer_weights):
        grad_first_gain += jnp.sum(mixer_back[place] * weight.astype(f32), axis=1)

    bias_placed = jnp.zeros((2, heads, spots, width), f32)
    bias_placed = lax.dynamic_update_slice(
        bias_placed, bias_part.reshape(1, heads, 1, width), (own_row, 0, own_spot, 0)
    )
    bias_back = lax.all_to_all(
        bias_placed.reshape(groups * members, share), everywhere, 0, 0, tiled=True
    )
    grad_bias = jnp.sum(bias_back, axis=0)

    return (
        block_output.reshape(block_input.shape),
        input_grad,
        mixer_back[0] * first_gain,
        mixer_back[1] * first_gain,
        mixer_back[2] * first_gain,
        mixer_back[3] * first_gain,
        grad_out * head_gain,
        grad_gate * mid_gain,
        grad_up * mid_gain,
        grad_down,
        grad_first_gain,
        grad_mid_gain,
        grad_head_gain,
        grad_bias,
    )


def solution(mesh):
    count, rows = mesh.devices.shape
    folded = Mesh(mesh.devices.reshape(count // 4, 2, 2, rows), everywhere)
    seq = ("z", "y", "x")
    token_spec = P("row", seq, None)
    matrix_spec = P(everywhere, None)
    vector_spec = P(everywhere)
    wide_spec = P(seq, "row")
    tall_spec = P("row", seq)
    in_specs = (
        (token_spec, token_spec, P("row", None))
        + (matrix_spec,) * 5
        + (wide_spec, wide_spec, tall_spec)
        + (vector_spec,) * 4
    )
    out_specs = (
        (token_spec, token_spec)
        + (matrix_spec,) * 5
        + (wide_spec, wide_spec, tall_spec)
        + (vector_spec,) * 4
    )
    return jax.shard_map(
        on_device, mesh=folded, in_specs=in_specs, out_specs=out_specs, check_vma=False
    )
```

```python
import jax
import jax.numpy as jnp
from jax import lax
from jax.experimental import pallas as pl
from jax.experimental.pallas import tpu as pltpu
from jax.sharding import Mesh, PartitionSpec as P

HEADS = 16

lower_bound = 0.85
span_bound = 1.0 - lower_bound
epsilon = 1e-06
f32 = jnp.float32
bf16 = jnp.bfloat16
swap = ((0, 1), (1, 0))
everywhere = ("z", "y", "x", "row")
group = ("y", "x", "row")
plane = ("y", "x")


def swap_x(a):
    return lax.ppermute(a, "x", swap)


def swap_y(a):
    return lax.ppermute(a, "y", swap)


def swap_row(a):
    return lax.ppermute(a, "row", swap)


def after(value, *others):
    return lax.optimization_barrier((value,) + others)[0]


def join(*groups):
    flat, tree = jax.tree.flatten(groups)
    return jax.tree.unflatten(tree, lax.optimization_barrier(flat))


def gather_first(a):
    return a, swap_x(a), swap_y(a)


def gather_second(a, from_x, from_y):
    half = a.shape[0] // 2
    return a, from_x, from_y, swap_y(from_x[:half]), swap_x(from_y[half:])


def lay_kernel(*refs):
    pieces, out_ref = refs[:-1], refs[-1]
    rows = out_ref.shape[0]
    start = 0
    for ref in pieces:
        block, low = start // rows, start % rows

        @pl.when(pl.program_id(0) == block)
        def _(ref=ref, low=low):
            out_ref[low : low + ref.shape[0], :] = ref[...]

        start += ref.shape[0]


def lay(pieces):
    rows, columns = pieces[0].shape
    total = sum(piece.shape[0] for piece in pieces)
    return pl.pallas_call(
        lay_kernel,
        grid=(total // rows,),
        in_specs=[pl.BlockSpec(piece.shape, lambda step: (0, 0)) for piece in pieces],
        out_specs=pl.BlockSpec((rows, columns), lambda step: (step, 0)),
        out_shape=jax.ShapeDtypeStruct((total, columns), pieces[0].dtype),
        compiler_params=pltpu.CompilerParams(
            dimension_semantics=("arbitrary",), vmem_limit_bytes=48 * 1024 * 1024
        ),
    )(*pieces)


def gather_last(near):
    return lay(near + tuple(swap_row(piece) for piece in near))


def gather_group(a):
    return gather_last(gather_second(*gather_first(a)))


def scatter_first(near, far):
    rows, columns = near.shape
    half = columns // 2
    mine = near.astype(f32) + swap_row(far.astype(bf16)).astype(f32)
    mine = mine.reshape(2, 2, rows // 4, columns)
    left, right = mine[..., :half], mine[..., half:]
    return left[:, 0], right[0], left[:, 1].astype(bf16), right[1].astype(bf16)


def scatter_second(left, right, to_x, to_y):
    return left, right, swap_x(to_x), swap_y(to_y)


def scatter_third(left, right, from_x, from_y):
    left = left + from_x.astype(f32)
    right = right + from_y.astype(f32)
    return left[0], right[0], swap_y(left[1].astype(bf16)), swap_x(right[1].astype(bf16))


def scatter_last(left, right, from_y, from_x):
    return jnp.concatenate([left + from_y.astype(f32), right + from_x.astype(f32)], axis=-1)


def scatter_group(near, far, first=(), second=()):
    state, first = join(scatter_second(*scatter_first(near, far)), first)
    state, second = join(scatter_third(*state), second)
    return scatter_last(*state), *first, *second


def hop(packed, forward):
    count = lax.axis_size("z")
    if forward:
        pairs = [(i, i + 1) for i in range(count - 1)]
    else:
        pairs = [(i + 1, i) for i in range(count - 1)]
    return lax.ppermute(packed, "z", pairs)


def relay(packed, forward):
    got = []
    for _ in range(lax.axis_size("z") - 1):
        packed = hop(packed, forward)
        got.append(packed)
    return got


def pair(values):
    high = values.astype(bf16)
    return high, (values - high.astype(f32)).astype(bf16)


def mm(a, b, dims):
    def dot(left, right):
        return lax.dot_general(left, right, (dims, ((), ())), preferred_element_type=f32)

    return dot(a[0], b[0]) + (dot(a[0], b[1]) + dot(a[1], b[0]))


def split_sum(ones_matrix, values, dims):
    first = values.astype(bf16)
    rest = values - first.astype(f32)
    second = rest.astype(bf16)
    third = (rest - second.astype(f32)).astype(bf16)
    total = lax.dot_general(ones_matrix, first, (dims, ((), ())), preferred_element_type=f32)
    total += lax.dot_general(ones_matrix, second, (dims, ((), ())), preferred_element_type=f32)
    total += lax.dot_general(ones_matrix, third, (dims, ((), ())), preferred_element_type=f32)
    return total


NT = ((1,), (1,))
NN = ((1,), (0,))
TN = ((0,), (0,))


def chunk_masks(docs_ref, row_at, start, size):
    at_row = lax.broadcasted_iota(jnp.int32, (size, size), 0)
    at_col = lax.broadcasted_iota(jnp.int32, (size, size), 1)
    same = at_row >= at_col
    opened = at_row >= 0
    tail = at_row >= 0
    whole = jnp.bool_(True)
    for entry in range(docs_ref.shape[1]):
        place = docs_ref[row_at, entry] - start
        same = same & ~((at_col < place) & (place <= at_row))
        opened = opened & ~((0 <= place) & (place <= at_row))
        tail = tail & ~((at_row < place) & (place <= size - 1))
        whole = whole & ~((0 <= place) & (place <= size - 1))
    return same, opened, tail, whole


def decay_terms(logit, tri):
    forget = lower_bound + span_bound * jax.nn.sigmoid(logit)
    key = span_bound * jax.nn.sigmoid(-logit)
    log_sum = split_sum(tri, jnp.log(forget), NN)
    return forget, key, log_sum


def lower_ones(size):
    at_row = lax.broadcasted_iota(jnp.int32, (size, size), 0)
    at_col = lax.broadcasted_iota(jnp.int32, (size, size), 1)
    return (at_row >= at_col).astype(f32).astype(bf16)


PAD = 16


def pack_state(ref, row, head, state, decay):
    width = state.shape[0]
    high = decay.astype(bf16).astype(f32)
    at_row = lax.broadcasted_iota(jnp.int32, (PAD, width), 0)
    extra = jnp.where(at_row == 0, high, jnp.where(at_row == 1, decay - high, 0.0))
    ref[row, head, :width, :] = state.astype(bf16)
    ref[row, head, width:, :] = extra.astype(bf16)


def unpack_carry(refs, row, head):
    width = refs[0].shape[3]
    carry = None
    for ref in refs[::-1]:
        state = ref[row, head, :width, :].astype(f32)
        if carry is not None:
            extra = ref[row, head, width:, :].astype(f32)
            state = state + (extra[0:1] + extra[1:2]) * carry
        carry = state
    return carry


def state_kernel(at_ref, docs_ref, zv_ref, bias_ref, packed_ref, state, decay):
    rows, size = zv_ref.shape[1:3]
    heads, width = state.shape[1:3]
    half, chunk = pl.program_id(0), pl.program_id(1)
    tri = lower_ones(size)

    @pl.when(chunk == 0)
    def _():
        state[...] = jnp.zeros_like(state)
        decay[...] = jnp.ones_like(decay)

    for row in range(rows):
        _, _, tail, whole = chunk_masks(
            docs_ref, half * rows + row, at_ref[1] + chunk * size, size
        )
        for head in range(heads):
            low = head * width
            logit = zv_ref[0, row, :, low : low + width] + bias_ref[:, low : low + width]
            value = zv_ref[0, row, :, heads * width + low : heads * width + low + width]
            _, key, log_sum = decay_terms(logit, tri)
            last = log_sum[size - 1 : size, :]
            passed = jnp.where(whole, jnp.exp(last), 0.0)
            weighted = jnp.where(tail, key * jnp.exp(last - log_sum), 0.0)
            state[row, head] = state[row, head] * passed + mm(pair(value), pair(weighted), TN)
            decay[row, head] = decay[row, head] * passed

    @pl.when(chunk == pl.num_programs(1) - 1)
    def _():
        for row in range(rows):
            for head in range(heads):
                pack_state(packed_ref, row, head, state[row, head], decay[row, head])


def forward_kernel(half, at_ref, docs_ref, qr_ref, zv_ref, bias_ref, gain_ref, *rest):
    carry_refs, (out_ref, mixed_ref, starts_ref, state) = rest[:-4], rest[-4:]
    rows, size = qr_ref.shape[1:3]
    heads, width = state.shape[1:3]
    chunk = pl.program_id(0)
    tri = lower_ones(size)

    @pl.when(chunk == 0)
    def _():
        for row in range(rows):
            for head in range(heads):
                state[row, head] = unpack_carry(carry_refs, row, head)

    for row in range(rows):
        same, opened, tail, whole = chunk_masks(
            docs_ref, half * rows + row, at_ref[1] + chunk * size, size
        )
        for head in range(heads):
            low = head * width
            high = (heads + head) * width
            query = qr_ref[0, row, :, low : low + width]
            gate = qr_ref[0, row, :, high : high + width]
            logit = zv_ref[0, row, :, low : low + width] + bias_ref[:, low : low + width]
            value = pair(zv_ref[0, row, :, high : high + width])
            _, key, log_sum = decay_terms(logit, tri)
            last = log_sum[size - 1 : size, :]
            lifted = pair(query * jax.nn.sigmoid(query) * jnp.exp(log_sum))
            lowered = pair(key * jnp.exp(-log_sum))
            scores = pair(jnp.where(same, mm(lifted, lowered, NT), 0.0))
            begin = state[row, head]
            starts_ref[0, row, head] = begin
            out = mm(scores, value, NN) + jnp.where(opened, mm(lifted, pair(begin), NT), 0.0)
            passed = jnp.where(whole, jnp.exp(last), 0.0)
            weighted = jnp.where(tail, key * jnp.exp(last - log_sum), 0.0)
            state[row, head] = begin * passed + mm(value, pair(weighted), TN)
            scale = lax.rsqrt(jnp.mean(out * out, axis=-1, keepdims=True) + epsilon)
            normed = out * scale * gain_ref[:, low : low + width]
            out_ref[0, row, :, low : low + width] = out
            mixed_ref[0, row, :, low : low + width] = (
                normed * (gate * jax.nn.sigmoid(gate))
            ).astype(bf16)


def open_kernel(
    at_ref,
    docs_ref,
    qr_ref,
    zv_ref,
    out_ref,
    grad_ref,
    bias_ref,
    gain_ref,
    starts_ref,
    qr_grad_ref,
    low_ref,
    part_ref,
    packed_ref,
    state,
    decay,
):
    rows, size = qr_ref.shape[1:3]
    heads, width = state.shape[1:3]
    half, step = pl.program_id(0), pl.program_id(1)
    chunk = pl.num_programs(1) - 1 - step
    tri = lower_ones(size)

    @pl.when(step == 0)
    def _():
        state[...] = jnp.zeros_like(state)
        decay[...] = jnp.ones_like(decay)

    for row in range(rows):
        same, opened, _, whole = chunk_masks(
            docs_ref, half * rows + row, at_ref[1] + chunk * size, size
        )
        for head in range(heads):
            low = head * width
            high = (heads + head) * width
            query = qr_ref[0, row, :, low : low + width]
            gate = qr_ref[0, row, :, high : high + width]
            logit = zv_ref[0, row, :, low : low + width] + bias_ref[:, low : low + width]
            value = pair(zv_ref[0, row, :, high : high + width])
            out = out_ref[0, row, :, low : low + width]
            grad_mixed = grad_ref[0, row, :, low : low + width] * gain_ref[:, low : low + width]
            _, key, log_sum = decay_terms(logit, tri)
            last = log_sum[size - 1 : size, :]
            rise = jnp.exp(log_sum)
            query_on = jax.nn.sigmoid(query)
            lifted = query * query_on * rise
            lowered = pair(key * jnp.exp(-log_sum))
            gate_on = jax.nn.sigmoid(gate)
            scale = lax.rsqrt(jnp.mean(out * out, axis=-1, keepdims=True) + epsilon)
            normed = out * scale
            grad_normed = grad_mixed * (gate * gate_on)
            grad_out = scale * (
                grad_normed - normed * jnp.mean(grad_normed * normed, axis=-1, keepdims=True)
            )
            grad_low = pair(grad_out)
            grad_scores = pair(jnp.where(same, mm(grad_low, value, NT), 0.0))
            grad_lifted = mm(grad_scores, lowered, NN) + jnp.where(
                opened, mm(grad_low, pair(starts_ref[0, row, head]), NN), 0.0
            )
            grad_query = grad_lifted * rise * query_on * (1.0 + query * (1.0 - query_on))
            grad_gate = grad_mixed * normed * gate_on * (1.0 + gate * (1.0 - gate_on))
            qr_grad_ref[0, row, :, low : low + width] = grad_query.astype(bf16)
            qr_grad_ref[0, row, :, high : high + width] = grad_gate.astype(bf16)
            low_ref[0, row, :, low : low + width] = grad_out
            part_ref[0, row, :, low : low + width] = grad_lifted * lifted
            passed = jnp.where(whole, jnp.exp(last), 0.0)
            state[row, head] = state[row, head] * passed + mm(
                grad_low, pair(jnp.where(opened, lifted, 0.0)), TN
            )
            decay[row, head] = decay[row, head] * passed

    @pl.when(step == pl.num_programs(1) - 1)
    def _():
        for row in range(rows):
            for head in range(heads):
                pack_state(packed_ref, row, head, state[row, head], decay[row, head])


def close_kernel(
    at_ref, docs_ref, kept_ref, qr_ref, zv_ref, low_ref, part_ref, bias_ref, starts_ref, *rest
):
    carry_refs, (zv_grad_ref, bias_grad_ref, state) = rest[:-3], rest[-3:]
    rows, size = qr_ref.shape[1:3]
    heads, width = state.shape[1:3]
    half, step = pl.program_id(0), pl.program_id(1)
    chunk = pl.num_programs(1) - 1 - step
    tri = lower_ones(size)

    @pl.when((step == 0) & (half == 0))
    def _():
        bias_grad_ref[...] = jnp.zeros_like(bias_grad_ref)

    @pl.when(step == 0)
    def _():
        for row in range(rows):
            for head in range(heads):
                state[row, head] = unpack_carry(carry_refs, row, head)

    for row in range(rows):
        same, opened, tail, whole = chunk_masks(
            docs_ref, half * rows + row, at_ref[1] + chunk * size, size
        )
        for head in range(heads):
            low = head * width
            high = (heads + head) * width
            query = qr_ref[0, row, :, low : low + width]
            logit = zv_ref[0, row, :, low : low + width] + bias_ref[:, low : low + width]
            value = pair(zv_ref[0, row, :, high : high + width])
            grad_low = pair(low_ref[0, row, :, low : low + width])
            forget, key, log_sum = decay_terms(logit, tri)
            last = log_sum[size - 1 : size, :]
            fall = jnp.exp(-log_sum)
            remain = jnp.where(tail, jnp.exp(last - log_sum), 0.0)
            lifted = query * jax.nn.sigmoid(query) * jnp.exp(log_sum)
            lowered = key * fall
            weighted = key * remain
            lifted_low = pair(lifted)
            scores = pair(jnp.where(same, mm(lifted_low, pair(lowered), NT), 0.0))
            begin = starts_ref[0, row, head]
            later = state[row, head]
            later_low = pair(later)
            grad_scores = pair(jnp.where(same, mm(grad_low, value, NT), 0.0))
            grad_value = mm(scores, grad_low, TN) + mm(pair(weighted), later_low, NT)
            grad_lowered = mm(grad_scores, lifted_low, TN)
            grad_weighted = mm(value, later_low, NN)
            passed = jnp.where(whole, jnp.exp(last), 0.0)
            open_lifted = pair(jnp.where(opened, lifted, 0.0))
            state[row, head] = later * passed + mm(grad_low, open_lifted, TN)
            through = jnp.sum(begin * later, axis=0, keepdims=True) * passed
            weighted_part = grad_weighted * weighted
            grad_log = (
                part_ref[0, row, :, low : low + width]
                - grad_lowered * lowered
                - weighted_part
            )
            grad_last = through + jnp.sum(weighted_part, axis=0, keepdims=True)
            grad_step = split_sum(tri, grad_log, TN) + grad_last
            grad_key = grad_lowered * fall + grad_weighted * remain
            grad_logit = (
                span_bound
                * jax.nn.sigmoid(logit)
                * jax.nn.sigmoid(-logit)
                * (grad_step / forget - grad_key)
            )
            bias_grad_ref[:, low : low + width] += jnp.sum(grad_logit, axis=0, keepdims=True)
            zv_grad_ref[0, row, :, low : low + width] = grad_logit.astype(bf16)
            zv_grad_ref[0, row, :, high : high + width] = grad_value.astype(bf16)


def local_call(
    kernel, at, docs, ins, in_specs, out_shapes, out_specs, grid, scratch, aliases=None
):
    return pl.pallas_call(
        kernel,
        grid_spec=pltpu.PrefetchScalarGridSpec(
            num_scalar_prefetch=2,
            grid=grid,
            in_specs=in_specs,
            out_specs=out_specs,
            scratch_shapes=scratch,
        ),
        out_shape=out_shapes,
        input_output_aliases=aliases or {},
        compiler_params=pltpu.CompilerParams(
            dimension_semantics=("arbitrary",) * len(grid), vmem_limit_bytes=48 * 1024 * 1024
        ),
    )(at, docs, *ins)


def contract_rows(left, right):
    return lax.dot_general(left, right, (TN, ((), ())), preferred_element_type=f32)


def times_transpose(left, right):
    return lax.dot_general(left, right, (NT, ((), ())), preferred_element_type=f32)


def times(left, right):
    return jnp.dot(left, right, preferred_element_type=f32)


def rms_rate(values):
    return lax.rsqrt(jnp.mean(values * values, axis=-1, keepdims=True) + epsilon)


def rms_back(grad, values, rate):
    return rate * grad - values * (
        rate * rate * rate * jnp.mean(grad * values, axis=-1, keepdims=True)
    )


def on_device(
    block_input,
    out_grad,
    doc_starts,
    w_query,
    w_forget,
    w_input,
    w_outgate,
    w_out,
    w_gate,
    w_up,
    w_down,
    norm_gain,
    mlp_gain,
    group_gain,
    forget_bias,
):
    row_count, span, features = block_input.shape
    groups = lax.axis_size("z")
    own_row = lax.axis_index("row")
    own_spot = lax.axis_index("y") * 2 + lax.axis_index("x")
    own_first = own_row == 0
    spots, members = 4, 8
    tokens = row_count * span
    width = features // HEADS
    heads = HEADS // members
    wide = heads * width
    share = w_query.shape[0]
    units = w_gate.shape[1] // spots
    block = w_gate.shape[0]
    half = spots * tokens

    by_chip = 2 * share == width and groups == 2 * heads
    if by_chip:
        held = lax.all_gather(w_out, "z", axis=0, tiled=False).reshape(2, heads, share, features)
    else:
        held = lax.all_gather(w_out, everywhere, axis=0, tiled=True)

    def cut_heads(first, second):
        both = jnp.stack([first, second]).reshape(2, share, 2, heads, spots, width)
        return both.transpose(4, 2, 1, 0, 3, 5).reshape(members, share, 2 * wide)

    def over_group(cut):
        return lax.all_to_all(cut, group, 0, 0, tiled=True)

    def over_plane(cut):
        return lax.all_to_all(cut, plane, 0, 0, tiled=True)

    def over_groups(cut):
        flat = cut.reshape(cut.shape[0] * cut.shape[1], cut.shape[2])
        return lax.all_gather(flat, "z", axis=0, tiled=True)

    vectors = jnp.stack([norm_gain, mlp_gain, group_gain, forget_bias]).astype(f32)
    vectors = jnp.broadcast_to(vectors.reshape(1, 4 * share), (groups * members, 4 * share))
    vectors = lax.all_to_all(vectors, everywhere, 0, 0, tiled=True)
    mixer_cut = over_group(
        after(
            jnp.stack([cut_heads(w_forget, w_input), cut_heads(w_query, w_outgate)], axis=1),
            vectors,
        )
    )
    zv_all = over_groups(mixer_cut[:, 0])
    qr_all = over_groups(mixer_cut[:, 1])

    vectors = vectors.reshape(groups * members, 4, share).transpose(1, 0, 2).reshape(4, features)
    here = lax.dynamic_index_in_dim(
        vectors.reshape(4, 2, heads, spots, width), own_row, 1, False
    )
    here = lax.dynamic_index_in_dim(here, own_spot, 2, False).reshape(4, wide)
    first_gain, mid_gain = vectors[0:1], vectors[1:2]
    gain_here, bias_here = here[2:3], here[3:4]

    input_float = block_input.astype(f32).reshape(tokens, features)
    first_rate = rms_rate(input_float)
    normed = (input_float * first_rate * first_gain).astype(bf16)
    normed_all = gather_group(normed)

    pair_cut = jnp.concatenate(
        [w_gate.reshape(block, spots, units), w_up.reshape(block, spots, units)], axis=-1
    ).transpose(1, 0, 2)
    pair_cut = over_plane(after(pair_cut, normed_all))
    down_cut = w_down.T.reshape(block, spots, units).transpose(1, 0, 2)
    down_cut = over_plane(after(down_cut, pair_cut)).reshape(spots * block, units)

    docs = jnp.concatenate([doc_starts, swap_row(doc_starts)], axis=0)
    at = jnp.stack([own_spot, lax.axis_index("z") * (spots * span)]).astype(jnp.int32)
    by_block = (members, row_count, span)
    zv = times(normed_all, zv_all).reshape(by_block + (2 * wide,))

    once = pl.BlockSpec((1, wide), lambda *_: (0, 0))
    packed_block = (row_count, heads, width + PAD, width)
    packed_shape = jax.ShapeDtypeStruct((2 * row_count,) + packed_block[1:], bf16)
    states = pltpu.VMEM((row_count, heads, width, width), f32)
    decays = pltpu.VMEM((row_count, heads, 1, width), f32)

    def slab(columns, index):
        return pl.BlockSpec((1, row_count, span, columns), index)

    def ahead(h, c, at_ref, docs_ref):
        return (h * spots + (c ^ at_ref[0]), 0, 0, 0)

    def behind(h, c, at_ref, docs_ref):
        return (h * spots + ((spots - 1 - c) ^ at_ref[0]), 0, 0, 0)

    by_half = pl.BlockSpec(packed_block, lambda h, c, at_ref, docs_ref: (h, 0, 0, 0))

    packed = local_call(
        state_kernel,
        at,
        docs,
        (zv, bias_here),
        [slab(2 * wide, ahead), once],
        packed_shape,
        by_half,
        (2, spots),
        (states, decays),
    )
    grad_low = out_grad.reshape(tokens, features)

    packed, pair_cut = join(packed, pair_cut.reshape(spots * block, 2 * units))
    pair_all = lax.all_gather(pair_cut, "z", axis=0, tiled=True)
    gate_all, up_all = pair_all[:, :units], pair_all[:, units:]
    carried = relay(packed, True)
    near = gather_second(*gather_first(after(grad_low, pair_cut)))
    qr = times(normed_all, qr_all)
    carried, near, qr, down_cut = join(carried, near, qr, down_cut)
    down_all = lax.all_gather(down_cut, "z", axis=0, tiled=True)
    grad_all = gather_last(near)
    qr = qr.reshape(by_block + (2 * wide,))

    def forward_half(side, qr):
        def place(c, at_ref, docs_ref):
            return (side * spots + (c ^ at_ref[0]), 0, 0, 0)

        def local(c, at_ref, docs_ref):
            return (c ^ at_ref[0], 0, 0, 0)

        def kernel(*refs):
            forward_kernel(side, *refs)

        return local_call(
            kernel,
            at,
            docs,
            (qr, zv, bias_here, gain_here, *carried),
            [slab(2 * wide, place), slab(2 * wide, place), once, once]
            + [pl.BlockSpec(packed_block, lambda c, at_ref, docs_ref: (side, 0, 0, 0))]
            * len(carried),
            (
                jax.ShapeDtypeStruct((spots,) + by_block[1:] + (wide,), f32),
                jax.ShapeDtypeStruct((spots,) + by_block[1:] + (wide,), bf16),
                jax.ShapeDtypeStruct((spots, row_count, heads, width, width), f32),
            ),
            (
                slab(wide, local),
                slab(wide, local),
                pl.BlockSpec(
                    (1, row_count, heads, width, width),
                    lambda c, at_ref, docs_ref: (c, 0, 0, 0, 0),
                ),
            ),
            (spots,),
            (states,),
        )

    if by_chip:
        keep = lax.dynamic_index_in_dim(held, own_row, 0, False)
        give = lax.dynamic_index_in_dim(held, 1 - own_row, 0, False)
        take = swap_row(give)
        out_here = jnp.stack(
            [jnp.where(own_first, keep, take), jnp.where(own_first, take, keep)], axis=1
        ).reshape(wide, features)
    else:
        held = held.reshape(2, heads, spots, width, features)
        held = lax.dynamic_index_in_dim(held, own_row, 0, False)
        out_here = lax.dynamic_index_in_dim(held, own_spot, 1, False).reshape(wide, features)

    far_out, far_mixed, far_starts = forward_half(1, qr)
    far_mixed = far_mixed.reshape(half, wide)
    far_part = times(far_mixed, out_here).astype(bf16)
    near_out, near_mixed, near_starts = forward_half(0, after(qr, far_part))
    near_mixed = near_mixed.reshape(half, wide)
    near_part = times(near_mixed, out_here)
    hidden = input_float + scatter_group(near_part, far_part)[0]

    mid_rate = rms_rate(hidden)
    first, grad_all, mixer_weights = join(
        gather_first((hidden * mid_rate * mid_gain).astype(bf16)),
        grad_all,
        jnp.concatenate([qr_all, zv_all], axis=1),
    )
    mid_all = gather_last(gather_second(*first))
    gate_a = times(mid_all, gate_all)
    up_b = times(mid_all, up_all)
    gate_on = jax.nn.sigmoid(gate_a)
    gate_act = gate_a * gate_on
    product = (gate_act * up_b).astype(bf16)

    def spread(partial):
        return lax.psum_scatter(partial.astype(bf16), "z", scatter_dimension=0, tiled=True)

    down_part = contract_rows(grad_all, product).astype(bf16)
    grad_down = spread(down_part)
    grad_product = times(after(grad_all, down_part), down_all)
    grad_a = (grad_product * up_b * gate_on * (1.0 + gate_a * (1.0 - gate_on))).astype(bf16)
    grad_b = (grad_product * gate_act).astype(bf16)
    far_mid = times_transpose(grad_a[half:], gate_all) + times_transpose(grad_b[half:], up_all)
    far_mid = far_mid.astype(bf16)
    near_mid = times_transpose(grad_a[:half], gate_all) + times_transpose(grad_b[:half], up_all)
    held_mid, held_a, held_b = lax.optimization_barrier((mid_all, grad_a, grad_b, near_mid))[:3]
    gate_part = contract_rows(held_mid, held_a).astype(bf16)
    up_part = contract_rows(held_mid, held_b).astype(bf16)
    grad_mid, gate_part, up_part, grad_down = scatter_group(
        near_mid, far_mid, (gate_part, up_part), (grad_down,)
    )
    grad_gate = spread(gate_part)
    grad_up = spread(up_part)
    grad_float = out_grad.astype(f32).reshape(tokens, features)
    grad_hidden = grad_float + rms_back(grad_mid * mid_gain, hidden, mid_rate)

    product_here = after(product, up_part)
    far_down = times_transpose(product_here[half:], down_all).astype(bf16)
    near_down = times_transpose(product_here[:half], down_all)
    first, sums = join(
        gather_first(grad_hidden.astype(bf16)), scatter_first(near_down, far_down)
    )
    near_gm = lay(gather_second(*first))
    far_gm = swap_row(near_gm)
    sums = scatter_second(*join(sums, near_gm)[0])
    grad_mixed = jnp.concatenate(
        [times_transpose(near_gm, out_here), times_transpose(far_gm, out_here)], axis=0
    ).reshape(by_block + (wide,))
    mixer_out = jnp.concatenate([near_out, far_out], axis=0)
    starts = jnp.concatenate([near_starts, far_starts], axis=0)
    starts_spec = pl.BlockSpec(
        (1, row_count, heads, width, width),
        lambda h, c, at_ref, docs_ref: (h * spots + spots - 1 - c, 0, 0, 0, 0),
    )
    all_grads, lows, parts, packed = local_call(
        open_kernel,
        at,
        docs,
        (qr, zv, mixer_out, grad_mixed, bias_here, gain_here, starts),
        [
            slab(2 * wide, behind),
            slab(2 * wide, behind),
            slab(wide, behind),
            slab(wide, behind),
            once,
            once,
            starts_spec,
        ],
        (
            jax.ShapeDtypeStruct(by_block + (4 * wide,), bf16),
            jax.ShapeDtypeStruct(by_block + (wide,), f32),
            jax.ShapeDtypeStruct(by_block + (wide,), f32),
            packed_shape,
        ),
        (slab(2 * wide, behind), slab(wide, behind), slab(wide, behind), by_half),
        (2, spots),
        (states, decays),
    )
    packed, sums, near_late, far_late = join(packed, sums, near_gm, far_gm)

    def out_rows():
        rows = contract_rows(near_mixed, near_late) + contract_rows(far_mixed, far_late)
        return rows.astype(bf16)

    def query_part():
        qr_grads = all_grads.reshape(2 * half, 4 * wide)[:, : 2 * wide]
        return contract_rows(normed_all, qr_grads).astype(bf16)

    def join_units(back):
        return back.astype(f32).transpose(1, 0, 2).reshape(block, spots * units)

    def turn_units(back):
        return back.transpose(0, 2, 1).reshape(spots * units, block).astype(f32)

    def units_back(cut):
        return over_plane(cut.reshape(spots, block, units))

    def beside(step):
        if step == 0:
            return (out_rows(), scatter_third(*sums))
        if step == 1:
            return (query_part(), turn_units(units_back(after(grad_down, later[0]))))
        if step == 2:
            return (join_units(units_back(after(grad_gate, later[1]))),)
        return ()

    later = []
    done = []
    for step in range(groups - 1):
        packed, extra = join(hop(packed, False), beside(step))
        later.append(packed)
        done += extra
    grad_out_rows, sums, qr_part, grad_down, grad_gate = done
    block_output = (hidden + scatter_last(*sums)).astype(bf16)
    if by_chip:
        cut = grad_out_rows.reshape(heads, 2, share, features)
        keep = lax.dynamic_index_in_dim(cut, own_row, 1, False)
        give = lax.dynamic_index_in_dim(cut, 1 - own_row, 1, False)
        take = swap_row(give)
        cut = jnp.concatenate(
            [jnp.where(own_first, keep, take), jnp.where(own_first, take, keep)], axis=0
        )
        grad_out = spread(cut.reshape(groups * share, features))
    else:
        placed = jnp.zeros((2, heads, spots, width, features), bf16)
        placed = lax.dynamic_update_slice(
            placed,
            grad_out_rows.reshape(1, heads, 1, width, features),
            (own_row, 0, own_spot, 0, 0),
        )
        grad_out = lax.psum_scatter(
            placed.reshape(features, features), everywhere, scatter_dimension=0, tiled=True
        )
    grad_qr = spread(qr_part)

    def behind_right(h, c, at_ref, docs_ref):
        return behind(h, c, at_ref, docs_ref)[:3] + (1,)

    all_grads, bias_part = local_call(
        close_kernel,
        at,
        docs,
        (all_grads, qr, zv, lows, parts, bias_here, starts, *later),
        [
            pl.BlockSpec(memory_space=pl.ANY),
            slab(2 * wide, behind),
            slab(2 * wide, behind),
            slab(wide, behind),
            slab(wide, behind),
            once,
            starts_spec,
        ]
        + [by_half] * len(later),
        (
            jax.ShapeDtypeStruct(by_block + (4 * wide,), bf16),
            jax.ShapeDtypeStruct((1, wide), f32),
        ),
        (slab(2 * wide, behind_right), once),
        (2, spots),
        (states,),
        {2: 0},
    )
    all_grads = all_grads.reshape(2 * half, 4 * wide)
    zv_part = contract_rows(normed_all, all_grads[:, 2 * wide :]).astype(bf16)
    grad_zv = spread(zv_part)
    late_grads = after(all_grads, zv_part)
    far_in = times_transpose(late_grads[half:], mixer_weights).astype(bf16)
    near_in = times_transpose(late_grads[:half], mixer_weights)
    bias_placed = jnp.zeros((2, heads, spots, width), f32)
    bias_placed = lax.dynamic_update_slice(
        bias_placed, bias_part.reshape(1, heads, 1, width), (own_row, 0, own_spot, 0)
    )
    bias_back = lax.all_to_all(
        bias_placed.reshape(groups * members, share), everywhere, 0, 0, tiled=True
    )
    grad_bias = jnp.sum(bias_back, axis=0)

    def join_heads(cut):
        back = over_group(cut.reshape(members, share, 2 * wide))
        back = back.reshape(spots, 2, share, 2, heads, width)
        return [
            back[:, :, :, at].transpose(2, 1, 3, 0, 4).reshape(share, features).astype(f32)
            for at in range(2)
        ]

    state, block_output, grad_out, grad_qr, grad_up = join(
        scatter_first(near_in, far_in), block_output, grad_out, grad_qr, grad_up
    )
    grad_out = grad_out.astype(f32)
    state, (query_back, outgate_back), grad_up, grad_out, block_output = join(
        scatter_second(*state),
        join_heads(grad_qr),
        join_units(units_back(grad_up)),
        grad_out,
        block_output,
    )
    grad_normed = scatter_last(*scatter_third(*state))
    input_grad = grad_hidden + rms_back(grad_normed * first_gain, input_float, first_rate)
    input_grad = input_grad.astype(bf16).reshape(block_input.shape)

    own_vectors = (norm_gain.astype(f32), mlp_gain.astype(f32), group_gain.astype(f32))
    grad_head_gain = jnp.sum(grad_out * w_out.astype(f32), axis=1) / own_vectors[2]

    mid_part = jnp.sum(grad_gate * w_gate.astype(f32) + grad_up * w_up.astype(f32), axis=1)
    mid_part = mid_part.reshape(2, share)
    mid_keep = lax.dynamic_index_in_dim(mid_part, own_row, 0, False)
    mid_give = lax.dynamic_index_in_dim(mid_part, 1 - own_row, 0, False)
    grad_mid_gain = (mid_keep + swap_row(mid_give)) / own_vectors[1]

    forget_back, input_back = join_heads(grad_zv)
    first_part = query_back * w_query.astype(f32) + outgate_back * w_outgate.astype(f32)
    first_part += forget_back * w_forget.astype(f32) + input_back * w_input.astype(f32)
    grad_first_gain = jnp.sum(first_part, axis=1) / own_vectors[0]

    return (
        block_output.reshape(block_input.shape),
        input_grad,
        query_back,
        forget_back,
        input_back,
        outgate_back,
        grad_out,
        grad_gate,
        grad_up,
        grad_down,
        grad_first_gain,
        grad_mid_gain,
        grad_head_gain,
        grad_bias,
    )


def solution(mesh):
    count, rows = mesh.devices.shape
    folded = Mesh(mesh.devices.reshape(count // 4, 2, 2, rows), everywhere)
    seq = ("z", "y", "x")
    token_spec = P("row", seq, None)
    matrix_spec = P(everywhere, None)
    vector_spec = P(everywhere)
    wide_spec = P(seq, "row")
    tall_spec = P("row", seq)
    in_specs = (
        (token_spec, token_spec, P("row", None))
        + (matrix_spec,) * 5
        + (wide_spec, wide_spec, tall_spec)
        + (vector_spec,) * 4
    )
    out_specs = (
        (token_spec, token_spec)
        + (matrix_spec,) * 5
        + (wide_spec, wide_spec, tall_spec)
        + (vector_spec,) * 4
    )
    return jax.shard_map(
        on_device, mesh=folded, in_specs=in_specs, out_specs=out_specs, check_vma=False
    )
```

```python
import jax
import jax.numpy as jnp
from jax import lax
from jax.experimental import pallas as pl
from jax.experimental.pallas import tpu as pltpu
from jax.sharding import Mesh, PartitionSpec as P

HEADS = 16

lower_bound = 0.85
span_bound = 1.0 - lower_bound
epsilon = 1e-06
f32 = jnp.float32
bf16 = jnp.bfloat16
swap = ((0, 1), (1, 0))
everywhere = ("z", "y", "x", "row")
group = ("y", "x", "row")
plane = ("y", "x")


def swap_x(a):
    return lax.ppermute(a, "x", swap)


def swap_y(a):
    return lax.ppermute(a, "y", swap)


def swap_row(a):
    return lax.ppermute(a, "row", swap)


def join(*groups):
    flat, tree = jax.tree.flatten(groups)
    return jax.tree.unflatten(tree, lax.optimization_barrier(flat))


def gather_first(a):
    return a, swap_x(a), swap_y(a)


def gather_second(a, from_x, from_y):
    half = a.shape[0] // 2
    return a, from_x, from_y, swap_y(from_x[:half]), swap_x(from_y[half:])


def lay_kernel(*refs):
    pieces, out_ref = refs[:-1], refs[-1]
    rows = out_ref.shape[0]
    start = 0
    for ref in pieces:
        block, low = start // rows, start % rows

        @pl.when(pl.program_id(0) == block)
        def _(ref=ref, low=low):
            out_ref[low : low + ref.shape[0], :] = ref[...]

        start += ref.shape[0]


def lay(pieces):
    rows, columns = pieces[0].shape
    total = sum(piece.shape[0] for piece in pieces)
    return pl.pallas_call(
        lay_kernel,
        grid=(total // rows,),
        in_specs=[pl.BlockSpec(piece.shape, lambda step: (0, 0)) for piece in pieces],
        out_specs=pl.BlockSpec((rows, columns), lambda step: (step, 0)),
        out_shape=jax.ShapeDtypeStruct((total, columns), pieces[0].dtype),
        compiler_params=pltpu.CompilerParams(
            dimension_semantics=("arbitrary",), vmem_limit_bytes=48 * 1024 * 1024
        ),
    )(*pieces)


def gather_last(near):
    return lay(near + tuple(swap_row(piece) for piece in near))


def gather_group(a):
    return gather_last(gather_second(*gather_first(a)))


def scatter_second(left, right, to_x, to_y):
    return left, right, swap_x(to_x), swap_y(to_y)


def scatter_sums(left, right, from_x, from_y):
    left = left + from_x.astype(f32)
    right = right + from_y.astype(f32)
    return left[0], right[0], left[1].astype(bf16), right[1].astype(bf16)


def scatter_fourth(left, right, to_y, to_x):
    return left, right, swap_y(to_y), swap_x(to_x)


def scatter_third(*state):
    return scatter_fourth(*scatter_sums(*state))


def scatter_last(left, right, from_y, from_x):
    return jnp.concatenate([left + from_y.astype(f32), right + from_x.astype(f32)], axis=-1)


def scatter_group(state, first=(), second=()):
    state, first = join(scatter_second(*state), first)
    state, second = join(scatter_third(*state), second)
    return scatter_last(*state), *first, *second


def hop(packed, forward):
    count = lax.axis_size("z")
    if forward:
        pairs = [(i, i + 1) for i in range(count - 1)]
    else:
        pairs = [(i + 1, i) for i in range(count - 1)]
    return lax.ppermute(packed, "z", pairs)


def relay(packed, forward):
    got = []
    for _ in range(lax.axis_size("z") - 1):
        packed = hop(packed, forward)
        got.append(packed)
    return got


def pair(values):
    high = values.astype(bf16)
    return high, (values - high.astype(f32)).astype(bf16)


def mm(a, b, dims):
    def dot(left, right):
        return lax.dot_general(left, right, (dims, ((), ())), preferred_element_type=f32)

    return dot(a[0], b[0]) + (dot(a[0], b[1]) + dot(a[1], b[0]))


def split_sum(ones_matrix, values, dims):
    first = values.astype(bf16)
    rest = values - first.astype(f32)
    second = rest.astype(bf16)
    third = (rest - second.astype(f32)).astype(bf16)
    total = lax.dot_general(ones_matrix, first, (dims, ((), ())), preferred_element_type=f32)
    total += lax.dot_general(ones_matrix, second, (dims, ((), ())), preferred_element_type=f32)
    total += lax.dot_general(ones_matrix, third, (dims, ((), ())), preferred_element_type=f32)
    return total


NT = ((1,), (1,))
NN = ((1,), (0,))
TN = ((0,), (0,))


def chunk_masks(docs_ref, row_at, start, size):
    at_row = lax.broadcasted_iota(jnp.int32, (size, size), 0)
    at_col = lax.broadcasted_iota(jnp.int32, (size, size), 1)
    same = at_row >= at_col
    opened = at_row >= 0
    tail = at_row >= 0
    whole = jnp.bool_(True)
    for entry in range(docs_ref.shape[1]):
        place = docs_ref[row_at, entry] - start
        same = same & ~((at_col < place) & (place <= at_row))
        opened = opened & ~((0 <= place) & (place <= at_row))
        tail = tail & ~((at_row < place) & (place <= size - 1))
        whole = whole & ~((0 <= place) & (place <= size - 1))
    return same, opened, tail, whole


def decay_terms(logit, tri):
    forget = lower_bound + span_bound * jax.nn.sigmoid(logit)
    key = span_bound * jax.nn.sigmoid(-logit)
    log_sum = split_sum(tri, jnp.log(forget), NN)
    return forget, key, log_sum


def lower_ones(size):
    at_row = lax.broadcasted_iota(jnp.int32, (size, size), 0)
    at_col = lax.broadcasted_iota(jnp.int32, (size, size), 1)
    return (at_row >= at_col).astype(f32).astype(bf16)


PAD = 16


def pack_state(ref, row, head, state, decay):
    width = state.shape[0]
    high = decay.astype(bf16).astype(f32)
    at_row = lax.broadcasted_iota(jnp.int32, (PAD, width), 0)
    extra = jnp.where(at_row == 0, high, jnp.where(at_row == 1, decay - high, 0.0))
    ref[row, head, :width, :] = state.astype(bf16)
    ref[row, head, width:, :] = extra.astype(bf16)


def unpack_carry(refs, row, head):
    width = refs[0].shape[3]
    carry = None
    for ref in refs[::-1]:
        state = ref[row, head, :width, :].astype(f32)
        if carry is not None:
            extra = ref[row, head, width:, :].astype(f32)
            state = state + (extra[0:1] + extra[1:2]) * carry
        carry = state
    return carry


def state_kernel(at_ref, docs_ref, zv_ref, bias_ref, packed_ref, state, decay):
    rows, size = zv_ref.shape[1:3]
    heads, width = state.shape[1:3]
    half, chunk = pl.program_id(0), pl.program_id(1)
    tri = lower_ones(size)

    @pl.when(chunk == 0)
    def _():
        state[...] = jnp.zeros_like(state)
        decay[...] = jnp.ones_like(decay)

    for row in range(rows):
        _, _, tail, whole = chunk_masks(
            docs_ref, half * rows + row, at_ref[1] + chunk * size, size
        )
        for head in range(heads):
            low = head * width
            logit = zv_ref[0, row, :, low : low + width] + bias_ref[:, low : low + width]
            value = zv_ref[0, row, :, heads * width + low : heads * width + low + width]
            _, key, log_sum = decay_terms(logit, tri)
            last = log_sum[size - 1 : size, :]
            passed = jnp.where(whole, jnp.exp(last), 0.0)
            weighted = jnp.where(tail, key * jnp.exp(last - log_sum), 0.0)
            state[row, head] = state[row, head] * passed + mm(pair(value), pair(weighted), TN)
            decay[row, head] = decay[row, head] * passed

    @pl.when(chunk == pl.num_programs(1) - 1)
    def _():
        for row in range(rows):
            for head in range(heads):
                pack_state(packed_ref, row, head, state[row, head], decay[row, head])


def forward_kernel(half, at_ref, docs_ref, qr_ref, zv_ref, bias_ref, gain_ref, *rest):
    carry_refs, (out_ref, mixed_ref, starts_ref, state) = rest[:-4], rest[-4:]
    rows, size = qr_ref.shape[1:3]
    heads, width = state.shape[1:3]
    chunk = pl.program_id(0)
    tri = lower_ones(size)

    @pl.when(chunk == 0)
    def _():
        for row in range(rows):
            for head in range(heads):
                state[row, head] = unpack_carry(carry_refs, row, head)

    for row in range(rows):
        same, opened, tail, whole = chunk_masks(
            docs_ref, half * rows + row, at_ref[1] + chunk * size, size
        )
        for head in range(heads):
            low = head * width
            high = (heads + head) * width
            query = qr_ref[0, row, :, low : low + width]
            gate = qr_ref[0, row, :, high : high + width]
            logit = zv_ref[0, row, :, low : low + width] + bias_ref[:, low : low + width]
            value = pair(zv_ref[0, row, :, high : high + width])
            _, key, log_sum = decay_terms(logit, tri)
            last = log_sum[size - 1 : size, :]
            lifted = pair(query * jax.nn.sigmoid(query) * jnp.exp(log_sum))
            lowered = pair(key * jnp.exp(-log_sum))
            scores = pair(jnp.where(same, mm(lifted, lowered, NT), 0.0))
            begin = state[row, head]
            starts_ref[0, row, head] = begin
            out = mm(scores, value, NN) + jnp.where(opened, mm(lifted, pair(begin), NT), 0.0)
            passed = jnp.where(whole, jnp.exp(last), 0.0)
            weighted = jnp.where(tail, key * jnp.exp(last - log_sum), 0.0)
            state[row, head] = begin * passed + mm(value, pair(weighted), TN)
            scale = lax.rsqrt(jnp.mean(out * out, axis=-1, keepdims=True) + epsilon)
            normed = out * scale * gain_ref[:, low : low + width]
            out_ref[0, row, :, low : low + width] = out
            mixed_ref[0, row, :, low : low + width] = (
                normed * (gate * jax.nn.sigmoid(gate))
            ).astype(bf16)


def open_kernel(
    at_ref,
    docs_ref,
    qr_ref,
    zv_ref,
    out_ref,
    grad_ref,
    bias_ref,
    gain_ref,
    starts_ref,
    qr_grad_ref,
    low_ref,
    part_ref,
    packed_ref,
    state,
    decay,
):
    rows, size = qr_ref.shape[1:3]
    heads, width = state.shape[1:3]
    half, step = pl.program_id(0), pl.program_id(1)
    chunk = pl.num_programs(1) - 1 - step
    tri = lower_ones(size)

    @pl.when(step == 0)
    def _():
        state[...] = jnp.zeros_like(state)
        decay[...] = jnp.ones_like(decay)

    for row in range(rows):
        same, opened, _, whole = chunk_masks(
            docs_ref, half * rows + row, at_ref[1] + chunk * size, size
        )
        for head in range(heads):
            low = head * width
            high = (heads + head) * width
            query = qr_ref[0, row, :, low : low + width]
            gate = qr_ref[0, row, :, high : high + width]
            logit = zv_ref[0, row, :, low : low + width] + bias_ref[:, low : low + width]
            value = pair(zv_ref[0, row, :, high : high + width])
            out = out_ref[0, row, :, low : low + width]
            grad_mixed = grad_ref[0, row, :, low : low + width] * gain_ref[:, low : low + width]
            _, key, log_sum = decay_terms(logit, tri)
            last = log_sum[size - 1 : size, :]
            rise = jnp.exp(log_sum)
            query_on = jax.nn.sigmoid(query)
            lifted = query * query_on * rise
            lowered = pair(key * jnp.exp(-log_sum))
            gate_on = jax.nn.sigmoid(gate)
            scale = lax.rsqrt(jnp.mean(out * out, axis=-1, keepdims=True) + epsilon)
            normed = out * scale
            grad_normed = grad_mixed * (gate * gate_on)
            grad_out = scale * (
                grad_normed - normed * jnp.mean(grad_normed * normed, axis=-1, keepdims=True)
            )
            grad_low = pair(grad_out)
            grad_scores = pair(jnp.where(same, mm(grad_low, value, NT), 0.0))
            grad_lifted = mm(grad_scores, lowered, NN) + jnp.where(
                opened, mm(grad_low, pair(starts_ref[0, row, head]), NN), 0.0
            )
            grad_query = grad_lifted * rise * query_on * (1.0 + query * (1.0 - query_on))
            grad_gate = grad_mixed * normed * gate_on * (1.0 + gate * (1.0 - gate_on))
            qr_grad_ref[0, row, :, low : low + width] = grad_query.astype(bf16)
            qr_grad_ref[0, row, :, high : high + width] = grad_gate.astype(bf16)
            low_ref[0, row, :, low : low + width] = grad_out
            part_ref[0, row, :, low : low + width] = grad_lifted * lifted
            passed = jnp.where(whole, jnp.exp(last), 0.0)
            state[row, head] = state[row, head] * passed + mm(
                grad_low, pair(jnp.where(opened, lifted, 0.0)), TN
            )
            decay[row, head] = decay[row, head] * passed

    @pl.when(step == pl.num_programs(1) - 1)
    def _():
        for row in range(rows):
            for head in range(heads):
                pack_state(packed_ref, row, head, state[row, head], decay[row, head])


def close_kernel(
    at_ref, docs_ref, kept_ref, qr_ref, zv_ref, low_ref, part_ref, bias_ref, starts_ref, *rest
):
    carry_refs, (zv_grad_ref, bias_grad_ref, state) = rest[:-3], rest[-3:]
    rows, size = qr_ref.shape[1:3]
    heads, width = state.shape[1:3]
    half, step = pl.program_id(0), pl.program_id(1)
    chunk = pl.num_programs(1) - 1 - step
    tri = lower_ones(size)

    @pl.when((step == 0) & (half == 0))
    def _():
        bias_grad_ref[...] = jnp.zeros_like(bias_grad_ref)

    @pl.when(step == 0)
    def _():
        for row in range(rows):
            for head in range(heads):
                state[row, head] = unpack_carry(carry_refs, row, head)

    for row in range(rows):
        same, opened, tail, whole = chunk_masks(
            docs_ref, half * rows + row, at_ref[1] + chunk * size, size
        )
        for head in range(heads):
            low = head * width
            high = (heads + head) * width
            query = qr_ref[0, row, :, low : low + width]
            logit = zv_ref[0, row, :, low : low + width] + bias_ref[:, low : low + width]
            value = pair(zv_ref[0, row, :, high : high + width])
            grad_low = pair(low_ref[0, row, :, low : low + width])
            forget, key, log_sum = decay_terms(logit, tri)
            last = log_sum[size - 1 : size, :]
            fall = jnp.exp(-log_sum)
            remain = jnp.where(tail, jnp.exp(last - log_sum), 0.0)
            lifted = query * jax.nn.sigmoid(query) * jnp.exp(log_sum)
            lowered = key * fall
            weighted = key * remain
            lifted_low = pair(lifted)
            scores = pair(jnp.where(same, mm(lifted_low, pair(lowered), NT), 0.0))
            begin = starts_ref[0, row, head]
            later = state[row, head]
            later_low = pair(later)
            grad_scores = pair(jnp.where(same, mm(grad_low, value, NT), 0.0))
            grad_value = mm(scores, grad_low, TN) + mm(pair(weighted), later_low, NT)
            grad_lowered = mm(grad_scores, lifted_low, TN)
            grad_weighted = mm(value, later_low, NN)
            passed = jnp.where(whole, jnp.exp(last), 0.0)
            open_lifted = pair(jnp.where(opened, lifted, 0.0))
            state[row, head] = later * passed + mm(grad_low, open_lifted, TN)
            through = jnp.sum(begin * later, axis=0, keepdims=True) * passed
            weighted_part = grad_weighted * weighted
            grad_log = (
                part_ref[0, row, :, low : low + width]
                - grad_lowered * lowered
                - weighted_part
            )
            grad_last = through + jnp.sum(weighted_part, axis=0, keepdims=True)
            grad_step = split_sum(tri, grad_log, TN) + grad_last
            grad_key = grad_lowered * fall + grad_weighted * remain
            grad_logit = (
                span_bound
                * jax.nn.sigmoid(logit)
                * jax.nn.sigmoid(-logit)
                * (grad_step / forget - grad_key)
            )
            bias_grad_ref[:, low : low + width] += jnp.sum(grad_logit, axis=0, keepdims=True)
            zv_grad_ref[0, row, :, low : low + width] = grad_logit.astype(bf16)
            zv_grad_ref[0, row, :, high : high + width] = grad_value.astype(bf16)


def local_call(
    kernel, at, docs, ins, in_specs, out_shapes, out_specs, grid, scratch, aliases=None
):
    return pl.pallas_call(
        kernel,
        grid_spec=pltpu.PrefetchScalarGridSpec(
            num_scalar_prefetch=2,
            grid=grid,
            in_specs=in_specs,
            out_specs=out_specs,
            scratch_shapes=scratch,
        ),
        out_shape=out_shapes,
        input_output_aliases=aliases or {},
        compiler_params=pltpu.CompilerParams(
            dimension_semantics=("arbitrary",) * len(grid), vmem_limit_bytes=48 * 1024 * 1024
        ),
    )(at, docs, *ins)


def big_call(kernel, grid, ins, in_specs, out_shapes, out_specs):
    return pl.pallas_call(
        kernel,
        grid=grid,
        in_specs=in_specs,
        out_shape=out_shapes,
        out_specs=out_specs,
        compiler_params=pltpu.CompilerParams(
            dimension_semantics=("arbitrary",) * len(grid), vmem_limit_bytes=48 * 1024 * 1024
        ),
    )(*ins)


def up_kernel(in_ref, pair_ref, slope_ref, product_ref):
    both = jnp.dot(in_ref[...], pair_ref[...], preferred_element_type=f32)
    units = both.shape[1] // 2
    gate, up = both[:, :units], both[:, units:]
    gate_on = jax.nn.sigmoid(gate)
    active = gate * gate_on
    product_ref[...] = (active * up).astype(bf16)
    slope_ref[0] = up * (gate_on + active * (1.0 - gate_on))
    slope_ref[1] = active


def down_kernel(grad_ref, down_ref, slope_ref, out_ref):
    grad = jnp.dot(grad_ref[...], down_ref[...], preferred_element_type=f32)
    out_ref[...] = jnp.concatenate(
        [grad * slope_ref[0], grad * slope_ref[1]], axis=-1
    ).astype(bf16)


def feed_up(mid_all, pair_all, tile):
    rows, features = mid_all.shape
    units = pair_all.shape[1]
    return big_call(
        up_kernel,
        (rows // tile,),
        (mid_all, pair_all),
        [
            pl.BlockSpec((tile, features), lambda i: (i, 0)),
            pl.BlockSpec((features, units), lambda i: (0, 0)),
        ],
        (
            jax.ShapeDtypeStruct((2, rows, units // 2), f32),
            jax.ShapeDtypeStruct((rows, units // 2), bf16),
        ),
        (
            pl.BlockSpec((2, tile, units // 2), lambda i: (0, i, 0)),
            pl.BlockSpec((tile, units // 2), lambda i: (i, 0)),
        ),
    )


def feed_back(grad_all, down_all, both, tile):
    rows, features = grad_all.shape
    units = 2 * both.shape[2]
    return big_call(
        down_kernel,
        (rows // tile,),
        (grad_all, down_all, both),
        [
            pl.BlockSpec((tile, features), lambda i: (i, 0)),
            pl.BlockSpec((features, units // 2), lambda i: (0, 0)),
            pl.BlockSpec((2, tile, units // 2), lambda i: (0, i, 0)),
        ],
        jax.ShapeDtypeStruct((rows, units), bf16),
        pl.BlockSpec((tile, units), lambda i: (i, 0)),
    )


def scatter_product(left, far_left, right, tile):
    depth = left.shape[1]
    columns = right.shape[1]
    half = columns // 2

    def dot(a_ref, b_ref):
        return jnp.dot(a_ref[...], b_ref[...], preferred_element_type=f32)

    def right_spec(side):
        return pl.BlockSpec((depth, half), lambda *_: (0, side))

    def far_kernel(a_ref, b_ref, out_ref):
        out_ref[...] = dot(a_ref, b_ref).astype(bf16)

    def far_part(side):
        return big_call(
            far_kernel,
            (4,),
            (far_left, right),
            [pl.BlockSpec((tile, depth), lambda i: (i, 0)), right_spec(side)],
            jax.ShapeDtypeStruct((4 * tile, half), bf16),
            pl.BlockSpec((tile, half), lambda i: (i, 0)),
        )

    def near_part(side, got):
        def kernel(a_ref, b_ref, got_ref, keep_ref, send_ref):
            value = dot(a_ref, b_ref) + got_ref[...].astype(f32)
            sent = pl.program_id(0) if side else pl.program_id(1)

            @pl.when(sent == 0)
            def _():
                keep_ref[0] = value

            @pl.when(sent == 1)
            def _():
                send_ref[0] = value.astype(bf16)

        if side:
            keep_at = lambda y, x: (jnp.where(y == 0, x, 1), 0, 0)
            send_at = lambda y, x: (jnp.where(y == 0, 0, x), 0, 0)
        else:
            keep_at = lambda y, x: (y, 0, 0)
            send_at = lambda y, x: (y, 0, 0)
        return big_call(
            kernel,
            (2, 2),
            (left, right, got),
            [
                pl.BlockSpec((tile, depth), lambda y, x: (2 * y + x, 0)),
                right_spec(side),
                pl.BlockSpec((tile, half), lambda y, x: (2 * y + x, 0)),
            ],
            (
                jax.ShapeDtypeStruct((2, tile, half), f32),
                jax.ShapeDtypeStruct((2, tile, half), bf16),
            ),
            (
                pl.BlockSpec((1, tile, half), keep_at),
                pl.BlockSpec((1, tile, half), send_at),
            ),
        )

    got = [swap_row(far_part(side)) for side in range(2)]
    (keep_left, to_x), (keep_right, to_y) = [near_part(side, got[side]) for side in range(2)]
    return keep_left, keep_right, to_x, to_y


def scatter_turned(left, right):
    half = left.shape[0] // 2
    far = times_transpose(left[half:], right).astype(bf16)
    near = times_transpose(left[:half], right)
    rows, columns = near.shape
    mine = (near + swap_row(far).astype(f32)).reshape(2, 2, rows // 4, columns)
    left_side, right_side = mine[..., : columns // 2], mine[..., columns // 2 :]
    return (
        left_side[:, 0],
        right_side[0],
        left_side[:, 1].astype(bf16),
        right_side[1].astype(bf16),
    )


def contract_rows(left, right):
    return lax.dot_general(left, right, (TN, ((), ())), preferred_element_type=f32)


def times_transpose(left, right):
    return lax.dot_general(left, right, (NT, ((), ())), preferred_element_type=f32)


def times(left, right):
    return jnp.dot(left, right, preferred_element_type=f32)


def rms_rate(values):
    return lax.rsqrt(jnp.mean(values * values, axis=-1, keepdims=True) + epsilon)


def rms_back(grad, values, rate):
    return rate * grad - values * (
        rate * rate * rate * jnp.mean(grad * values, axis=-1, keepdims=True)
    )


def on_device(
    block_input,
    out_grad,
    doc_starts,
    w_query,
    w_forget,
    w_input,
    w_outgate,
    w_out,
    w_gate,
    w_up,
    w_down,
    norm_gain,
    mlp_gain,
    group_gain,
    forget_bias,
):
    row_count, span, features = block_input.shape
    groups = lax.axis_size("z")
    own_row = lax.axis_index("row")
    own_spot = lax.axis_index("y") * 2 + lax.axis_index("x")
    own_first = own_row == 0
    spots, members = 4, 8
    tokens = row_count * span
    width = features // HEADS
    heads = HEADS // members
    wide = heads * width
    share = w_query.shape[0]
    units = w_gate.shape[1] // spots
    block = w_gate.shape[0]
    half = spots * tokens

    by_chip = 2 * share == width and groups == 2 * heads
    if by_chip:
        held = lax.all_gather(w_out, "z", axis=0, tiled=False).reshape(2, heads, share, features)
    else:
        held = lax.all_gather(w_out, everywhere, axis=0, tiled=True)

    def cut_heads(first, second):
        both = jnp.stack([first, second]).reshape(2, share, 2, heads, spots, width)
        return both.transpose(4, 2, 1, 0, 3, 5).reshape(members, share, 2 * wide)

    def over_group(cut):
        return lax.all_to_all(cut, group, 0, 0, tiled=True)

    def over_plane(cut):
        return lax.all_to_all(cut, plane, 0, 0, tiled=True)

    def over_groups(cut):
        flat = cut.reshape(cut.shape[0] * cut.shape[1], cut.shape[2])
        return lax.all_gather(flat, "z", axis=0, tiled=True)

    vectors = jnp.stack([norm_gain, mlp_gain, group_gain, forget_bias]).astype(f32)
    vectors = jnp.broadcast_to(vectors.reshape(1, 4 * share), (groups * members, 4 * share))
    vectors = lax.all_to_all(vectors, everywhere, 0, 0, tiled=True)
    mixer_cut, vectors = join(
        jnp.stack([cut_heads(w_forget, w_input), cut_heads(w_query, w_outgate)], axis=1), vectors
    )
    mixer_cut = over_group(mixer_cut)
    zv_all = over_groups(mixer_cut[:, 0])
    qr_all = over_groups(mixer_cut[:, 1])

    vectors = vectors.reshape(groups * members, 4, share).transpose(1, 0, 2).reshape(4, features)
    here = lax.dynamic_index_in_dim(
        vectors.reshape(4, 2, heads, spots, width), own_row, 1, False
    )
    here = lax.dynamic_index_in_dim(here, own_spot, 2, False).reshape(4, wide)
    first_gain, mid_gain = vectors[0:1], vectors[1:2]
    gain_here, bias_here = here[2:3], here[3:4]

    input_float = block_input.astype(f32).reshape(tokens, features)
    first_rate = rms_rate(input_float)
    normed = (input_float * first_rate * first_gain).astype(bf16)
    pair_cut = jnp.concatenate(
        [w_gate.reshape(block, spots, units), w_up.reshape(block, spots, units)], axis=-1
    ).transpose(1, 0, 2)
    down_cut = w_down.T.reshape(block, spots, units).transpose(1, 0, 2)

    first, pair_cut, down_cut = join(gather_first(normed), pair_cut, down_cut)
    normed_all = gather_last(gather_second(*first))

    docs = jnp.concatenate([doc_starts, swap_row(doc_starts)], axis=0)
    at = jnp.stack([own_spot, lax.axis_index("z") * (spots * span)]).astype(jnp.int32)
    by_block = (members, row_count, span)
    zv = times(normed_all, zv_all).reshape(by_block + (2 * wide,))
    zv, pair_cut, down_cut = join(zv, pair_cut, down_cut)
    pair_cut = over_plane(pair_cut)

    once = pl.BlockSpec((1, wide), lambda *_: (0, 0))
    packed_block = (row_count, heads, width + PAD, width)
    packed_shape = jax.ShapeDtypeStruct((2 * row_count,) + packed_block[1:], bf16)
    states = pltpu.VMEM((row_count, heads, width, width), f32)
    decays = pltpu.VMEM((row_count, heads, 1, width), f32)

    def slab(columns, index):
        return pl.BlockSpec((1, row_count, span, columns), index)

    def ahead(h, c, at_ref, docs_ref):
        return (h * spots + (c ^ at_ref[0]), 0, 0, 0)

    def behind(h, c, at_ref, docs_ref):
        return (h * spots + ((spots - 1 - c) ^ at_ref[0]), 0, 0, 0)

    by_half = pl.BlockSpec(packed_block, lambda h, c, at_ref, docs_ref: (h, 0, 0, 0))

    packed = local_call(
        state_kernel,
        at,
        docs,
        (zv, bias_here),
        [slab(2 * wide, ahead), once],
        packed_shape,
        by_half,
        (2, spots),
        (states, decays),
    )
    grad_low = out_grad.reshape(tokens, features)

    carried = []
    for step in range(groups - 1):
        packed = hop(packed, True)
        if step == 0:
            packed, pair_cut = join(packed, pair_cut.reshape(spots * block, 2 * units))
            grad_sent, down_cut, pair_cut = join(grad_low, down_cut, pair_cut)
            pair_all = lax.all_gather(pair_cut, "z", axis=0, tiled=True)
            near = gather_second(*gather_first(grad_sent))
            down_cut = over_plane(down_cut).reshape(spots * block, units)
        carried.append(packed)
    qr = times(normed_all, qr_all)
    carried, near, qr, down_cut = join(carried, near, qr, down_cut)
    down_all = lax.all_gather(down_cut, "z", axis=0, tiled=True)
    grad_all = gather_last(near)
    qr = qr.reshape(by_block + (2 * wide,))

    def forward_half(side, qr):
        def place(c, at_ref, docs_ref):
            return (side * spots + (c ^ at_ref[0]), 0, 0, 0)

        def local(c, at_ref, docs_ref):
            return (c ^ at_ref[0], 0, 0, 0)

        def kernel(*refs):
            forward_kernel(side, *refs)

        return local_call(
            kernel,
            at,
            docs,
            (qr, zv, bias_here, gain_here, *carried),
            [slab(2 * wide, place), slab(2 * wide, place), once, once]
            + [pl.BlockSpec(packed_block, lambda c, at_ref, docs_ref: (side, 0, 0, 0))]
            * len(carried),
            (
                jax.ShapeDtypeStruct((spots,) + by_block[1:] + (wide,), f32),
                jax.ShapeDtypeStruct((spots,) + by_block[1:] + (wide,), bf16),
                jax.ShapeDtypeStruct((spots, row_count, heads, width, width), f32),
            ),
            (
                slab(wide, local),
                slab(wide, local),
                pl.BlockSpec(
                    (1, row_count, heads, width, width),
                    lambda c, at_ref, docs_ref: (c, 0, 0, 0, 0),
                ),
            ),
            (spots,),
            (states,),
        )

    if by_chip:
        keep = lax.dynamic_index_in_dim(held, own_row, 0, False)
        give = lax.dynamic_index_in_dim(held, 1 - own_row, 0, False)
        take = swap_row(give)
        out_here = jnp.stack(
            [jnp.where(own_first, keep, take), jnp.where(own_first, take, keep)], axis=1
        ).reshape(wide, features)
    else:
        held = held.reshape(2, heads, spots, width, features)
        held = lax.dynamic_index_in_dim(held, own_row, 0, False)
        out_here = lax.dynamic_index_in_dim(held, own_spot, 1, False).reshape(wide, features)

    far_out, far_mixed, far_starts = forward_half(1, qr)
    far_mixed = far_mixed.reshape(half, wide)
    near_out, near_mixed, near_starts = forward_half(0, qr)
    near_mixed = near_mixed.reshape(half, wide)
    state = scatter_product(near_mixed, far_mixed, out_here, tokens)
    hidden = input_float + scatter_group(state)[0]

    mid_rate = rms_rate(hidden)
    first, grad_all, mixer_weights = join(
        gather_first((hidden * mid_rate * mid_gain).astype(bf16)),
        grad_all,
        jnp.concatenate([qr_all, zv_all], axis=1),
    )
    mid_all = gather_last(gather_second(*first))
    both, product = feed_up(mid_all, pair_all, tokens)

    def spread(partial):
        return lax.psum_scatter(partial.astype(bf16), "z", scatter_dimension=0, tiled=True)

    down_part = contract_rows(grad_all, product).astype(bf16)
    grad_down = spread(down_part)
    grad_both = feed_back(grad_all, down_all, both, tokens)
    state, mid_late, both_late, product = join(
        scatter_turned(grad_both, pair_all), mid_all, grad_both, product
    )
    pair_part = contract_rows(mid_late, both_late).astype(bf16)
    grad_mid, pair_part, grad_down = scatter_group(state, (pair_part,), (grad_down,))
    grad_pair = spread(pair_part)
    grad_float = out_grad.astype(f32).reshape(tokens, features)
    grad_hidden = grad_float + rms_back(grad_mid * mid_gain, hidden, mid_rate)

    first, sums = join(
        gather_first(grad_hidden.astype(bf16)),
        scatter_turned(product, down_all),
    )
    near_gm = lay(gather_second(*first))
    far_gm = swap_row(near_gm)
    sums = scatter_second(*join(sums, near_gm)[0])
    grad_mixed = jnp.concatenate(
        [times_transpose(near_gm, out_here), times_transpose(far_gm, out_here)], axis=0
    ).reshape(by_block + (wide,))
    mixer_out = jnp.concatenate([near_out, far_out], axis=0)
    starts = jnp.concatenate([near_starts, far_starts], axis=0)
    starts_spec = pl.BlockSpec(
        (1, row_count, heads, width, width),
        lambda h, c, at_ref, docs_ref: (h * spots + spots - 1 - c, 0, 0, 0, 0),
    )
    all_grads, lows, parts, packed = local_call(
        open_kernel,
        at,
        docs,
        (qr, zv, mixer_out, grad_mixed, bias_here, gain_here, starts),
        [
            slab(2 * wide, behind),
            slab(2 * wide, behind),
            slab(wide, behind),
            slab(wide, behind),
            once,
            once,
            starts_spec,
        ],
        (
            jax.ShapeDtypeStruct(by_block + (4 * wide,), bf16),
            jax.ShapeDtypeStruct(by_block + (wide,), f32),
            jax.ShapeDtypeStruct(by_block + (wide,), f32),
            packed_shape,
        ),
        (slab(2 * wide, behind), slab(wide, behind), slab(wide, behind), by_half),
        (2, spots),
        (states, decays),
    )
    packed, sums, near_late, far_late = join(packed, sums, near_gm, far_gm)

    def out_rows():
        rows = contract_rows(near_mixed, near_late) + contract_rows(far_mixed, far_late)
        return rows.astype(bf16)

    def query_part():
        qr_grads = all_grads.reshape(2 * half, 4 * wide)[:, : 2 * wide]
        return contract_rows(normed_all, qr_grads).astype(bf16)

    def turn_units(back):
        return back.transpose(0, 2, 1).reshape(spots * units, block).astype(f32)

    def pair_parts(back):
        return [
            jnp.concatenate(
                [back[spot, :, low : low + units].astype(f32) for spot in range(spots)], axis=1
            )
            for low in (0, units)
        ]

    packed, grad_down = join(packed, grad_down)
    down_back = over_plane(grad_down.reshape(spots, block, units))
    pair_back = over_plane(grad_pair.reshape(spots, block, 2 * units))

    def beside(step):
        if step == 0:
            return (out_rows(), scatter_third(*sums), down_back)
        if step == 1:
            return (query_part(), turn_units(done[2]), pair_back)
        if step == 2:
            return tuple(pair_parts(done[5]))
        return ()

    later = []
    done = []
    for step in range(groups - 1):
        packed, extra = join(hop(packed, False), beside(step))
        later.append(packed)
        done += extra
    grad_out_rows, sums, _, qr_part, grad_down, _, grad_gate, grad_up = done
    block_output = (hidden + scatter_last(*sums)).astype(bf16)
    if by_chip:
        cut = grad_out_rows.reshape(heads, 2, share, features)
        keep = lax.dynamic_index_in_dim(cut, own_row, 1, False)
        give = lax.dynamic_index_in_dim(cut, 1 - own_row, 1, False)
        take = swap_row(give)
        cut = jnp.concatenate(
            [jnp.where(own_first, keep, take), jnp.where(own_first, take, keep)], axis=0
        )
        grad_out = spread(cut.reshape(groups * share, features))
    else:
        placed = jnp.zeros((2, heads, spots, width, features), bf16)
        placed = lax.dynamic_update_slice(
            placed,
            grad_out_rows.reshape(1, heads, 1, width, features),
            (own_row, 0, own_spot, 0, 0),
        )
        grad_out = lax.psum_scatter(
            placed.reshape(features, features), everywhere, scatter_dimension=0, tiled=True
        )
    grad_qr = spread(qr_part)

    def behind_right(h, c, at_ref, docs_ref):
        return behind(h, c, at_ref, docs_ref)[:3] + (1,)

    all_grads, bias_part = local_call(
        close_kernel,
        at,
        docs,
        (all_grads, qr, zv, lows, parts, bias_here, starts, *later),
        [
            pl.BlockSpec(memory_space=pl.ANY),
            slab(2 * wide, behind),
            slab(2 * wide, behind),
            slab(wide, behind),
            slab(wide, behind),
            once,
            starts_spec,
        ]
        + [by_half] * len(later),
        (
            jax.ShapeDtypeStruct(by_block + (4 * wide,), bf16),
            jax.ShapeDtypeStruct((1, wide), f32),
        ),
        (slab(2 * wide, behind_right), once),
        (2, spots),
        (states,),
        {2: 0},
    )
    all_grads = all_grads.reshape(2 * half, 4 * wide)
    zv_part = contract_rows(normed_all, all_grads[:, 2 * wide :]).astype(bf16)
    late_grads, zv_part = join(all_grads, zv_part)
    grad_zv = spread(zv_part)
    state = scatter_turned(late_grads, mixer_weights)
    bias_placed = jnp.zeros((2, heads, spots, width), f32)
    bias_placed = lax.dynamic_update_slice(
        bias_placed, bias_part.reshape(1, heads, 1, width), (own_row, 0, own_spot, 0)
    )
    bias_back = lax.all_to_all(
        bias_placed.reshape(groups * members, share), everywhere, 0, 0, tiled=True
    )
    grad_bias = jnp.sum(bias_back, axis=0)

    def join_heads(cut):
        back = over_group(cut.reshape(members, share, 2 * wide))
        back = back.reshape(spots, 2, share, 2, heads, width)
        return [
            back[:, :, :, at].transpose(2, 1, 3, 0, 4).reshape(share, features).astype(f32)
            for at in range(2)
        ]

    state, block_output, grad_out, grad_qr = join(state, block_output, grad_out, grad_qr)
    grad_out = grad_out.astype(f32)
    state, (query_back, outgate_back), grad_out, block_output = join(
        scatter_second(*state), join_heads(grad_qr), grad_out, block_output
    )
    state, grad_zv = join(scatter_sums(*state), grad_zv)
    state, (forget_back, input_back) = join(scatter_fourth(*state), join_heads(grad_zv))
    grad_normed = scatter_last(*state)
    input_grad = grad_hidden + rms_back(grad_normed * first_gain, input_float, first_rate)
    input_grad = input_grad.astype(bf16).reshape(block_input.shape)

    own_vectors = (norm_gain.astype(f32), mlp_gain.astype(f32), group_gain.astype(f32))
    grad_head_gain = jnp.sum(grad_out * w_out.astype(f32), axis=1) / own_vectors[2]

    mid_part = jnp.sum(grad_gate * w_gate.astype(f32) + grad_up * w_up.astype(f32), axis=1)
    mid_part = mid_part.reshape(2, share)
    mid_keep = lax.dynamic_index_in_dim(mid_part, own_row, 0, False)
    mid_give = lax.dynamic_index_in_dim(mid_part, 1 - own_row, 0, False)
    grad_mid_gain = (mid_keep + swap_row(mid_give)) / own_vectors[1]

    first_part = query_back * w_query.astype(f32) + outgate_back * w_outgate.astype(f32)
    first_part += forget_back * w_forget.astype(f32) + input_back * w_input.astype(f32)
    grad_first_gain = jnp.sum(first_part, axis=1) / own_vectors[0]

    return (
        block_output.reshape(block_input.shape),
        input_grad,
        query_back,
        forget_back,
        input_back,
        outgate_back,
        grad_out,
        grad_gate,
        grad_up,
        grad_down,
        grad_first_gain,
        grad_mid_gain,
        grad_head_gain,
        grad_bias,
    )


def solution(mesh):
    count, rows = mesh.devices.shape
    folded = Mesh(mesh.devices.reshape(count // 4, 2, 2, rows), everywhere)
    seq = ("z", "y", "x")
    token_spec = P("row", seq, None)
    matrix_spec = P(everywhere, None)
    vector_spec = P(everywhere)
    wide_spec = P(seq, "row")
    tall_spec = P("row", seq)
    in_specs = (
        (token_spec, token_spec, P("row", None))
        + (matrix_spec,) * 5
        + (wide_spec, wide_spec, tall_spec)
        + (vector_spec,) * 4
    )
    out_specs = (
        (token_spec, token_spec)
        + (matrix_spec,) * 5
        + (wide_spec, wide_spec, tall_spec)
        + (vector_spec,) * 4
    )
    return jax.shard_map(
        on_device, mesh=folded, in_specs=in_specs, out_specs=out_specs, check_vma=False
    )
```

```python
import jax
import jax.numpy as jnp
from jax import lax
from jax.experimental import pallas as pl
from jax.experimental.pallas import tpu as pltpu
from jax.sharding import Mesh, PartitionSpec as P

HEADS = 16

lower_bound = 0.85
span_bound = 1.0 - lower_bound
epsilon = 1e-06
f32 = jnp.float32
bf16 = jnp.bfloat16
swap = ((0, 1), (1, 0))
everywhere = ("z", "y", "x", "row")
group = ("y", "x", "row")
plane = ("y", "x")


def swap_x(a):
    return lax.ppermute(a, "x", swap)


def swap_y(a):
    return lax.ppermute(a, "y", swap)


def swap_row(a):
    return lax.ppermute(a, "row", swap)


def join(*groups):
    flat, tree = jax.tree.flatten(groups)
    return jax.tree.unflatten(tree, lax.optimization_barrier(flat))


def gather_first(a):
    return a, swap_x(a), swap_y(a)


def gather_second(a, from_x, from_y):
    half = a.shape[0] // 2
    return a, from_x, from_y, swap_y(from_x[:half]), swap_x(from_y[half:])


def lay_kernel(*refs):
    pieces, out_ref = refs[:-1], refs[-1]
    rows = out_ref.shape[0]
    start = 0
    for ref in pieces:
        block, low = start // rows, start % rows

        @pl.when(pl.program_id(0) == block)
        def _(ref=ref, low=low):
            out_ref[low : low + ref.shape[0], :] = ref[...]

        start += ref.shape[0]


def lay(pieces):
    rows, columns = pieces[0].shape
    total = sum(piece.shape[0] for piece in pieces)
    return pl.pallas_call(
        lay_kernel,
        grid=(total // rows,),
        in_specs=[pl.BlockSpec(piece.shape, lambda step: (0, 0)) for piece in pieces],
        out_specs=pl.BlockSpec((rows, columns), lambda step: (step, 0)),
        out_shape=jax.ShapeDtypeStruct((total, columns), pieces[0].dtype),
        compiler_params=pltpu.CompilerParams(
            dimension_semantics=("arbitrary",), vmem_limit_bytes=48 * 1024 * 1024
        ),
    )(*pieces)


def gather_last(near):
    return lay(near + tuple(swap_row(piece) for piece in near))


def gather_group(a):
    return gather_last(gather_second(*gather_first(a)))


def scatter_second(left, right, to_x, to_y):
    return left, right, swap_x(to_x), swap_y(to_y)


def scatter_sums(left, right, from_x, from_y):
    left = left + from_x.astype(f32)
    right = right + from_y.astype(f32)
    return left[0], right[0], left[1].astype(bf16), right[1].astype(bf16)


def scatter_fourth(left, right, to_y, to_x):
    return left, right, swap_y(to_y), swap_x(to_x)


def scatter_third(*state):
    return scatter_fourth(*scatter_sums(*state))


def scatter_last(left, right, from_y, from_x):
    return jnp.concatenate([left + from_y.astype(f32), right + from_x.astype(f32)], axis=-1)


def scatter_group(state, first=(), second=()):
    state, first = join(scatter_second(*state), first)
    state, second = join(scatter_third(*state), second)
    return scatter_last(*state), *first, *second


def hop(packed, forward):
    count = lax.axis_size("z")
    if forward:
        pairs = [(i, i + 1) for i in range(count - 1)]
    else:
        pairs = [(i + 1, i) for i in range(count - 1)]
    return lax.ppermute(packed, "z", pairs)


def relay(packed, forward):
    got = []
    for _ in range(lax.axis_size("z") - 1):
        packed = hop(packed, forward)
        got.append(packed)
    return got


def pair(values):
    high = values.astype(bf16)
    return high, (values - high.astype(f32)).astype(bf16)


def mm(a, b, dims):
    def dot(left, right):
        return lax.dot_general(left, right, (dims, ((), ())), preferred_element_type=f32)

    return dot(a[0], b[0]) + (dot(a[0], b[1]) + dot(a[1], b[0]))


def split_sum(ones_matrix, values, dims):
    first = values.astype(bf16)
    rest = values - first.astype(f32)
    second = rest.astype(bf16)
    third = (rest - second.astype(f32)).astype(bf16)
    total = lax.dot_general(ones_matrix, first, (dims, ((), ())), preferred_element_type=f32)
    total += lax.dot_general(ones_matrix, second, (dims, ((), ())), preferred_element_type=f32)
    total += lax.dot_general(ones_matrix, third, (dims, ((), ())), preferred_element_type=f32)
    return total


NT = ((1,), (1,))
NN = ((1,), (0,))
TN = ((0,), (0,))


def chunk_masks(docs_ref, row_at, start, size):
    at_row = lax.broadcasted_iota(jnp.int32, (size, size), 0)
    at_col = lax.broadcasted_iota(jnp.int32, (size, size), 1)
    same = at_row >= at_col
    opened = at_row >= 0
    tail = at_row >= 0
    whole = jnp.bool_(True)
    for entry in range(docs_ref.shape[1]):
        place = docs_ref[row_at, entry] - start
        same = same & ~((at_col < place) & (place <= at_row))
        opened = opened & ~((0 <= place) & (place <= at_row))
        tail = tail & ~((at_row < place) & (place <= size - 1))
        whole = whole & ~((0 <= place) & (place <= size - 1))
    return same, opened, tail, whole


def key_of(logit):
    return span_bound * jax.nn.sigmoid(-logit)


def forget_of(logit):
    return lower_bound + span_bound * jax.nn.sigmoid(logit)


def lower_ones(size):
    at_row = lax.broadcasted_iota(jnp.int32, (size, size), 0)
    at_col = lax.broadcasted_iota(jnp.int32, (size, size), 1)
    return (at_row >= at_col).astype(f32).astype(bf16)


PAD = 16


def pack_state(ref, row, head, state, decay):
    width = state.shape[0]
    high = decay.astype(bf16).astype(f32)
    at_row = lax.broadcasted_iota(jnp.int32, (PAD, width), 0)
    extra = jnp.where(at_row == 0, high, jnp.where(at_row == 1, decay - high, 0.0))
    ref[row, head, :width, :] = state.astype(bf16)
    ref[row, head, width:, :] = extra.astype(bf16)


def unpack_carry(refs, row, head):
    width = refs[0].shape[3]
    carry = None
    for ref in refs[::-1]:
        state = ref[row, head, :width, :].astype(f32)
        if carry is not None:
            extra = ref[row, head, width:, :].astype(f32)
            state = state + (extra[0:1] + extra[1:2]) * carry
        carry = state
    return carry


def state_kernel(at_ref, docs_ref, zv_ref, bias_ref, packed_ref, logs_ref, state, decay):
    rows, size = zv_ref.shape[1:3]
    heads, width = state.shape[1:3]
    half, chunk = pl.program_id(0), pl.program_id(1)
    tri = lower_ones(size)

    @pl.when(chunk == 0)
    def _():
        state[...] = jnp.zeros_like(state)
        decay[...] = jnp.ones_like(decay)

    for row in range(rows):
        _, _, tail, whole = chunk_masks(
            docs_ref, half * rows + row, at_ref[1] + chunk * size, size
        )
        for head in range(heads):
            low = head * width
            logit = zv_ref[0, row, :, low : low + width] + bias_ref[:, low : low + width]
            value = zv_ref[0, row, :, heads * width + low : heads * width + low + width]
            key = key_of(logit)
            log_sum = split_sum(tri, jnp.log(forget_of(logit)), NN)
            logs_ref[0, row, :, low : low + width] = log_sum
            last = log_sum[size - 1 : size, :]
            passed = jnp.where(whole, jnp.exp(last), 0.0)
            weighted = jnp.where(tail, key * jnp.exp(last - log_sum), 0.0)
            state[row, head] = state[row, head] * passed + mm(pair(value), pair(weighted), TN)
            decay[row, head] = decay[row, head] * passed

    @pl.when(chunk == pl.num_programs(1) - 1)
    def _():
        for row in range(rows):
            for head in range(heads):
                pack_state(packed_ref, row, head, state[row, head], decay[row, head])


def forward_kernel(half, at_ref, docs_ref, qr_ref, zv_ref, logs_ref, bias_ref, gain_ref, *rest):
    carry_refs, (out_ref, mixed_ref, starts_ref, scores_ref, state) = rest[:-5], rest[-5:]
    rows, size = qr_ref.shape[1:3]
    heads, width = state.shape[1:3]
    chunk = pl.program_id(0)

    @pl.when(chunk == 0)
    def _():
        for row in range(rows):
            for head in range(heads):
                state[row, head] = unpack_carry(carry_refs, row, head)

    for row in range(rows):
        same, opened, tail, whole = chunk_masks(
            docs_ref, half * rows + row, at_ref[1] + chunk * size, size
        )
        for head in range(heads):
            low = head * width
            high = (heads + head) * width
            query = qr_ref[0, row, :, low : low + width]
            gate = qr_ref[0, row, :, high : high + width]
            logit = zv_ref[0, row, :, low : low + width] + bias_ref[:, low : low + width]
            value = pair(zv_ref[0, row, :, high : high + width])
            key = key_of(logit)
            log_sum = logs_ref[0, row, :, low : low + width]
            last = log_sum[size - 1 : size, :]
            lifted = pair(query * jax.nn.sigmoid(query) * jnp.exp(log_sum))
            lowered = pair(key * jnp.exp(-log_sum))
            scores = jnp.where(same, mm(lifted, lowered, NT), 0.0)
            scores_ref[0, row, head] = scores
            scores = pair(scores)
            begin = state[row, head]
            starts_ref[0, row, head] = begin
            out = mm(scores, value, NN) + jnp.where(opened, mm(lifted, pair(begin), NT), 0.0)
            passed = jnp.where(whole, jnp.exp(last), 0.0)
            weighted = jnp.where(tail, key * jnp.exp(last - log_sum), 0.0)
            state[row, head] = begin * passed + mm(value, pair(weighted), TN)
            scale = lax.rsqrt(jnp.mean(out * out, axis=-1, keepdims=True) + epsilon)
            normed = out * scale * gain_ref[:, low : low + width]
            out_ref[0, row, :, low : low + width] = out
            mixed_ref[0, row, :, low : low + width] = (
                normed * (gate * jax.nn.sigmoid(gate))
            ).astype(bf16)


def open_kernel(
    at_ref,
    docs_ref,
    qr_ref,
    zv_ref,
    logs_ref,
    out_ref,
    grad_ref,
    bias_ref,
    gain_ref,
    starts_ref,
    qr_grad_ref,
    low_ref,
    part_ref,
    packed_ref,
    slopes_ref,
    state,
    decay,
):
    rows, size = qr_ref.shape[1:3]
    heads, width = state.shape[1:3]
    half, step = pl.program_id(0), pl.program_id(1)
    chunk = pl.num_programs(1) - 1 - step

    @pl.when(step == 0)
    def _():
        state[...] = jnp.zeros_like(state)
        decay[...] = jnp.ones_like(decay)

    for row in range(rows):
        same, opened, _, whole = chunk_masks(
            docs_ref, half * rows + row, at_ref[1] + chunk * size, size
        )
        for head in range(heads):
            low = head * width
            high = (heads + head) * width
            query = qr_ref[0, row, :, low : low + width]
            gate = qr_ref[0, row, :, high : high + width]
            logit = zv_ref[0, row, :, low : low + width] + bias_ref[:, low : low + width]
            value = pair(zv_ref[0, row, :, high : high + width])
            out = out_ref[0, row, :, low : low + width]
            grad_mixed = grad_ref[0, row, :, low : low + width] * gain_ref[:, low : low + width]
            key = key_of(logit)
            log_sum = logs_ref[0, row, :, low : low + width]
            last = log_sum[size - 1 : size, :]
            rise = jnp.exp(log_sum)
            query_on = jax.nn.sigmoid(query)
            lifted = query * query_on * rise
            lowered = pair(key * jnp.exp(-log_sum))
            gate_on = jax.nn.sigmoid(gate)
            scale = lax.rsqrt(jnp.mean(out * out, axis=-1, keepdims=True) + epsilon)
            normed = out * scale
            grad_normed = grad_mixed * (gate * gate_on)
            grad_out = scale * (
                grad_normed - normed * jnp.mean(grad_normed * normed, axis=-1, keepdims=True)
            )
            grad_low = pair(grad_out)
            grad_scores = jnp.where(same, mm(grad_low, value, NT), 0.0)
            slopes_ref[0, row, head] = grad_scores
            grad_scores = pair(grad_scores)
            grad_lifted = mm(grad_scores, lowered, NN) + jnp.where(
                opened, mm(grad_low, pair(starts_ref[0, row, head]), NN), 0.0
            )
            grad_query = grad_lifted * rise * query_on * (1.0 + query * (1.0 - query_on))
            grad_gate = grad_mixed * normed * gate_on * (1.0 + gate * (1.0 - gate_on))
            qr_grad_ref[0, row, :, low : low + width] = grad_query.astype(bf16)
            qr_grad_ref[0, row, :, high : high + width] = grad_gate.astype(bf16)
            low_ref[0, row, :, low : low + width] = grad_out
            part_ref[0, row, :, low : low + width] = grad_lifted * lifted
            passed = jnp.where(whole, jnp.exp(last), 0.0)
            state[row, head] = state[row, head] * passed + mm(
                grad_low, pair(jnp.where(opened, lifted, 0.0)), TN
            )
            decay[row, head] = decay[row, head] * passed

    @pl.when(step == pl.num_programs(1) - 1)
    def _():
        for row in range(rows):
            for head in range(heads):
                pack_state(packed_ref, row, head, state[row, head], decay[row, head])


def close_kernel(
    at_ref,
    docs_ref,
    kept_ref,
    qr_ref,
    zv_ref,
    logs_ref,
    low_ref,
    part_ref,
    bias_ref,
    starts_ref,
    scores_ref,
    slopes_ref,
    *rest,
):
    carry_refs, (zv_grad_ref, bias_grad_ref, state) = rest[:-3], rest[-3:]
    rows, size = qr_ref.shape[1:3]
    heads, width = state.shape[1:3]
    half, step = pl.program_id(0), pl.program_id(1)
    chunk = pl.num_programs(1) - 1 - step
    tri = lower_ones(size)

    @pl.when((step == 0) & (half == 0))
    def _():
        bias_grad_ref[...] = jnp.zeros_like(bias_grad_ref)

    @pl.when(step == 0)
    def _():
        for row in range(rows):
            for head in range(heads):
                state[row, head] = unpack_carry(carry_refs, row, head)

    for row in range(rows):
        _, opened, tail, whole = chunk_masks(
            docs_ref, half * rows + row, at_ref[1] + chunk * size, size
        )
        for head in range(heads):
            low = head * width
            high = (heads + head) * width
            query = qr_ref[0, row, :, low : low + width]
            logit = zv_ref[0, row, :, low : low + width] + bias_ref[:, low : low + width]
            value = pair(zv_ref[0, row, :, high : high + width])
            grad_low = pair(low_ref[0, row, :, low : low + width])
            key = key_of(logit)
            log_sum = logs_ref[0, row, :, low : low + width]
            forget = forget_of(logit)
            last = log_sum[size - 1 : size, :]
            fall = jnp.exp(-log_sum)
            remain = jnp.where(tail, jnp.exp(last - log_sum), 0.0)
            lifted = query * jax.nn.sigmoid(query) * jnp.exp(log_sum)
            lowered = key * fall
            weighted = key * remain
            lifted_low = pair(lifted)
            scores = pair(scores_ref[0, row, head])
            begin = starts_ref[0, row, head]
            later = state[row, head]
            later_low = pair(later)
            grad_scores = pair(slopes_ref[0, row, head])
            grad_value = mm(scores, grad_low, TN) + mm(pair(weighted), later_low, NT)
            grad_lowered = mm(grad_scores, lifted_low, TN)
            grad_weighted = mm(value, later_low, NN)
            passed = jnp.where(whole, jnp.exp(last), 0.0)
            open_lifted = pair(jnp.where(opened, lifted, 0.0))
            state[row, head] = later * passed + mm(grad_low, open_lifted, TN)
            through = jnp.sum(begin * later, axis=0, keepdims=True) * passed
            weighted_part = grad_weighted * weighted
            grad_log = (
                part_ref[0, row, :, low : low + width]
                - grad_lowered * lowered
                - weighted_part
            )
            grad_last = through + jnp.sum(weighted_part, axis=0, keepdims=True)
            grad_step = split_sum(tri, grad_log, TN) + grad_last
            grad_key = grad_lowered * fall + grad_weighted * remain
            grad_logit = (
                span_bound
                * jax.nn.sigmoid(logit)
                * jax.nn.sigmoid(-logit)
                * (grad_step / forget - grad_key)
            )
            bias_grad_ref[:, low : low + width] += jnp.sum(grad_logit, axis=0, keepdims=True)
            zv_grad_ref[0, row, :, low : low + width] = grad_logit.astype(bf16)
            zv_grad_ref[0, row, :, high : high + width] = grad_value.astype(bf16)


def local_call(
    kernel, at, docs, ins, in_specs, out_shapes, out_specs, grid, scratch, aliases=None
):
    return pl.pallas_call(
        kernel,
        grid_spec=pltpu.PrefetchScalarGridSpec(
            num_scalar_prefetch=2,
            grid=grid,
            in_specs=in_specs,
            out_specs=out_specs,
            scratch_shapes=scratch,
        ),
        out_shape=out_shapes,
        input_output_aliases=aliases or {},
        compiler_params=pltpu.CompilerParams(
            dimension_semantics=("arbitrary",) * len(grid), vmem_limit_bytes=48 * 1024 * 1024
        ),
    )(at, docs, *ins)


def big_call(kernel, grid, ins, in_specs, out_shapes, out_specs):
    return pl.pallas_call(
        kernel,
        grid=grid,
        in_specs=in_specs,
        out_shape=out_shapes,
        out_specs=out_specs,
        compiler_params=pltpu.CompilerParams(
            dimension_semantics=("arbitrary",) * len(grid), vmem_limit_bytes=48 * 1024 * 1024
        ),
    )(*ins)


def up_kernel(in_ref, pair_ref, slope_ref, product_ref):
    rows = in_ref.shape[0] // 2
    units = pair_ref.shape[1] // 2
    cuts = [slice(0, rows), slice(rows, 2 * rows)]
    boths = [jnp.dot(in_ref[cut, :], pair_ref[...], preferred_element_type=f32) for cut in cuts]
    for cut, both in zip(cuts, boths):
        gate, up = both[:, :units], both[:, units:]
        gate_on = jax.nn.sigmoid(gate)
        active = gate * gate_on
        product_ref[cut, :] = (active * up).astype(bf16)
        slope_ref[0, cut, :] = up * (gate_on + active * (1.0 - gate_on))
        slope_ref[1, cut, :] = active


def down_kernel(grad_ref, down_ref, slope_ref, out_ref):
    rows = grad_ref.shape[0] // 2
    cuts = [slice(0, rows), slice(rows, 2 * rows)]
    grads = [jnp.dot(grad_ref[cut, :], down_ref[...], preferred_element_type=f32) for cut in cuts]
    for cut, grad in zip(cuts, grads):
        out_ref[cut, :] = jnp.concatenate(
            [grad * slope_ref[0, cut, :], grad * slope_ref[1, cut, :]], axis=-1
        ).astype(bf16)


def feed_up(mid_all, pair_all, tile):
    rows, features = mid_all.shape
    units = pair_all.shape[1]
    return big_call(
        up_kernel,
        (rows // tile,),
        (mid_all, pair_all),
        [
            pl.BlockSpec((tile, features), lambda i: (i, 0)),
            pl.BlockSpec((features, units), lambda i: (0, 0)),
        ],
        (
            jax.ShapeDtypeStruct((2, rows, units // 2), f32),
            jax.ShapeDtypeStruct((rows, units // 2), bf16),
        ),
        (
            pl.BlockSpec((2, tile, units // 2), lambda i: (0, i, 0)),
            pl.BlockSpec((tile, units // 2), lambda i: (i, 0)),
        ),
    )


def feed_back(grad_all, down_all, both, tile):
    rows, features = grad_all.shape
    units = 2 * both.shape[2]
    return big_call(
        down_kernel,
        (rows // tile,),
        (grad_all, down_all, both),
        [
            pl.BlockSpec((tile, features), lambda i: (i, 0)),
            pl.BlockSpec((features, units // 2), lambda i: (0, 0)),
            pl.BlockSpec((2, tile, units // 2), lambda i: (0, i, 0)),
        ],
        jax.ShapeDtypeStruct((rows, units), bf16),
        pl.BlockSpec((tile, units), lambda i: (i, 0)),
    )


def scatter_product(left, far_left, right, tile):
    depth = left.shape[1]
    columns = right.shape[1]
    half = columns // 2

    def dot(a_ref, b_ref):
        return jnp.dot(a_ref[...], b_ref[...], preferred_element_type=f32)

    def right_spec(side):
        return pl.BlockSpec((depth, half), lambda *_: (0, side))

    def far_kernel(a_ref, b_ref, out_ref):
        out_ref[...] = dot(a_ref, b_ref).astype(bf16)

    def far_part(side):
        return big_call(
            far_kernel,
            (4,),
            (far_left, right),
            [pl.BlockSpec((tile, depth), lambda i: (i, 0)), right_spec(side)],
            jax.ShapeDtypeStruct((4 * tile, half), bf16),
            pl.BlockSpec((tile, half), lambda i: (i, 0)),
        )

    def near_part(side, got):
        def kernel(a_ref, b_ref, got_ref, keep_ref, send_ref):
            value = dot(a_ref, b_ref) + got_ref[...].astype(f32)
            sent = pl.program_id(0) if side else pl.program_id(1)

            @pl.when(sent == 0)
            def _():
                keep_ref[0] = value

            @pl.when(sent == 1)
            def _():
                send_ref[0] = value.astype(bf16)

        if side:
            keep_at = lambda y, x: (jnp.where(y == 0, x, 1), 0, 0)
            send_at = lambda y, x: (jnp.where(y == 0, 0, x), 0, 0)
        else:
            keep_at = lambda y, x: (y, 0, 0)
            send_at = lambda y, x: (y, 0, 0)
        return big_call(
            kernel,
            (2, 2),
            (left, right, got),
            [
                pl.BlockSpec((tile, depth), lambda y, x: (2 * y + x, 0)),
                right_spec(side),
                pl.BlockSpec((tile, half), lambda y, x: (2 * y + x, 0)),
            ],
            (
                jax.ShapeDtypeStruct((2, tile, half), f32),
                jax.ShapeDtypeStruct((2, tile, half), bf16),
            ),
            (
                pl.BlockSpec((1, tile, half), keep_at),
                pl.BlockSpec((1, tile, half), send_at),
            ),
        )

    got = [swap_row(far_part(side)) for side in range(2)]
    (keep_left, to_x), (keep_right, to_y) = [near_part(side, got[side]) for side in range(2)]
    return keep_left, keep_right, to_x, to_y


def scatter_turned(left, right):
    half = left.shape[0] // 2
    far = times_transpose(left[half:], right).astype(bf16)
    near = times_transpose(left[:half], right)
    rows, columns = near.shape
    mine = (near + swap_row(far).astype(f32)).reshape(2, 2, rows // 4, columns)
    left_side, right_side = mine[..., : columns // 2], mine[..., columns // 2 :]
    return (
        left_side[:, 0],
        right_side[0],
        left_side[:, 1].astype(bf16),
        right_side[1].astype(bf16),
    )


def contract_rows(left, right):
    return lax.dot_general(left, right, (TN, ((), ())), preferred_element_type=f32)


def times_transpose(left, right):
    return lax.dot_general(left, right, (NT, ((), ())), preferred_element_type=f32)


def times(left, right):
    return jnp.dot(left, right, preferred_element_type=f32)


def rms_rate(values):
    return lax.rsqrt(jnp.mean(values * values, axis=-1, keepdims=True) + epsilon)


def rms_back(grad, values, rate):
    return rate * grad - values * (
        rate * rate * rate * jnp.mean(grad * values, axis=-1, keepdims=True)
    )


def on_device(
    block_input,
    out_grad,
    doc_starts,
    w_query,
    w_forget,
    w_input,
    w_outgate,
    w_out,
    w_gate,
    w_up,
    w_down,
    norm_gain,
    mlp_gain,
    group_gain,
    forget_bias,
):
    row_count, span, features = block_input.shape
    groups = lax.axis_size("z")
    own_row = lax.axis_index("row")
    own_spot = lax.axis_index("y") * 2 + lax.axis_index("x")
    own_first = own_row == 0
    spots, members = 4, 8
    tokens = row_count * span
    width = features // HEADS
    heads = HEADS // members
    wide = heads * width
    share = w_query.shape[0]
    units = w_gate.shape[1] // spots
    block = w_gate.shape[0]
    half = spots * tokens

    by_chip = 2 * share == width and groups == 2 * heads
    if by_chip:
        held = lax.all_gather(w_out, "z", axis=0, tiled=False).reshape(2, heads, share, features)
    else:
        held = lax.all_gather(w_out, everywhere, axis=0, tiled=True)

    def cut_heads(first, second):
        both = jnp.stack([first, second]).reshape(2, share, 2, heads, spots, width)
        return both.transpose(4, 2, 1, 0, 3, 5).reshape(members, share, 2 * wide)

    def over_group(cut):
        return lax.all_to_all(cut, group, 0, 0, tiled=True)

    def over_plane(cut):
        return lax.all_to_all(cut, plane, 0, 0, tiled=True)

    def over_groups(cut):
        flat = cut.reshape(cut.shape[0] * cut.shape[1], cut.shape[2])
        return lax.all_gather(flat, "z", axis=0, tiled=True)

    vectors = jnp.stack([norm_gain, mlp_gain, group_gain, forget_bias]).astype(f32)
    vectors = jnp.broadcast_to(vectors.reshape(1, 4 * share), (groups * members, 4 * share))
    vectors = lax.all_to_all(vectors, everywhere, 0, 0, tiled=True)
    mixer_cut, vectors = join(
        jnp.stack([cut_heads(w_forget, w_input), cut_heads(w_query, w_outgate)], axis=1), vectors
    )
    mixer_cut = over_group(mixer_cut)
    zv_all = over_groups(mixer_cut[:, 0])
    qr_all = over_groups(mixer_cut[:, 1])

    vectors = vectors.reshape(groups * members, 4, share).transpose(1, 0, 2).reshape(4, features)
    here = lax.dynamic_index_in_dim(
        vectors.reshape(4, 2, heads, spots, width), own_row, 1, False
    )
    here = lax.dynamic_index_in_dim(here, own_spot, 2, False).reshape(4, wide)
    first_gain, mid_gain = vectors[0:1], vectors[1:2]
    gain_here, bias_here = here[2:3], here[3:4]

    input_float = block_input.astype(f32).reshape(tokens, features)
    first_rate = rms_rate(input_float)
    normed = (input_float * first_rate * first_gain).astype(bf16)
    pair_cut = jnp.concatenate(
        [w_gate.reshape(block, spots, units), w_up.reshape(block, spots, units)], axis=-1
    ).transpose(1, 0, 2)
    down_cut = w_down.T.reshape(block, spots, units).transpose(1, 0, 2)

    normed, held = join(normed, held)
    first, pair_cut, down_cut = join(gather_first(normed), pair_cut, down_cut)
    normed_all = gather_last(gather_second(*first))

    docs = jnp.concatenate([doc_starts, swap_row(doc_starts)], axis=0)
    at = jnp.stack([own_spot, lax.axis_index("z") * (spots * span)]).astype(jnp.int32)
    by_block = (members, row_count, span)
    zv = times(normed_all, zv_all).reshape(by_block + (2 * wide,))
    zv, pair_cut, down_cut = join(zv, pair_cut, down_cut)
    pair_cut = over_plane(pair_cut)

    once = pl.BlockSpec((1, wide), lambda *_: (0, 0))
    packed_block = (row_count, heads, width + PAD, width)
    packed_shape = jax.ShapeDtypeStruct((2 * row_count,) + packed_block[1:], bf16)
    states = pltpu.VMEM((row_count, heads, width, width), f32)
    decays = pltpu.VMEM((row_count, heads, 1, width), f32)

    def slab(columns, index):
        return pl.BlockSpec((1, row_count, span, columns), index)

    def ahead(h, c, at_ref, docs_ref):
        return (h * spots + (c ^ at_ref[0]), 0, 0, 0)

    def behind(h, c, at_ref, docs_ref):
        return (h * spots + ((spots - 1 - c) ^ at_ref[0]), 0, 0, 0)

    by_half = pl.BlockSpec(packed_block, lambda h, c, at_ref, docs_ref: (h, 0, 0, 0))

    packed, logs = local_call(
        state_kernel,
        at,
        docs,
        (zv, bias_here),
        [slab(2 * wide, ahead), once],
        (packed_shape, jax.ShapeDtypeStruct(by_block + (wide,), f32)),
        (by_half, slab(wide, ahead)),
        (2, spots),
        (states, decays),
    )
    grad_low = out_grad.reshape(tokens, features)

    carried = []
    for step in range(groups - 1):
        packed = hop(packed, True)
        if step == 0:
            packed, pair_cut = join(packed, pair_cut.reshape(spots * block, 2 * units))
            grad_sent, down_cut, pair_cut = join(grad_low, down_cut, pair_cut)
            pair_all = lax.all_gather(pair_cut, "z", axis=0, tiled=True)
            near = gather_second(*gather_first(grad_sent))
            down_cut = over_plane(down_cut).reshape(spots * block, units)
        carried.append(packed)
    qr = times(normed_all, qr_all)
    carried, near, qr, down_cut = join(carried, near, qr, down_cut)
    down_all = lax.all_gather(down_cut, "z", axis=0, tiled=True)
    grad_all = gather_last(near)
    qr = qr.reshape(by_block + (2 * wide,))

    def forward_half(side, qr):
        def place(c, at_ref, docs_ref):
            return (side * spots + (c ^ at_ref[0]), 0, 0, 0)

        def local(c, at_ref, docs_ref):
            return (c ^ at_ref[0], 0, 0, 0)

        def kernel(*refs):
            forward_kernel(side, *refs)

        return local_call(
            kernel,
            at,
            docs,
            (qr, zv, logs, bias_here, gain_here, *carried),
            [slab(2 * wide, place), slab(2 * wide, place), slab(wide, place), once, once]
            + [pl.BlockSpec(packed_block, lambda c, at_ref, docs_ref: (side, 0, 0, 0))]
            * len(carried),
            (
                jax.ShapeDtypeStruct((spots,) + by_block[1:] + (wide,), f32),
                jax.ShapeDtypeStruct((spots,) + by_block[1:] + (wide,), bf16),
                jax.ShapeDtypeStruct((spots, row_count, heads, width, width), f32),
                jax.ShapeDtypeStruct((spots, row_count, heads, span, span), f32),
            ),
            (
                slab(wide, local),
                slab(wide, local),
                pl.BlockSpec(
                    (1, row_count, heads, width, width),
                    lambda c, at_ref, docs_ref: (c, 0, 0, 0, 0),
                ),
                pl.BlockSpec(
                    (1, row_count, heads, span, span),
                    lambda c, at_ref, docs_ref: (c, 0, 0, 0, 0),
                ),
            ),
            (spots,),
            (states,),
        )

    if by_chip:
        keep = lax.dynamic_index_in_dim(held, own_row, 0, False)
        give = lax.dynamic_index_in_dim(held, 1 - own_row, 0, False)
        take = swap_row(give)
        out_here = jnp.stack(
            [jnp.where(own_first, keep, take), jnp.where(own_first, take, keep)], axis=1
        ).reshape(wide, features)
    else:
        held = held.reshape(2, heads, spots, width, features)
        held = lax.dynamic_index_in_dim(held, own_row, 0, False)
        out_here = lax.dynamic_index_in_dim(held, own_spot, 1, False).reshape(wide, features)

    far_out, far_mixed, far_starts, far_scores = forward_half(1, qr)
    far_mixed = far_mixed.reshape(half, wide)
    near_out, near_mixed, near_starts, near_scores = forward_half(0, qr)
    near_mixed = near_mixed.reshape(half, wide)
    state = scatter_product(near_mixed, far_mixed, out_here, tokens)
    hidden = input_float + scatter_group(state)[0]

    mid_rate = rms_rate(hidden)
    first, grad_all, mixer_weights = join(
        gather_first((hidden * mid_rate * mid_gain).astype(bf16)),
        grad_all,
        jnp.concatenate([qr_all, zv_all], axis=1),
    )
    mid_all = gather_last(gather_second(*first))
    both, product = feed_up(mid_all, pair_all, tokens)

    def spread(partial):
        return lax.psum_scatter(partial.astype(bf16), "z", scatter_dimension=0, tiled=True)

    down_part = contract_rows(grad_all, product).astype(bf16)
    grad_down = spread(down_part)
    grad_both = feed_back(grad_all, down_all, both, tokens)
    state, mid_late, both_late, product = join(
        scatter_turned(grad_both, pair_all), mid_all, grad_both, product
    )
    pair_part = contract_rows(mid_late, both_late).astype(bf16)
    grad_mid, pair_part, grad_down = scatter_group(state, (pair_part,), (grad_down,))
    grad_pair = spread(pair_part)
    grad_float = out_grad.astype(f32).reshape(tokens, features)
    grad_hidden = grad_float + rms_back(grad_mid * mid_gain, hidden, mid_rate)

    first, sums = join(
        gather_first(grad_hidden.astype(bf16)),
        scatter_turned(product, down_all),
    )
    near_gm = lay(gather_second(*first))
    far_gm = swap_row(near_gm)
    sums = scatter_second(*join(sums, near_gm)[0])
    grad_mixed = jnp.concatenate(
        [times_transpose(near_gm, out_here), times_transpose(far_gm, out_here)], axis=0
    ).reshape(by_block + (wide,))
    mixer_out = jnp.concatenate([near_out, far_out], axis=0)
    starts = jnp.concatenate([near_starts, far_starts], axis=0)
    scores = jnp.concatenate([near_scores, far_scores], axis=0)
    scores_spec = pl.BlockSpec(
        (1, row_count, heads, span, span),
        lambda h, c, at_ref, docs_ref: (h * spots + spots - 1 - c, 0, 0, 0, 0),
    )
    starts_spec = pl.BlockSpec(
        (1, row_count, heads, width, width),
        lambda h, c, at_ref, docs_ref: (h * spots + spots - 1 - c, 0, 0, 0, 0),
    )
    all_grads, lows, parts, packed, slopes = local_call(
        open_kernel,
        at,
        docs,
        (qr, zv, logs, mixer_out, grad_mixed, bias_here, gain_here, starts),
        [
            slab(2 * wide, behind),
            slab(2 * wide, behind),
            slab(wide, behind),
            slab(wide, behind),
            slab(wide, behind),
            once,
            once,
            starts_spec,
        ],
        (
            jax.ShapeDtypeStruct(by_block + (4 * wide,), bf16),
            jax.ShapeDtypeStruct(by_block + (wide,), f32),
            jax.ShapeDtypeStruct(by_block + (wide,), f32),
            packed_shape,
            jax.ShapeDtypeStruct((2 * spots, row_count, heads, span, span), f32),
        ),
        (slab(2 * wide, behind), slab(wide, behind), slab(wide, behind), by_half, scores_spec),
        (2, spots),
        (states, decays),
    )
    packed, sums, near_late, far_late = join(packed, sums, near_gm, far_gm)

    def out_rows():
        rows = contract_rows(near_mixed, near_late) + contract_rows(far_mixed, far_late)
        return rows.astype(bf16)

    def query_part():
        qr_grads = all_grads.reshape(2 * half, 4 * wide)[:, : 2 * wide]
        return contract_rows(normed_all, qr_grads).astype(bf16)

    def turn_units(back):
        return back.transpose(0, 2, 1).reshape(spots * units, block).astype(f32)

    def pair_parts(back):
        return [
            jnp.concatenate(
                [back[spot, :, low : low + units].astype(f32) for spot in range(spots)], axis=1
            )
            for low in (0, units)
        ]

    packed, grad_down = join(packed, grad_down)
    down_back = over_plane(grad_down.reshape(spots, block, units))

    def beside(step):
        if step == 0:
            return (out_rows(), scatter_third(*sums), down_back)
        if step == 1:
            return (query_part(), turn_units(done[2]))
        return ()

    later = []
    done = []
    for step in range(groups - 1):
        packed, extra = join(hop(packed, False), beside(step))
        later.append(packed)
        done += extra
    grad_out_rows, sums, _, qr_part, grad_down = done
    later, grad_pair = join(later, grad_pair)
    pair_back = over_plane(grad_pair.reshape(spots, block, 2 * units))
    block_output = (hidden + scatter_last(*sums)).astype(bf16)
    if by_chip:
        cut = grad_out_rows.reshape(heads, 2, share, features)
        keep = lax.dynamic_index_in_dim(cut, own_row, 1, False)
        give = lax.dynamic_index_in_dim(cut, 1 - own_row, 1, False)
        take = swap_row(give)
        cut = jnp.concatenate(
            [jnp.where(own_first, keep, take), jnp.where(own_first, take, keep)], axis=0
        )
        grad_out = spread(cut.reshape(groups * share, features))
    else:
        placed = jnp.zeros((2, heads, spots, width, features), bf16)
        placed = lax.dynamic_update_slice(
            placed,
            grad_out_rows.reshape(1, heads, 1, width, features),
            (own_row, 0, own_spot, 0, 0),
        )
        grad_out = lax.psum_scatter(
            placed.reshape(features, features), everywhere, scatter_dimension=0, tiled=True
        )
    grad_qr = spread(qr_part)

    def behind_right(h, c, at_ref, docs_ref):
        return behind(h, c, at_ref, docs_ref)[:3] + (1,)

    all_grads, bias_part = local_call(
        close_kernel,
        at,
        docs,
        (all_grads, qr, zv, logs, lows, parts, bias_here, starts, scores, slopes, *later),
        [
            pl.BlockSpec(memory_space=pl.ANY),
            slab(2 * wide, behind),
            slab(2 * wide, behind),
            slab(wide, behind),
            slab(wide, behind),
            slab(wide, behind),
            once,
            starts_spec,
            scores_spec,
            scores_spec,
        ]
        + [by_half] * len(later),
        (
            jax.ShapeDtypeStruct(by_block + (4 * wide,), bf16),
            jax.ShapeDtypeStruct((1, wide), f32),
        ),
        (slab(2 * wide, behind_right), once),
        (2, spots),
        (states,),
        {2: 0},
    )
    all_grads, pair_back = join(all_grads, pair_back)
    all_grads = all_grads.reshape(2 * half, 4 * wide)
    zv_part = contract_rows(normed_all, all_grads[:, 2 * wide :]).astype(bf16)
    late_grads, zv_part = join(all_grads, zv_part)
    grad_zv = spread(zv_part)
    state = scatter_turned(late_grads, mixer_weights)
    bias_placed = jnp.zeros((2, heads, spots, width), f32)
    bias_placed = lax.dynamic_update_slice(
        bias_placed, bias_part.reshape(1, heads, 1, width), (own_row, 0, own_spot, 0)
    )
    bias_back = lax.all_to_all(
        bias_placed.reshape(groups * members, share), everywhere, 0, 0, tiled=True
    )
    grad_bias = jnp.sum(bias_back, axis=0)

    def join_heads(cut):
        back = cut.reshape(spots, 2, share, 2, heads, width)
        return [
            back[:, :, :, at].transpose(2, 1, 3, 0, 4).reshape(share, features).astype(f32)
            for at in range(2)
        ]

    state, block_output, grad_out, grad_qr = join(
        state, block_output, grad_out, over_group(grad_qr.reshape(members, share, 2 * wide))
    )
    grad_out = grad_out.astype(f32)
    state, (query_back, outgate_back), grad_out, block_output, (grad_gate, grad_up) = join(
        scatter_second(*state), join_heads(grad_qr), grad_out, block_output, pair_parts(pair_back)
    )
    state, grad_zv = join(scatter_sums(*state), grad_zv)
    state, (forget_back, input_back) = join(
        scatter_fourth(*state),
        join_heads(over_group(grad_zv.reshape(members, share, 2 * wide))),
    )
    grad_normed = scatter_last(*state)
    input_grad = grad_hidden + rms_back(grad_normed * first_gain, input_float, first_rate)
    input_grad = input_grad.astype(bf16).reshape(block_input.shape)

    own_vectors = (norm_gain.astype(f32), mlp_gain.astype(f32), group_gain.astype(f32))
    grad_head_gain = jnp.sum(grad_out * w_out.astype(f32), axis=1) / own_vectors[2]

    mid_part = jnp.sum(grad_gate * w_gate.astype(f32) + grad_up * w_up.astype(f32), axis=1)
    mid_part = mid_part.reshape(2, share)
    mid_keep = lax.dynamic_index_in_dim(mid_part, own_row, 0, False)
    mid_give = lax.dynamic_index_in_dim(mid_part, 1 - own_row, 0, False)
    grad_mid_gain = (mid_keep + swap_row(mid_give)) / own_vectors[1]

    first_part = query_back * w_query.astype(f32) + outgate_back * w_outgate.astype(f32)
    first_part += forget_back * w_forget.astype(f32) + input_back * w_input.astype(f32)
    grad_first_gain = jnp.sum(first_part, axis=1) / own_vectors[0]

    return (
        block_output.reshape(block_input.shape),
        input_grad,
        query_back,
        forget_back,
        input_back,
        outgate_back,
        grad_out,
        grad_gate,
        grad_up,
        grad_down,
        grad_first_gain,
        grad_mid_gain,
        grad_head_gain,
        grad_bias,
    )


def solution(mesh):
    count, rows = mesh.devices.shape
    folded = Mesh(mesh.devices.reshape(count // 4, 2, 2, rows), everywhere)
    seq = ("z", "y", "x")
    token_spec = P("row", seq, None)
    matrix_spec = P(everywhere, None)
    vector_spec = P(everywhere)
    wide_spec = P(seq, "row")
    tall_spec = P("row", seq)
    in_specs = (
        (token_spec, token_spec, P("row", None))
        + (matrix_spec,) * 5
        + (wide_spec, wide_spec, tall_spec)
        + (vector_spec,) * 4
    )
    out_specs = (
        (token_spec, token_spec)
        + (matrix_spec,) * 5
        + (wide_spec, wide_spec, tall_spec)
        + (vector_spec,) * 4
    )
    return jax.shard_map(
        on_device, mesh=folded, in_specs=in_specs, out_specs=out_specs, check_vma=False
    )
```

```python
import jax
import jax.numpy as jnp
from jax import lax
from jax.experimental import pallas as pl
from jax.experimental.pallas import tpu as pltpu
from jax.sharding import Mesh, PartitionSpec as P

HEADS = 16

lower_bound = 0.85
span_bound = 1.0 - lower_bound
epsilon = 1e-06
f32 = jnp.float32
bf16 = jnp.bfloat16
swap = ((0, 1), (1, 0))
everywhere = ("z", "y", "x", "row")
group = ("y", "x", "row")
plane = ("y", "x")


def swap_x(a):
    return lax.ppermute(a, "x", swap)


def swap_y(a):
    return lax.ppermute(a, "y", swap)


def swap_row(a):
    return lax.ppermute(a, "row", swap)


def join(*groups):
    flat, tree = jax.tree.flatten(groups)
    return jax.tree.unflatten(tree, lax.optimization_barrier(flat))


def gather_first(a):
    return a, swap_x(a), swap_y(a)


def gather_second(a, from_x, from_y):
    half = a.shape[0] // 2
    return a, from_x, from_y, swap_y(from_x[:half]), swap_x(from_y[half:])


def lay_kernel(*refs):
    pieces, out_ref = refs[:-1], refs[-1]
    rows = out_ref.shape[0]
    start = 0
    for ref in pieces:
        block, low = start // rows, start % rows

        @pl.when(pl.program_id(0) == block)
        def _(ref=ref, low=low):
            out_ref[low : low + ref.shape[0], :] = ref[...]

        start += ref.shape[0]


def lay(pieces):
    rows, columns = pieces[0].shape
    total = sum(piece.shape[0] for piece in pieces)
    return pl.pallas_call(
        lay_kernel,
        grid=(total // rows,),
        in_specs=[pl.BlockSpec(piece.shape, lambda step: (0, 0)) for piece in pieces],
        out_specs=pl.BlockSpec((rows, columns), lambda step: (step, 0)),
        out_shape=jax.ShapeDtypeStruct((total, columns), pieces[0].dtype),
        compiler_params=pltpu.CompilerParams(
            dimension_semantics=("arbitrary",), vmem_limit_bytes=48 * 1024 * 1024
        ),
    )(*pieces)


def gather_last(near):
    return lay(near + tuple(swap_row(piece) for piece in near))


def gather_group(a):
    return gather_last(gather_second(*gather_first(a)))


def scatter_second(left, right, to_x, to_y):
    return left, right, swap_x(to_x), swap_y(to_y)


def scatter_sums(left, right, from_x, from_y):
    left = left + from_x.astype(f32)
    right = right + from_y.astype(f32)
    return left[0], right[0], left[1].astype(bf16), right[1].astype(bf16)


def scatter_fourth(left, right, to_y, to_x):
    return left, right, swap_y(to_y), swap_x(to_x)


def scatter_third(*state):
    return scatter_fourth(*scatter_sums(*state))


def scatter_last(left, right, from_y, from_x):
    return jnp.concatenate([left + from_y.astype(f32), right + from_x.astype(f32)], axis=-1)


def scatter_group(state, first=(), second=()):
    state, first = join(scatter_second(*state), first)
    state, second = join(scatter_third(*state), second)
    return scatter_last(*state), *first, *second


def hop(packed, forward):
    count = lax.axis_size("z")
    if forward:
        pairs = [(i, i + 1) for i in range(count - 1)]
    else:
        pairs = [(i + 1, i) for i in range(count - 1)]
    return lax.ppermute(packed, "z", pairs)


def relay(packed, forward):
    got = []
    for _ in range(lax.axis_size("z") - 1):
        packed = hop(packed, forward)
        got.append(packed)
    return got


def pair(values):
    high = values.astype(bf16)
    return high, (values - high.astype(f32)).astype(bf16)


def mm(a, b, dims):
    def dot(left, right):
        return lax.dot_general(left, right, (dims, ((), ())), preferred_element_type=f32)

    return dot(a[0], b[0]) + (dot(a[0], b[1]) + dot(a[1], b[0]))


def split_sum(ones_matrix, values, dims):
    first = values.astype(bf16)
    rest = values - first.astype(f32)
    second = rest.astype(bf16)
    third = (rest - second.astype(f32)).astype(bf16)
    total = lax.dot_general(ones_matrix, first, (dims, ((), ())), preferred_element_type=f32)
    total += lax.dot_general(ones_matrix, second, (dims, ((), ())), preferred_element_type=f32)
    total += lax.dot_general(ones_matrix, third, (dims, ((), ())), preferred_element_type=f32)
    return total


NT = ((1,), (1,))
NN = ((1,), (0,))
TN = ((0,), (0,))


def chunk_masks(docs_ref, row_at, start, size):
    at_row = lax.broadcasted_iota(jnp.int32, (size, size), 0)
    at_col = lax.broadcasted_iota(jnp.int32, (size, size), 1)
    same = at_row >= at_col
    opened = at_row >= 0
    tail = at_row >= 0
    whole = jnp.bool_(True)
    for entry in range(docs_ref.shape[1]):
        place = docs_ref[row_at, entry] - start
        same = same & ~((at_col < place) & (place <= at_row))
        opened = opened & ~((0 <= place) & (place <= at_row))
        tail = tail & ~((at_row < place) & (place <= size - 1))
        whole = whole & ~((0 <= place) & (place <= size - 1))
    return same, opened, tail, whole


def key_of(logit):
    return span_bound * jax.nn.sigmoid(-logit)


def forget_of(logit):
    return lower_bound + span_bound * jax.nn.sigmoid(logit)


def lower_ones(size):
    at_row = lax.broadcasted_iota(jnp.int32, (size, size), 0)
    at_col = lax.broadcasted_iota(jnp.int32, (size, size), 1)
    return (at_row >= at_col).astype(f32).astype(bf16)


PAD = 16


def pack_state(ref, row, head, state, decay):
    width = state.shape[0]
    high = decay.astype(bf16).astype(f32)
    at_row = lax.broadcasted_iota(jnp.int32, (PAD, width), 0)
    extra = jnp.where(at_row == 0, high, jnp.where(at_row == 1, decay - high, 0.0))
    ref[row, head, :width, :] = state.astype(bf16)
    ref[row, head, width:, :] = extra.astype(bf16)


def unpack_carry(refs, row, head):
    width = refs[0].shape[3]
    carry = None
    for ref in refs[::-1]:
        state = ref[row, head, :width, :].astype(f32)
        if carry is not None:
            extra = ref[row, head, width:, :].astype(f32)
            state = state + (extra[0:1] + extra[1:2]) * carry
        carry = state
    return carry


def state_kernel(at_ref, docs_ref, zv_ref, bias_ref, packed_ref, logs_ref, state, decay):
    rows, size = zv_ref.shape[1:3]
    heads, width = state.shape[1:3]
    half, chunk = pl.program_id(0), pl.program_id(1)
    tri = lower_ones(size)

    @pl.when(chunk == 0)
    def _():
        state[...] = jnp.zeros_like(state)
        decay[...] = jnp.ones_like(decay)

    for row in range(rows):
        _, _, tail, whole = chunk_masks(
            docs_ref, half * rows + row, at_ref[1] + chunk * size, size
        )
        for head in range(heads):
            low = head * width
            logit = zv_ref[0, row, :, low : low + width] + bias_ref[:, low : low + width]
            value = zv_ref[0, row, :, heads * width + low : heads * width + low + width]
            key = key_of(logit)
            log_sum = split_sum(tri, jnp.log(forget_of(logit)), NN)
            logs_ref[0, row, :, low : low + width] = log_sum
            last = log_sum[size - 1 : size, :]
            passed = jnp.where(whole, jnp.exp(last), 0.0)
            weighted = jnp.where(tail, key * jnp.exp(last - log_sum), 0.0)
            state[row, head] = state[row, head] * passed + mm(pair(value), pair(weighted), TN)
            decay[row, head] = decay[row, head] * passed

    @pl.when(chunk == pl.num_programs(1) - 1)
    def _():
        for row in range(rows):
            for head in range(heads):
                pack_state(packed_ref, row, head, state[row, head], decay[row, head])


def forward_kernel(half, at_ref, docs_ref, qr_ref, zv_ref, logs_ref, bias_ref, gain_ref, *rest):
    carry_refs, (out_ref, mixed_ref, starts_ref, scores_ref, state) = rest[:-5], rest[-5:]
    rows, size = qr_ref.shape[1:3]
    heads, width = state.shape[1:3]
    chunk = pl.program_id(0)

    @pl.when(chunk == 0)
    def _():
        for row in range(rows):
            for head in range(heads):
                state[row, head] = unpack_carry(carry_refs, row, head)

    for row in range(rows):
        same, opened, tail, whole = chunk_masks(
            docs_ref, half * rows + row, at_ref[1] + chunk * size, size
        )
        for head in range(heads):
            low = head * width
            high = (heads + head) * width
            query = qr_ref[0, row, :, low : low + width]
            gate = qr_ref[0, row, :, high : high + width]
            logit = zv_ref[0, row, :, low : low + width] + bias_ref[:, low : low + width]
            value = pair(zv_ref[0, row, :, high : high + width])
            key = key_of(logit)
            log_sum = logs_ref[0, row, :, low : low + width]
            last = log_sum[size - 1 : size, :]
            lifted = pair(query * jax.nn.sigmoid(query) * jnp.exp(log_sum))
            lowered = pair(key * jnp.exp(-log_sum))
            scores = jnp.where(same, mm(lifted, lowered, NT), 0.0)
            scores_ref[0, row, head] = scores
            scores = pair(scores)
            begin = state[row, head]
            starts_ref[0, row, head] = begin
            out = mm(scores, value, NN) + jnp.where(opened, mm(lifted, pair(begin), NT), 0.0)
            passed = jnp.where(whole, jnp.exp(last), 0.0)
            weighted = jnp.where(tail, key * jnp.exp(last - log_sum), 0.0)
            state[row, head] = begin * passed + mm(value, pair(weighted), TN)
            scale = lax.rsqrt(jnp.mean(out * out, axis=-1, keepdims=True) + epsilon)
            normed = out * scale * gain_ref[:, low : low + width]
            out_ref[0, row, :, low : low + width] = out
            mixed_ref[0, row, :, low : low + width] = (
                normed * (gate * jax.nn.sigmoid(gate))
            ).astype(bf16)


def open_kernel(
    at_ref,
    docs_ref,
    qr_ref,
    zv_ref,
    logs_ref,
    out_ref,
    grad_ref,
    bias_ref,
    gain_ref,
    starts_ref,
    qr_grad_ref,
    low_ref,
    part_ref,
    packed_ref,
    slopes_ref,
    state,
    decay,
):
    rows, size = qr_ref.shape[1:3]
    heads, width = state.shape[1:3]
    half, step = pl.program_id(0), pl.program_id(1)
    chunk = pl.num_programs(1) - 1 - step

    @pl.when(step == 0)
    def _():
        state[...] = jnp.zeros_like(state)
        decay[...] = jnp.ones_like(decay)

    for row in range(rows):
        same, opened, _, whole = chunk_masks(
            docs_ref, half * rows + row, at_ref[1] + chunk * size, size
        )
        for head in range(heads):
            low = head * width
            high = (heads + head) * width
            query = qr_ref[0, row, :, low : low + width]
            gate = qr_ref[0, row, :, high : high + width]
            logit = zv_ref[0, row, :, low : low + width] + bias_ref[:, low : low + width]
            value = pair(zv_ref[0, row, :, high : high + width])
            out = out_ref[0, row, :, low : low + width]
            grad_mixed = grad_ref[0, row, :, low : low + width] * gain_ref[:, low : low + width]
            key = key_of(logit)
            log_sum = logs_ref[0, row, :, low : low + width]
            last = log_sum[size - 1 : size, :]
            rise = jnp.exp(log_sum)
            query_on = jax.nn.sigmoid(query)
            lifted = query * query_on * rise
            lowered = pair(key * jnp.exp(-log_sum))
            gate_on = jax.nn.sigmoid(gate)
            scale = lax.rsqrt(jnp.mean(out * out, axis=-1, keepdims=True) + epsilon)
            normed = out * scale
            grad_normed = grad_mixed * (gate * gate_on)
            grad_out = scale * (
                grad_normed - normed * jnp.mean(grad_normed * normed, axis=-1, keepdims=True)
            )
            grad_low = pair(grad_out)
            grad_scores = jnp.where(same, mm(grad_low, value, NT), 0.0)
            slopes_ref[0, row, head] = grad_scores
            grad_scores = pair(grad_scores)
            grad_lifted = mm(grad_scores, lowered, NN) + jnp.where(
                opened, mm(grad_low, pair(starts_ref[0, row, head]), NN), 0.0
            )
            grad_query = grad_lifted * rise * query_on * (1.0 + query * (1.0 - query_on))
            grad_gate = grad_mixed * normed * gate_on * (1.0 + gate * (1.0 - gate_on))
            qr_grad_ref[0, row, :, low : low + width] = grad_query.astype(bf16)
            qr_grad_ref[0, row, :, high : high + width] = grad_gate.astype(bf16)
            low_ref[0, row, :, low : low + width] = grad_out
            part_ref[0, row, :, low : low + width] = grad_lifted * lifted
            passed = jnp.where(whole, jnp.exp(last), 0.0)
            state[row, head] = state[row, head] * passed + mm(
                grad_low, pair(jnp.where(opened, lifted, 0.0)), TN
            )
            decay[row, head] = decay[row, head] * passed

    @pl.when(step == pl.num_programs(1) - 1)
    def _():
        for row in range(rows):
            for head in range(heads):
                pack_state(packed_ref, row, head, state[row, head], decay[row, head])


def close_kernel(
    at_ref,
    docs_ref,
    kept_ref,
    qr_ref,
    zv_ref,
    logs_ref,
    low_ref,
    part_ref,
    bias_ref,
    starts_ref,
    scores_ref,
    slopes_ref,
    *rest,
):
    carry_refs, (zv_grad_ref, bias_grad_ref, state) = rest[:-3], rest[-3:]
    rows, size = qr_ref.shape[1:3]
    heads, width = state.shape[1:3]
    half, step = pl.program_id(0), pl.program_id(1)
    chunk = pl.num_programs(1) - 1 - step
    tri = lower_ones(size)

    @pl.when((step == 0) & (half == 0))
    def _():
        bias_grad_ref[...] = jnp.zeros_like(bias_grad_ref)

    @pl.when(step == 0)
    def _():
        for row in range(rows):
            for head in range(heads):
                state[row, head] = unpack_carry(carry_refs, row, head)

    for row in range(rows):
        _, opened, tail, whole = chunk_masks(
            docs_ref, half * rows + row, at_ref[1] + chunk * size, size
        )
        for head in range(heads):
            low = head * width
            high = (heads + head) * width
            query = qr_ref[0, row, :, low : low + width]
            logit = zv_ref[0, row, :, low : low + width] + bias_ref[:, low : low + width]
            value = pair(zv_ref[0, row, :, high : high + width])
            grad_low = pair(low_ref[0, row, :, low : low + width])
            key = key_of(logit)
            log_sum = logs_ref[0, row, :, low : low + width]
            forget = forget_of(logit)
            last = log_sum[size - 1 : size, :]
            fall = jnp.exp(-log_sum)
            remain = jnp.where(tail, jnp.exp(last - log_sum), 0.0)
            lifted = query * jax.nn.sigmoid(query) * jnp.exp(log_sum)
            lowered = key * fall
            weighted = key * remain
            lifted_low = pair(lifted)
            scores = pair(scores_ref[0, row, head])
            begin = starts_ref[0, row, head]
            later = state[row, head]
            later_low = pair(later)
            grad_scores = pair(slopes_ref[0, row, head])
            grad_value = mm(scores, grad_low, TN) + mm(pair(weighted), later_low, NT)
            grad_lowered = mm(grad_scores, lifted_low, TN)
            grad_weighted = mm(value, later_low, NN)
            passed = jnp.where(whole, jnp.exp(last), 0.0)
            open_lifted = pair(jnp.where(opened, lifted, 0.0))
            state[row, head] = later * passed + mm(grad_low, open_lifted, TN)
            through = jnp.sum(begin * later, axis=0, keepdims=True) * passed
            weighted_part = grad_weighted * weighted
            grad_log = (
                part_ref[0, row, :, low : low + width]
                - grad_lowered * lowered
                - weighted_part
            )
            grad_last = through + jnp.sum(weighted_part, axis=0, keepdims=True)
            grad_step = split_sum(tri, grad_log, TN) + grad_last
            grad_key = grad_lowered * fall + grad_weighted * remain
            grad_logit = (
                span_bound
                * jax.nn.sigmoid(logit)
                * jax.nn.sigmoid(-logit)
                * (grad_step / forget - grad_key)
            )
            bias_grad_ref[:, low : low + width] += jnp.sum(grad_logit, axis=0, keepdims=True)
            zv_grad_ref[0, row, :, low : low + width] = grad_logit.astype(bf16)
            zv_grad_ref[0, row, :, high : high + width] = grad_value.astype(bf16)


def local_call(
    kernel, at, docs, ins, in_specs, out_shapes, out_specs, grid, scratch, aliases=None
):
    return pl.pallas_call(
        kernel,
        grid_spec=pltpu.PrefetchScalarGridSpec(
            num_scalar_prefetch=2,
            grid=grid,
            in_specs=in_specs,
            out_specs=out_specs,
            scratch_shapes=scratch,
        ),
        out_shape=out_shapes,
        input_output_aliases=aliases or {},
        compiler_params=pltpu.CompilerParams(
            dimension_semantics=("arbitrary",) * len(grid), vmem_limit_bytes=48 * 1024 * 1024
        ),
    )(at, docs, *ins)


def big_call(kernel, grid, ins, in_specs, out_shapes, out_specs):
    return pl.pallas_call(
        kernel,
        grid=grid,
        in_specs=in_specs,
        out_shape=out_shapes,
        out_specs=out_specs,
        compiler_params=pltpu.CompilerParams(
            dimension_semantics=("arbitrary",) * len(grid), vmem_limit_bytes=48 * 1024 * 1024
        ),
    )(*ins)


def up_kernel(in_ref, pair_ref, slope_ref, product_ref):
    rows = in_ref.shape[0] // 2
    units = pair_ref.shape[1] // 2
    cuts = [slice(0, rows), slice(rows, 2 * rows)]
    boths = [jnp.dot(in_ref[cut, :], pair_ref[...], preferred_element_type=f32) for cut in cuts]
    for cut, both in zip(cuts, boths):
        gate, up = both[:, :units], both[:, units:]
        gate_on = jax.nn.sigmoid(gate)
        active = gate * gate_on
        product_ref[cut, :] = (active * up).astype(bf16)
        slope_ref[0, cut, :] = up * (gate_on + active * (1.0 - gate_on))
        slope_ref[1, cut, :] = active


def down_kernel(grad_ref, down_ref, slope_ref, out_ref):
    rows = grad_ref.shape[0] // 2
    cuts = [slice(0, rows), slice(rows, 2 * rows)]
    grads = [jnp.dot(grad_ref[cut, :], down_ref[...], preferred_element_type=f32) for cut in cuts]
    for cut, grad in zip(cuts, grads):
        out_ref[cut, :] = jnp.concatenate(
            [grad * slope_ref[0, cut, :], grad * slope_ref[1, cut, :]], axis=-1
        ).astype(bf16)


def feed_up(mid_all, pair_all, tile):
    rows, features = mid_all.shape
    units = pair_all.shape[1]
    return big_call(
        up_kernel,
        (rows // tile,),
        (mid_all, pair_all),
        [
            pl.BlockSpec((tile, features), lambda i: (i, 0)),
            pl.BlockSpec((features, units), lambda i: (0, 0)),
        ],
        (
            jax.ShapeDtypeStruct((2, rows, units // 2), f32),
            jax.ShapeDtypeStruct((rows, units // 2), bf16),
        ),
        (
            pl.BlockSpec((2, tile, units // 2), lambda i: (0, i, 0)),
            pl.BlockSpec((tile, units // 2), lambda i: (i, 0)),
        ),
    )


def feed_back(grad_all, down_all, both, tile):
    rows, features = grad_all.shape
    units = 2 * both.shape[2]
    return big_call(
        down_kernel,
        (rows // tile,),
        (grad_all, down_all, both),
        [
            pl.BlockSpec((tile, features), lambda i: (i, 0)),
            pl.BlockSpec((features, units // 2), lambda i: (0, 0)),
            pl.BlockSpec((2, tile, units // 2), lambda i: (0, i, 0)),
        ],
        jax.ShapeDtypeStruct((rows, units), bf16),
        pl.BlockSpec((tile, units), lambda i: (i, 0)),
    )


def scatter_product(left, far_left, right, tile):
    depth = left.shape[1]
    columns = right.shape[1]
    half = columns // 2

    def dot(a_ref, b_ref):
        return jnp.dot(a_ref[...], b_ref[...], preferred_element_type=f32)

    def right_spec(side):
        return pl.BlockSpec((depth, half), lambda *_: (0, side))

    def far_kernel(a_ref, b_ref, out_ref):
        out_ref[...] = dot(a_ref, b_ref).astype(bf16)

    def far_part(side):
        return big_call(
            far_kernel,
            (4,),
            (far_left, right),
            [pl.BlockSpec((tile, depth), lambda i: (i, 0)), right_spec(side)],
            jax.ShapeDtypeStruct((4 * tile, half), bf16),
            pl.BlockSpec((tile, half), lambda i: (i, 0)),
        )

    def near_part(side, got):
        def kernel(a_ref, b_ref, got_ref, keep_ref, send_ref):
            value = dot(a_ref, b_ref) + got_ref[...].astype(f32)
            sent = pl.program_id(0) if side else pl.program_id(1)

            @pl.when(sent == 0)
            def _():
                keep_ref[0] = value

            @pl.when(sent == 1)
            def _():
                send_ref[0] = value.astype(bf16)

        if side:
            keep_at = lambda y, x: (jnp.where(y == 0, x, 1), 0, 0)
            send_at = lambda y, x: (jnp.where(y == 0, 0, x), 0, 0)
        else:
            keep_at = lambda y, x: (y, 0, 0)
            send_at = lambda y, x: (y, 0, 0)
        return big_call(
            kernel,
            (2, 2),
            (left, right, got),
            [
                pl.BlockSpec((tile, depth), lambda y, x: (2 * y + x, 0)),
                right_spec(side),
                pl.BlockSpec((tile, half), lambda y, x: (2 * y + x, 0)),
            ],
            (
                jax.ShapeDtypeStruct((2, tile, half), f32),
                jax.ShapeDtypeStruct((2, tile, half), bf16),
            ),
            (
                pl.BlockSpec((1, tile, half), keep_at),
                pl.BlockSpec((1, tile, half), send_at),
            ),
        )

    got = [swap_row(far_part(side)) for side in range(2)]
    (keep_left, to_x), (keep_right, to_y) = [near_part(side, got[side]) for side in range(2)]
    return keep_left, keep_right, to_x, to_y


def scatter_turned(left, right):
    half = left.shape[0] // 2
    far = times_transpose(left[half:], right).astype(bf16)
    near = times_transpose(left[:half], right)
    rows, columns = near.shape
    mine = (near + swap_row(far).astype(f32)).reshape(2, 2, rows // 4, columns)
    left_side, right_side = mine[..., : columns // 2], mine[..., columns // 2 :]
    return (
        left_side[:, 0],
        right_side[0],
        left_side[:, 1].astype(bf16),
        right_side[1].astype(bf16),
    )


def contract_rows(left, right):
    return lax.dot_general(left, right, (TN, ((), ())), preferred_element_type=f32)


def times_transpose(left, right):
    return lax.dot_general(left, right, (NT, ((), ())), preferred_element_type=f32)


def times(left, right):
    return jnp.dot(left, right, preferred_element_type=f32)


def rms_rate(values):
    return lax.rsqrt(jnp.mean(values * values, axis=-1, keepdims=True) + epsilon)


def rms_back(grad, values, rate):
    return rate * grad - values * (
        rate * rate * rate * jnp.mean(grad * values, axis=-1, keepdims=True)
    )


def on_device(
    block_input,
    out_grad,
    doc_starts,
    w_query,
    w_forget,
    w_input,
    w_outgate,
    w_out,
    w_gate,
    w_up,
    w_down,
    norm_gain,
    mlp_gain,
    group_gain,
    forget_bias,
):
    row_count, span, features = block_input.shape
    groups = lax.axis_size("z")
    own_row = lax.axis_index("row")
    own_spot = lax.axis_index("y") * 2 + lax.axis_index("x")
    own_first = own_row == 0
    spots, members = 4, 8
    tokens = row_count * span
    width = features // HEADS
    heads = HEADS // members
    wide = heads * width
    share = w_query.shape[0]
    units = w_gate.shape[1] // spots
    block = w_gate.shape[0]
    half = spots * tokens

    by_chip = 2 * share == width and groups == 2 * heads
    if by_chip:
        held = lax.all_gather(w_out, "z", axis=0, tiled=False).reshape(2, heads, share, features)
    else:
        held = lax.all_gather(w_out, everywhere, axis=0, tiled=True)

    def cut_heads(first, second):
        both = jnp.stack([first, second]).reshape(2, share, 2, heads, spots, width)
        return both.transpose(4, 2, 1, 0, 3, 5).reshape(members, share, 2 * wide)

    def over_group(cut):
        return lax.all_to_all(cut, group, 0, 0, tiled=True)

    def over_plane(cut):
        return lax.all_to_all(cut, plane, 0, 0, tiled=True)

    def over_groups(cut):
        flat = cut.reshape(cut.shape[0] * cut.shape[1], cut.shape[2])
        return lax.all_gather(flat, "z", axis=0, tiled=True)

    vectors = jnp.stack([norm_gain, mlp_gain, group_gain, forget_bias]).astype(f32)
    vectors = jnp.broadcast_to(vectors.reshape(1, 4 * share), (groups * members, 4 * share))
    vectors = lax.all_to_all(vectors, everywhere, 0, 0, tiled=True)
    mixer_cut, vectors = join(
        jnp.stack([cut_heads(w_forget, w_input), cut_heads(w_query, w_outgate)], axis=1), vectors
    )
    mixer_cut = over_group(mixer_cut)
    zv_all = over_groups(mixer_cut[:, 0])
    qr_all = over_groups(mixer_cut[:, 1])

    vectors = vectors.reshape(groups * members, 4, share).transpose(1, 0, 2).reshape(4, features)
    here = lax.dynamic_index_in_dim(
        vectors.reshape(4, 2, heads, spots, width), own_row, 1, False
    )
    here = lax.dynamic_index_in_dim(here, own_spot, 2, False).reshape(4, wide)
    first_gain, mid_gain = vectors[0:1], vectors[1:2]
    gain_here, bias_here = here[2:3], here[3:4]

    input_float = block_input.astype(f32).reshape(tokens, features)
    first_rate = rms_rate(input_float)
    normed = (input_float * first_rate * first_gain).astype(bf16)
    pair_cut = jnp.concatenate(
        [w_gate.reshape(block, spots, units), w_up.reshape(block, spots, units)], axis=-1
    ).transpose(1, 0, 2)
    down_cut = w_down.T.reshape(block, spots, units).transpose(1, 0, 2)

    normed, held = join(normed, held)
    first, pair_cut, down_cut = join(gather_first(normed), pair_cut, down_cut)
    normed_all = gather_last(gather_second(*first))

    docs = jnp.concatenate([doc_starts, swap_row(doc_starts)], axis=0)
    at = jnp.stack([own_spot, lax.axis_index("z") * (spots * span)]).astype(jnp.int32)
    by_block = (members, row_count, span)
    zv = times(normed_all, zv_all).reshape(by_block + (2 * wide,))
    zv, pair_cut, down_cut = join(zv, pair_cut, down_cut)
    pair_cut = over_plane(pair_cut)

    once = pl.BlockSpec((1, wide), lambda *_: (0, 0))
    packed_block = (row_count, heads, width + PAD, width)
    packed_shape = jax.ShapeDtypeStruct((2 * row_count,) + packed_block[1:], bf16)
    states = pltpu.VMEM((row_count, heads, width, width), f32)
    decays = pltpu.VMEM((row_count, heads, 1, width), f32)

    def slab(columns, index):
        return pl.BlockSpec((1, row_count, span, columns), index)

    def ahead(h, c, at_ref, docs_ref):
        return (h * spots + (c ^ at_ref[0]), 0, 0, 0)

    def behind(h, c, at_ref, docs_ref):
        return (h * spots + ((spots - 1 - c) ^ at_ref[0]), 0, 0, 0)

    by_half = pl.BlockSpec(packed_block, lambda h, c, at_ref, docs_ref: (h, 0, 0, 0))

    packed, logs = local_call(
        state_kernel,
        at,
        docs,
        (zv, bias_here),
        [slab(2 * wide, ahead), once],
        (packed_shape, jax.ShapeDtypeStruct(by_block + (wide,), f32)),
        (by_half, slab(wide, ahead)),
        (2, spots),
        (states, decays),
    )
    grad_low = out_grad.reshape(tokens, features)

    carried = []
    for step in range(groups - 1):
        packed = hop(packed, True)
        if step == 0:
            packed, pair_cut = join(packed, pair_cut.reshape(spots * block, 2 * units))
            grad_sent, down_cut, pair_cut = join(grad_low, down_cut, pair_cut)
            pair_all = lax.all_gather(pair_cut, "z", axis=0, tiled=True)
            near = gather_second(*gather_first(grad_sent))
            down_cut = over_plane(down_cut).reshape(spots * block, units)
        carried.append(packed)
    qr = times(normed_all, qr_all)
    carried, near, qr, down_cut = join(carried, near, qr, down_cut)
    down_all = lax.all_gather(down_cut, "z", axis=0, tiled=True)
    grad_all = gather_last(near)
    qr = qr.reshape(by_block + (2 * wide,))

    def forward_half(side, qr):
        def place(c, at_ref, docs_ref):
            return (side * spots + (c ^ at_ref[0]), 0, 0, 0)

        def local(c, at_ref, docs_ref):
            return (c ^ at_ref[0], 0, 0, 0)

        def kernel(*refs):
            forward_kernel(side, *refs)

        return local_call(
            kernel,
            at,
            docs,
            (qr, zv, logs, bias_here, gain_here, *carried),
            [slab(2 * wide, place), slab(2 * wide, place), slab(wide, place), once, once]
            + [pl.BlockSpec(packed_block, lambda c, at_ref, docs_ref: (side, 0, 0, 0))]
            * len(carried),
            (
                jax.ShapeDtypeStruct((spots,) + by_block[1:] + (wide,), f32),
                jax.ShapeDtypeStruct((spots,) + by_block[1:] + (wide,), bf16),
                jax.ShapeDtypeStruct((spots, row_count, heads, width, width), f32),
                jax.ShapeDtypeStruct((spots, row_count, heads, span, span), f32),
            ),
            (
                slab(wide, local),
                slab(wide, local),
                pl.BlockSpec(
                    (1, row_count, heads, width, width),
                    lambda c, at_ref, docs_ref: (c, 0, 0, 0, 0),
                ),
                pl.BlockSpec(
                    (1, row_count, heads, span, span),
                    lambda c, at_ref, docs_ref: (c, 0, 0, 0, 0),
                ),
            ),
            (spots,),
            (states,),
        )

    if by_chip:
        keep = lax.dynamic_index_in_dim(held, own_row, 0, False)
        give = lax.dynamic_index_in_dim(held, 1 - own_row, 0, False)
        take = swap_row(give)
        out_here = jnp.stack(
            [jnp.where(own_first, keep, take), jnp.where(own_first, take, keep)], axis=1
        ).reshape(wide, features)
    else:
        held = held.reshape(2, heads, spots, width, features)
        held = lax.dynamic_index_in_dim(held, own_row, 0, False)
        out_here = lax.dynamic_index_in_dim(held, own_spot, 1, False).reshape(wide, features)

    far_out, far_mixed, far_starts, far_scores = forward_half(1, qr)
    far_mixed = far_mixed.reshape(half, wide)
    near_out, near_mixed, near_starts, near_scores = forward_half(0, qr)
    near_mixed = near_mixed.reshape(half, wide)
    state = scatter_product(near_mixed, far_mixed, out_here, tokens)
    hidden = input_float + scatter_group(state)[0]

    mid_rate = rms_rate(hidden)
    first, grad_all, mixer_weights = join(
        gather_first((hidden * mid_rate * mid_gain).astype(bf16)),
        grad_all,
        jnp.concatenate([qr_all, zv_all], axis=1),
    )
    mid_all = gather_last(gather_second(*first))
    both, product = feed_up(mid_all, pair_all, tokens)

    def spread(partial):
        return lax.psum_scatter(partial.astype(bf16), "z", scatter_dimension=0, tiled=True)

    down_part = contract_rows(grad_all, product).astype(bf16)
    grad_down = spread(down_part)
    grad_both = feed_back(grad_all, down_all, both, tokens)
    state, mid_late, both_late, product = join(
        scatter_turned(grad_both, pair_all), mid_all, grad_both, product
    )
    pair_part = contract_rows(mid_late, both_late).astype(bf16)
    grad_mid, pair_part, grad_down = scatter_group(state, (pair_part,), (grad_down,))
    grad_pair = spread(pair_part)
    grad_float = out_grad.astype(f32).reshape(tokens, features)
    grad_hidden = grad_float + rms_back(grad_mid * mid_gain, hidden, mid_rate)

    first, sums = join(
        gather_first(grad_hidden.astype(bf16)),
        scatter_turned(product, down_all),
    )
    near_gm = lay(gather_second(*first))
    far_gm = swap_row(near_gm)
    sums = scatter_second(*join(sums, near_gm)[0])
    grad_mixed = jnp.concatenate(
        [times_transpose(near_gm, out_here), times_transpose(far_gm, out_here)], axis=0
    ).reshape(by_block + (wide,))
    mixer_out = jnp.concatenate([near_out, far_out], axis=0)
    starts = jnp.concatenate([near_starts, far_starts], axis=0)
    scores = jnp.concatenate([near_scores, far_scores], axis=0)
    scores_spec = pl.BlockSpec(
        (1, row_count, heads, span, span),
        lambda h, c, at_ref, docs_ref: (h * spots + spots - 1 - c, 0, 0, 0, 0),
    )
    starts_spec = pl.BlockSpec(
        (1, row_count, heads, width, width),
        lambda h, c, at_ref, docs_ref: (h * spots + spots - 1 - c, 0, 0, 0, 0),
    )
    all_grads, lows, parts, packed, slopes = local_call(
        open_kernel,
        at,
        docs,
        (qr, zv, logs, mixer_out, grad_mixed, bias_here, gain_here, starts),
        [
            slab(2 * wide, behind),
            slab(2 * wide, behind),
            slab(wide, behind),
            slab(wide, behind),
            slab(wide, behind),
            once,
            once,
            starts_spec,
        ],
        (
            jax.ShapeDtypeStruct(by_block + (4 * wide,), bf16),
            jax.ShapeDtypeStruct(by_block + (wide,), f32),
            jax.ShapeDtypeStruct(by_block + (wide,), f32),
            packed_shape,
            jax.ShapeDtypeStruct((2 * spots, row_count, heads, span, span), f32),
        ),
        (slab(2 * wide, behind), slab(wide, behind), slab(wide, behind), by_half, scores_spec),
        (2, spots),
        (states, decays),
    )
    packed, sums, near_late, far_late = join(packed, sums, near_gm, far_gm)

    def out_rows():
        rows = contract_rows(near_mixed, near_late) + contract_rows(far_mixed, far_late)
        return rows.astype(bf16)

    def query_part():
        qr_grads = all_grads.reshape(2 * half, 4 * wide)[:, : 2 * wide]
        return contract_rows(normed_all, qr_grads).astype(bf16)

    def turn_units(back):
        return back.transpose(0, 2, 1).reshape(spots * units, block).astype(f32)

    def pair_parts(back):
        return [
            jnp.concatenate(
                [back[spot, :, low : low + units].astype(f32) for spot in range(spots)], axis=1
            )
            for low in (0, units)
        ]

    packed, grad_down = join(packed, grad_down)
    down_back = over_plane(grad_down.reshape(spots, block, units))

    def beside(step):
        if step == 0:
            return (out_rows(), scatter_third(*sums), down_back)
        if step == 1:
            return (query_part(), turn_units(done[2]))
        return ()

    later = []
    done = []
    for step in range(groups - 1):
        packed, extra = join(hop(packed, False), beside(step))
        later.append(packed)
        done += extra
    grad_out_rows, sums, _, qr_part, grad_down = done
    later, grad_pair = join(later, grad_pair)
    pair_back = over_plane(grad_pair.reshape(spots, block, 2 * units))
    block_output = (hidden + scatter_last(*sums)).astype(bf16)
    if by_chip:
        cut = grad_out_rows.reshape(heads, 2, share, features)
        keep = lax.dynamic_index_in_dim(cut, own_row, 1, False)
        give = lax.dynamic_index_in_dim(cut, 1 - own_row, 1, False)
        take = swap_row(give)
        cut = jnp.concatenate(
            [jnp.where(own_first, keep, take), jnp.where(own_first, take, keep)], axis=0
        )
        grad_out = spread(cut.reshape(groups * share, features))
    else:
        placed = jnp.zeros((2, heads, spots, width, features), bf16)
        placed = lax.dynamic_update_slice(
            placed,
            grad_out_rows.reshape(1, heads, 1, width, features),
            (own_row, 0, own_spot, 0, 0),
        )
        grad_out = lax.psum_scatter(
            placed.reshape(features, features), everywhere, scatter_dimension=0, tiled=True
        )
    grad_qr = spread(qr_part)

    def behind_right(h, c, at_ref, docs_ref):
        return behind(h, c, at_ref, docs_ref)[:3] + (1,)

    all_grads, bias_part = local_call(
        close_kernel,
        at,
        docs,
        (all_grads, qr, zv, logs, lows, parts, bias_here, starts, scores, slopes, *later),
        [
            pl.BlockSpec(memory_space=pl.ANY),
            slab(2 * wide, behind),
            slab(2 * wide, behind),
            slab(wide, behind),
            slab(wide, behind),
            slab(wide, behind),
            once,
            starts_spec,
            scores_spec,
            scores_spec,
        ]
        + [by_half] * len(later),
        (
            jax.ShapeDtypeStruct(by_block + (4 * wide,), bf16),
            jax.ShapeDtypeStruct((1, wide), f32),
        ),
        (slab(2 * wide, behind_right), once),
        (2, spots),
        (states,),
        {2: 0},
    )
    all_grads, pair_back, grad_out = join(all_grads, pair_back, grad_out)
    all_grads = all_grads.reshape(2 * half, 4 * wide)
    zv_part = contract_rows(normed_all, all_grads[:, 2 * wide :]).astype(bf16)
    late_grads, zv_part = join(all_grads, zv_part)
    grad_zv = spread(zv_part)
    state = scatter_turned(late_grads, mixer_weights)
    bias_placed = jnp.zeros((2, heads, spots, width), f32)
    bias_placed = lax.dynamic_update_slice(
        bias_placed, bias_part.reshape(1, heads, 1, width), (own_row, 0, own_spot, 0)
    )
    bias_back = lax.all_to_all(
        bias_placed.reshape(groups * members, share), everywhere, 0, 0, tiled=True
    )
    grad_bias = jnp.sum(bias_back, axis=0)

    def join_heads(cut):
        back = cut.reshape(spots, 2, share, 2, heads, width)
        return [
            back[:, :, :, at].transpose(2, 1, 3, 0, 4).reshape(share, features).astype(f32)
            for at in range(2)
        ]

    state, block_output, grad_out, grad_qr = join(
        state, block_output, grad_out, over_group(grad_qr.reshape(members, share, 2 * wide))
    )
    grad_out = grad_out.astype(f32)
    state, (query_back, outgate_back), grad_out, block_output, (grad_gate, grad_up) = join(
        scatter_second(*state), join_heads(grad_qr), grad_out, block_output, pair_parts(pair_back)
    )
    state, grad_zv = join(scatter_sums(*state), grad_zv)
    state, (forget_back, input_back) = join(
        scatter_fourth(*state),
        join_heads(over_group(grad_zv.reshape(members, share, 2 * wide))),
    )
    grad_normed = scatter_last(*state)
    input_grad = grad_hidden + rms_back(grad_normed * first_gain, input_float, first_rate)
    input_grad = input_grad.astype(bf16).reshape(block_input.shape)

    own_vectors = (norm_gain.astype(f32), mlp_gain.astype(f32), group_gain.astype(f32))
    grad_head_gain = jnp.sum(grad_out * w_out.astype(f32), axis=1) / own_vectors[2]

    mid_part = jnp.sum(grad_gate * w_gate.astype(f32) + grad_up * w_up.astype(f32), axis=1)
    mid_part = mid_part.reshape(2, share)
    mid_keep = lax.dynamic_index_in_dim(mid_part, own_row, 0, False)
    mid_give = lax.dynamic_index_in_dim(mid_part, 1 - own_row, 0, False)
    grad_mid_gain = (mid_keep + swap_row(mid_give)) / own_vectors[1]

    first_part = query_back * w_query.astype(f32) + outgate_back * w_outgate.astype(f32)
    first_part += forget_back * w_forget.astype(f32) + input_back * w_input.astype(f32)
    grad_first_gain = jnp.sum(first_part, axis=1) / own_vectors[0]

    return (
        block_output.reshape(block_input.shape),
        input_grad,
        query_back,
        forget_back,
        input_back,
        outgate_back,
        grad_out,
        grad_gate,
        grad_up,
        grad_down,
        grad_first_gain,
        grad_mid_gain,
        grad_head_gain,
        grad_bias,
    )


def solution(mesh):
    count, rows = mesh.devices.shape
    folded = Mesh(mesh.devices.reshape(count // 4, 2, 2, rows), everywhere)
    seq = ("z", "y", "x")
    token_spec = P("row", seq, None)
    matrix_spec = P(everywhere, None)
    vector_spec = P(everywhere)
    wide_spec = P(seq, "row")
    tall_spec = P("row", seq)
    in_specs = (
        (token_spec, token_spec, P("row", None))
        + (matrix_spec,) * 5
        + (wide_spec, wide_spec, tall_spec)
        + (vector_spec,) * 4
    )
    out_specs = (
        (token_spec, token_spec)
        + (matrix_spec,) * 5
        + (wide_spec, wide_spec, tall_spec)
        + (vector_spec,) * 4
    )
    return jax.shard_map(
        on_device, mesh=folded, in_specs=in_specs, out_specs=out_specs, check_vma=False
    )
```

```python
import jax
import jax.numpy as jnp
from jax import lax
from jax.experimental import pallas as pl
from jax.experimental.pallas import tpu as pltpu
from jax.sharding import Mesh, PartitionSpec as P

HEADS = 16

lower_bound = 0.85
span_bound = 1.0 - lower_bound
epsilon = 1e-06
f32 = jnp.float32
bf16 = jnp.bfloat16
swap = ((0, 1), (1, 0))
everywhere = ("z", "y", "x", "row")
group = ("y", "x", "row")
plane = ("y", "x")


def swap_x(a):
    return lax.ppermute(a, "x", swap)


def swap_y(a):
    return lax.ppermute(a, "y", swap)


def swap_row(a):
    return lax.ppermute(a, "row", swap)


def join(*groups):
    flat, tree = jax.tree.flatten(groups)
    return jax.tree.unflatten(tree, lax.optimization_barrier(flat))


def gather_first(a):
    return a, swap_x(a), swap_y(a)


def gather_second(a, from_x, from_y):
    half = a.shape[0] // 2
    return a, from_x, from_y, swap_y(from_x[:half]), swap_x(from_y[half:])


def lay_kernel(*refs):
    pieces, out_ref = refs[:-1], refs[-1]
    rows = out_ref.shape[0]
    start = 0
    for ref in pieces:
        block, low = start // rows, start % rows

        @pl.when(pl.program_id(0) == block)
        def _(ref=ref, low=low):
            out_ref[low : low + ref.shape[0], :] = ref[...]

        start += ref.shape[0]


def lay(pieces):
    rows, columns = pieces[0].shape
    total = sum(piece.shape[0] for piece in pieces)
    return pl.pallas_call(
        lay_kernel,
        grid=(total // rows,),
        in_specs=[pl.BlockSpec(piece.shape, lambda step: (0, 0)) for piece in pieces],
        out_specs=pl.BlockSpec((rows, columns), lambda step: (step, 0)),
        out_shape=jax.ShapeDtypeStruct((total, columns), pieces[0].dtype),
        compiler_params=pltpu.CompilerParams(
            dimension_semantics=("arbitrary",), vmem_limit_bytes=48 * 1024 * 1024
        ),
    )(*pieces)


def gather_last(near):
    return lay(near + tuple(swap_row(piece) for piece in near))


def gather_group(a):
    return gather_last(gather_second(*gather_first(a)))


def scatter_second(left, right, to_x, to_y):
    return left, right, swap_x(to_x), swap_y(to_y)


def scatter_sums(left, right, from_x, from_y):
    left = left + from_x.astype(f32)
    right = right + from_y.astype(f32)
    return left[0], right[0], left[1].astype(bf16), right[1].astype(bf16)


def scatter_fourth(left, right, to_y, to_x):
    return left, right, swap_y(to_y), swap_x(to_x)


def scatter_third(*state):
    return scatter_fourth(*scatter_sums(*state))


def scatter_last(left, right, from_y, from_x):
    return jnp.concatenate([left + from_y.astype(f32), right + from_x.astype(f32)], axis=-1)


def scatter_group(state, first=(), second=()):
    state, first = join(scatter_second(*state), first)
    state, second = join(scatter_third(*state), second)
    return scatter_last(*state), *first, *second


def hop(packed, forward):
    count = lax.axis_size("z")
    if forward:
        pairs = [(i, i + 1) for i in range(count - 1)]
    else:
        pairs = [(i + 1, i) for i in range(count - 1)]
    return lax.ppermute(packed, "z", pairs)


def relay(packed, forward):
    got = []
    for _ in range(lax.axis_size("z") - 1):
        packed = hop(packed, forward)
        got.append(packed)
    return got


def pair(values):
    high = values.astype(bf16)
    return high, (values - high.astype(f32)).astype(bf16)


def mm(a, b, dims):
    def dot(left, right):
        return lax.dot_general(left, right, (dims, ((), ())), preferred_element_type=f32)

    return dot(a[0], b[0]) + (dot(a[0], b[1]) + dot(a[1], b[0]))


def split_sum(ones_matrix, values, dims):
    first = values.astype(bf16)
    rest = values - first.astype(f32)
    second = rest.astype(bf16)
    third = (rest - second.astype(f32)).astype(bf16)
    total = lax.dot_general(ones_matrix, first, (dims, ((), ())), preferred_element_type=f32)
    total += lax.dot_general(ones_matrix, second, (dims, ((), ())), preferred_element_type=f32)
    total += lax.dot_general(ones_matrix, third, (dims, ((), ())), preferred_element_type=f32)
    return total


NT = ((1,), (1,))
NN = ((1,), (0,))
TN = ((0,), (0,))


def chunk_masks(docs_ref, row_at, start, size):
    at_row = lax.broadcasted_iota(jnp.int32, (size, size), 0)
    at_col = lax.broadcasted_iota(jnp.int32, (size, size), 1)
    same = at_row >= at_col
    opened = at_row >= 0
    tail = at_row >= 0
    whole = jnp.bool_(True)
    for entry in range(docs_ref.shape[1]):
        place = docs_ref[row_at, entry] - start
        same = same & ~((at_col < place) & (place <= at_row))
        opened = opened & ~((0 <= place) & (place <= at_row))
        tail = tail & ~((at_row < place) & (place <= size - 1))
        whole = whole & ~((0 <= place) & (place <= size - 1))
    return same, opened, tail, whole


def key_of(logit):
    return span_bound * jax.nn.sigmoid(-logit)


def forget_of(logit):
    return lower_bound + span_bound * jax.nn.sigmoid(logit)


def lower_ones(size):
    at_row = lax.broadcasted_iota(jnp.int32, (size, size), 0)
    at_col = lax.broadcasted_iota(jnp.int32, (size, size), 1)
    return (at_row >= at_col).astype(f32).astype(bf16)


PAD = 16


def pack_state(ref, row, head, state, decay):
    width = state.shape[0]
    high = decay.astype(bf16).astype(f32)
    at_row = lax.broadcasted_iota(jnp.int32, (PAD, width), 0)
    extra = jnp.where(at_row == 0, high, jnp.where(at_row == 1, decay - high, 0.0))
    ref[row, head, :width, :] = state.astype(bf16)
    ref[row, head, width:, :] = extra.astype(bf16)


def unpack_carry(refs, row, head):
    width = refs[0].shape[3]
    carry = None
    for ref in refs[::-1]:
        state = ref[row, head, :width, :].astype(f32)
        if carry is not None:
            extra = ref[row, head, width:, :].astype(f32)
            state = state + (extra[0:1] + extra[1:2]) * carry
        carry = state
    return carry


def state_kernel(at_ref, docs_ref, zv_ref, bias_ref, packed_ref, logs_ref, state, decay):
    rows, size = zv_ref.shape[1:3]
    heads, width = state.shape[1:3]
    half, chunk = pl.program_id(0), pl.program_id(1)
    tri = lower_ones(size)

    @pl.when(chunk == 0)
    def _():
        state[...] = jnp.zeros_like(state)
        decay[...] = jnp.ones_like(decay)

    for row in range(rows):
        _, _, tail, whole = chunk_masks(
            docs_ref, half * rows + row, at_ref[1] + chunk * size, size
        )
        for head in range(heads):
            low = head * width
            logit = zv_ref[0, row, :, low : low + width] + bias_ref[:, low : low + width]
            value = zv_ref[0, row, :, heads * width + low : heads * width + low + width]
            key = key_of(logit)
            log_sum = split_sum(tri, jnp.log(forget_of(logit)), NN)
            logs_ref[0, row, :, low : low + width] = log_sum
            last = log_sum[size - 1 : size, :]
            passed = jnp.where(whole, jnp.exp(last), 0.0)
            weighted = jnp.where(tail, key * jnp.exp(last - log_sum), 0.0)
            state[row, head] = state[row, head] * passed + mm(pair(value), pair(weighted), TN)
            decay[row, head] = decay[row, head] * passed

    @pl.when(chunk == pl.num_programs(1) - 1)
    def _():
        for row in range(rows):
            for head in range(heads):
                pack_state(packed_ref, row, head, state[row, head], decay[row, head])


def forward_kernel(half, at_ref, docs_ref, qr_ref, zv_ref, logs_ref, bias_ref, gain_ref, *rest):
    carry_refs, (out_ref, mixed_ref, starts_ref, scores_ref, state) = rest[:-5], rest[-5:]
    rows, size = qr_ref.shape[1:3]
    heads, width = state.shape[1:3]
    chunk = pl.program_id(0)

    @pl.when(chunk == 0)
    def _():
        for row in range(rows):
            for head in range(heads):
                state[row, head] = unpack_carry(carry_refs, row, head)

    for row in range(rows):
        same, opened, tail, whole = chunk_masks(
            docs_ref, half * rows + row, at_ref[1] + chunk * size, size
        )
        for head in range(heads):
            low = head * width
            high = (heads + head) * width
            query = qr_ref[0, row, :, low : low + width]
            gate = qr_ref[0, row, :, high : high + width]
            logit = zv_ref[0, row, :, low : low + width] + bias_ref[:, low : low + width]
            value = pair(zv_ref[0, row, :, high : high + width])
            key = key_of(logit)
            log_sum = logs_ref[0, row, :, low : low + width]
            last = log_sum[size - 1 : size, :]
            lifted = pair(query * jax.nn.sigmoid(query) * jnp.exp(log_sum))
            lowered = pair(key * jnp.exp(-log_sum))
            scores = jnp.where(same, mm(lifted, lowered, NT), 0.0)
            scores_ref[0, row, head] = scores
            scores = pair(scores)
            begin = state[row, head]
            starts_ref[0, row, head] = begin
            out = mm(scores, value, NN) + jnp.where(opened, mm(lifted, pair(begin), NT), 0.0)
            passed = jnp.where(whole, jnp.exp(last), 0.0)
            weighted = jnp.where(tail, key * jnp.exp(last - log_sum), 0.0)
            state[row, head] = begin * passed + mm(value, pair(weighted), TN)
            scale = lax.rsqrt(jnp.mean(out * out, axis=-1, keepdims=True) + epsilon)
            normed = out * scale * gain_ref[:, low : low + width]
            out_ref[0, row, :, low : low + width] = out
            mixed_ref[0, row, :, low : low + width] = (
                normed * (gate * jax.nn.sigmoid(gate))
            ).astype(bf16)


def open_kernel(
    at_ref,
    docs_ref,
    qr_ref,
    zv_ref,
    logs_ref,
    out_ref,
    grad_ref,
    bias_ref,
    gain_ref,
    starts_ref,
    qr_grad_ref,
    low_ref,
    part_ref,
    packed_ref,
    slopes_ref,
    state,
    decay,
):
    rows, size = qr_ref.shape[1:3]
    heads, width = state.shape[1:3]
    half, step = pl.program_id(0), pl.program_id(1)
    chunk = pl.num_programs(1) - 1 - step

    @pl.when(step == 0)
    def _():
        state[...] = jnp.zeros_like(state)
        decay[...] = jnp.ones_like(decay)

    for row in range(rows):
        same, opened, _, whole = chunk_masks(
            docs_ref, half * rows + row, at_ref[1] + chunk * size, size
        )
        for head in range(heads):
            low = head * width
            high = (heads + head) * width
            query = qr_ref[0, row, :, low : low + width]
            gate = qr_ref[0, row, :, high : high + width]
            logit = zv_ref[0, row, :, low : low + width] + bias_ref[:, low : low + width]
            value = pair(zv_ref[0, row, :, high : high + width])
            out = out_ref[0, row, :, low : low + width]
            grad_mixed = grad_ref[0, row, :, low : low + width] * gain_ref[:, low : low + width]
            key = key_of(logit)
            log_sum = logs_ref[0, row, :, low : low + width]
            last = log_sum[size - 1 : size, :]
            rise = jnp.exp(log_sum)
            query_on = jax.nn.sigmoid(query)
            lifted = query * query_on * rise
            lowered = pair(key * jnp.exp(-log_sum))
            gate_on = jax.nn.sigmoid(gate)
            scale = lax.rsqrt(jnp.mean(out * out, axis=-1, keepdims=True) + epsilon)
            normed = out * scale
            grad_normed = grad_mixed * (gate * gate_on)
            grad_out = scale * (
                grad_normed - normed * jnp.mean(grad_normed * normed, axis=-1, keepdims=True)
            )
            grad_low = pair(grad_out)
            grad_scores = jnp.where(same, mm(grad_low, value, NT), 0.0)
            slopes_ref[0, row, head] = grad_scores
            grad_scores = pair(grad_scores)
            grad_lifted = mm(grad_scores, lowered, NN) + jnp.where(
                opened, mm(grad_low, pair(starts_ref[0, row, head]), NN), 0.0
            )
            grad_query = grad_lifted * rise * query_on * (1.0 + query * (1.0 - query_on))
            grad_gate = grad_mixed * normed * gate_on * (1.0 + gate * (1.0 - gate_on))
            qr_grad_ref[0, row, :, low : low + width] = grad_query.astype(bf16)
            qr_grad_ref[0, row, :, high : high + width] = grad_gate.astype(bf16)
            low_ref[0, row, :, low : low + width] = grad_out
            part_ref[0, row, :, low : low + width] = grad_lifted * lifted
            passed = jnp.where(whole, jnp.exp(last), 0.0)
            state[row, head] = state[row, head] * passed + mm(
                grad_low, pair(jnp.where(opened, lifted, 0.0)), TN
            )
            decay[row, head] = decay[row, head] * passed

    @pl.when(step == pl.num_programs(1) - 1)
    def _():
        for row in range(rows):
            for head in range(heads):
                pack_state(packed_ref, row, head, state[row, head], decay[row, head])


def close_kernel(
    at_ref,
    docs_ref,
    kept_ref,
    qr_ref,
    zv_ref,
    logs_ref,
    low_ref,
    part_ref,
    bias_ref,
    starts_ref,
    scores_ref,
    slopes_ref,
    *rest,
):
    carry_refs, (zv_grad_ref, bias_grad_ref, state) = rest[:-3], rest[-3:]
    rows, size = qr_ref.shape[1:3]
    heads, width = state.shape[1:3]
    half, step = pl.program_id(0), pl.program_id(1)
    chunk = pl.num_programs(1) - 1 - step
    tri = lower_ones(size)

    @pl.when((step == 0) & (half == 0))
    def _():
        bias_grad_ref[...] = jnp.zeros_like(bias_grad_ref)

    @pl.when(step == 0)
    def _():
        for row in range(rows):
            for head in range(heads):
                state[row, head] = unpack_carry(carry_refs, row, head)

    for row in range(rows):
        _, opened, tail, whole = chunk_masks(
            docs_ref, half * rows + row, at_ref[1] + chunk * size, size
        )
        for head in range(heads):
            low = head * width
            high = (heads + head) * width
            query = qr_ref[0, row, :, low : low + width]
            logit = zv_ref[0, row, :, low : low + width] + bias_ref[:, low : low + width]
            value = pair(zv_ref[0, row, :, high : high + width])
            grad_low = pair(low_ref[0, row, :, low : low + width])
            key = key_of(logit)
            log_sum = logs_ref[0, row, :, low : low + width]
            forget = forget_of(logit)
            last = log_sum[size - 1 : size, :]
            fall = jnp.exp(-log_sum)
            remain = jnp.where(tail, jnp.exp(last - log_sum), 0.0)
            lifted = query * jax.nn.sigmoid(query) * jnp.exp(log_sum)
            lowered = key * fall
            weighted = key * remain
            lifted_low = pair(lifted)
            scores = pair(scores_ref[0, row, head])
            begin = starts_ref[0, row, head]
            later = state[row, head]
            later_low = pair(later)
            grad_scores = pair(slopes_ref[0, row, head])
            grad_value = mm(scores, grad_low, TN) + mm(pair(weighted), later_low, NT)
            grad_lowered = mm(grad_scores, lifted_low, TN)
            grad_weighted = mm(value, later_low, NN)
            passed = jnp.where(whole, jnp.exp(last), 0.0)
            open_lifted = pair(jnp.where(opened, lifted, 0.0))
            state[row, head] = later * passed + mm(grad_low, open_lifted, TN)
            through = jnp.sum(begin * later, axis=0, keepdims=True) * passed
            weighted_part = grad_weighted * weighted
            grad_log = (
                part_ref[0, row, :, low : low + width]
                - grad_lowered * lowered
                - weighted_part
            )
            grad_last = through + jnp.sum(weighted_part, axis=0, keepdims=True)
            grad_step = split_sum(tri, grad_log, TN) + grad_last
            grad_key = grad_lowered * fall + grad_weighted * remain
            grad_logit = (
                span_bound
                * jax.nn.sigmoid(logit)
                * jax.nn.sigmoid(-logit)
                * (grad_step / forget - grad_key)
            )
            bias_grad_ref[:, low : low + width] += jnp.sum(grad_logit, axis=0, keepdims=True)
            zv_grad_ref[0, row, :, low : low + width] = grad_logit.astype(bf16)
            zv_grad_ref[0, row, :, high : high + width] = grad_value.astype(bf16)


def local_call(
    kernel, at, docs, ins, in_specs, out_shapes, out_specs, grid, scratch, aliases=None
):
    return pl.pallas_call(
        kernel,
        grid_spec=pltpu.PrefetchScalarGridSpec(
            num_scalar_prefetch=2,
            grid=grid,
            in_specs=in_specs,
            out_specs=out_specs,
            scratch_shapes=scratch,
        ),
        out_shape=out_shapes,
        input_output_aliases=aliases or {},
        compiler_params=pltpu.CompilerParams(
            dimension_semantics=("arbitrary",) * len(grid), vmem_limit_bytes=48 * 1024 * 1024
        ),
    )(at, docs, *ins)


def big_call(kernel, grid, ins, in_specs, out_shapes, out_specs):
    return pl.pallas_call(
        kernel,
        grid=grid,
        in_specs=in_specs,
        out_shape=out_shapes,
        out_specs=out_specs,
        compiler_params=pltpu.CompilerParams(
            dimension_semantics=("arbitrary",) * len(grid), vmem_limit_bytes=48 * 1024 * 1024
        ),
    )(*ins)


def up_kernel(in_ref, pair_ref, slope_ref, product_ref):
    rows = in_ref.shape[0] // 2
    units = pair_ref.shape[1] // 2
    cuts = [slice(0, rows), slice(rows, 2 * rows)]
    boths = [jnp.dot(in_ref[cut, :], pair_ref[...], preferred_element_type=f32) for cut in cuts]
    for cut, both in zip(cuts, boths):
        gate, up = both[:, :units], both[:, units:]
        gate_on = jax.nn.sigmoid(gate)
        active = gate * gate_on
        product_ref[cut, :] = (active * up).astype(bf16)
        slope_ref[0, cut, :] = up * (gate_on + active * (1.0 - gate_on))
        slope_ref[1, cut, :] = active


def down_kernel(grad_ref, down_ref, slope_ref, out_ref):
    rows = grad_ref.shape[0] // 2
    cuts = [slice(0, rows), slice(rows, 2 * rows)]
    grads = [jnp.dot(grad_ref[cut, :], down_ref[...], preferred_element_type=f32) for cut in cuts]
    for cut, grad in zip(cuts, grads):
        out_ref[cut, :] = jnp.concatenate(
            [grad * slope_ref[0, cut, :], grad * slope_ref[1, cut, :]], axis=-1
        ).astype(bf16)


def feed_up(mid_all, pair_all, tile):
    rows, features = mid_all.shape
    units = pair_all.shape[1]
    return big_call(
        up_kernel,
        (rows // tile,),
        (mid_all, pair_all),
        [
            pl.BlockSpec((tile, features), lambda i: (i, 0)),
            pl.BlockSpec((features, units), lambda i: (0, 0)),
        ],
        (
            jax.ShapeDtypeStruct((2, rows, units // 2), f32),
            jax.ShapeDtypeStruct((rows, units // 2), bf16),
        ),
        (
            pl.BlockSpec((2, tile, units // 2), lambda i: (0, i, 0)),
            pl.BlockSpec((tile, units // 2), lambda i: (i, 0)),
        ),
    )


def feed_back(grad_all, down_all, both, tile):
    rows, features = grad_all.shape
    units = 2 * both.shape[2]
    return big_call(
        down_kernel,
        (rows // tile,),
        (grad_all, down_all, both),
        [
            pl.BlockSpec((tile, features), lambda i: (i, 0)),
            pl.BlockSpec((features, units // 2), lambda i: (0, 0)),
            pl.BlockSpec((2, tile, units // 2), lambda i: (0, i, 0)),
        ],
        jax.ShapeDtypeStruct((rows, units), bf16),
        pl.BlockSpec((tile, units), lambda i: (i, 0)),
    )


def scatter_product(left, far_left, right, tile):
    depth = left.shape[1]
    columns = right.shape[1]
    half = columns // 2

    def dot(a_ref, b_ref):
        return jnp.dot(a_ref[...], b_ref[...], preferred_element_type=f32)

    def right_spec(side):
        return pl.BlockSpec((depth, half), lambda *_: (0, side))

    def far_kernel(a_ref, b_ref, out_ref):
        out_ref[...] = dot(a_ref, b_ref).astype(bf16)

    def far_part(side):
        return big_call(
            far_kernel,
            (4,),
            (far_left, right),
            [pl.BlockSpec((tile, depth), lambda i: (i, 0)), right_spec(side)],
            jax.ShapeDtypeStruct((4 * tile, half), bf16),
            pl.BlockSpec((tile, half), lambda i: (i, 0)),
        )

    def near_part(side, got):
        def kernel(a_ref, b_ref, got_ref, keep_ref, send_ref):
            value = dot(a_ref, b_ref) + got_ref[...].astype(f32)
            sent = pl.program_id(0) if side else pl.program_id(1)

            @pl.when(sent == 0)
            def _():
                keep_ref[0] = value

            @pl.when(sent == 1)
            def _():
                send_ref[0] = value.astype(bf16)

        if side:
            keep_at = lambda y, x: (jnp.where(y == 0, x, 1), 0, 0)
            send_at = lambda y, x: (jnp.where(y == 0, 0, x), 0, 0)
        else:
            keep_at = lambda y, x: (y, 0, 0)
            send_at = lambda y, x: (y, 0, 0)
        return big_call(
            kernel,
            (2, 2),
            (left, right, got),
            [
                pl.BlockSpec((tile, depth), lambda y, x: (2 * y + x, 0)),
                right_spec(side),
                pl.BlockSpec((tile, half), lambda y, x: (2 * y + x, 0)),
            ],
            (
                jax.ShapeDtypeStruct((2, tile, half), f32),
                jax.ShapeDtypeStruct((2, tile, half), bf16),
            ),
            (
                pl.BlockSpec((1, tile, half), keep_at),
                pl.BlockSpec((1, tile, half), send_at),
            ),
        )

    got = [swap_row(far_part(side)) for side in range(2)]
    (keep_left, to_x), (keep_right, to_y) = [near_part(side, got[side]) for side in range(2)]
    return keep_left, keep_right, to_x, to_y


def scatter_turned(left, right):
    half = left.shape[0] // 2
    far = times_transpose(left[half:], right).astype(bf16)
    near = times_transpose(left[:half], right)
    rows, columns = near.shape
    mine = (near + swap_row(far).astype(f32)).reshape(2, 2, rows // 4, columns)
    left_side, right_side = mine[..., : columns // 2], mine[..., columns // 2 :]
    return (
        left_side[:, 0],
        right_side[0],
        left_side[:, 1].astype(bf16),
        right_side[1].astype(bf16),
    )


def contract_rows(left, right):
    return lax.dot_general(left, right, (TN, ((), ())), preferred_element_type=f32)


def times_transpose(left, right):
    return lax.dot_general(left, right, (NT, ((), ())), preferred_element_type=f32)


def times(left, right):
    return jnp.dot(left, right, preferred_element_type=f32)


def rms_rate(values):
    return lax.rsqrt(jnp.mean(values * values, axis=-1, keepdims=True) + epsilon)


def rms_back(grad, values, rate):
    return rate * grad - values * (
        rate * rate * rate * jnp.mean(grad * values, axis=-1, keepdims=True)
    )


def on_device(
    block_input,
    out_grad,
    doc_starts,
    w_query,
    w_forget,
    w_input,
    w_outgate,
    w_out,
    w_gate,
    w_up,
    w_down,
    norm_gain,
    mlp_gain,
    group_gain,
    forget_bias,
):
    row_count, span, features = block_input.shape
    groups = lax.axis_size("z")
    own_row = lax.axis_index("row")
    own_spot = lax.axis_index("y") * 2 + lax.axis_index("x")
    own_first = own_row == 0
    spots, members = 4, 8
    tokens = row_count * span
    width = features // HEADS
    heads = HEADS // members
    wide = heads * width
    share = w_query.shape[0]
    units = w_gate.shape[1] // spots
    block = w_gate.shape[0]
    half = spots * tokens

    by_chip = 2 * share == width and groups == 2 * heads
    if by_chip:
        held = lax.all_gather(w_out, "z", axis=0, tiled=False).reshape(2, heads, share, features)
    else:
        held = lax.all_gather(w_out, everywhere, axis=0, tiled=True)

    def cut_heads(first, second):
        both = jnp.stack([first, second]).reshape(2, share, 2, heads, spots, width)
        return both.transpose(4, 2, 1, 0, 3, 5).reshape(members, share, 2 * wide)

    def over_group(cut):
        return lax.all_to_all(cut, group, 0, 0, tiled=True)

    def over_plane(cut):
        return lax.all_to_all(cut, plane, 0, 0, tiled=True)

    def over_groups(cut):
        flat = cut.reshape(cut.shape[0] * cut.shape[1], cut.shape[2])
        return lax.all_gather(flat, "z", axis=0, tiled=True)

    vectors = jnp.stack([norm_gain, mlp_gain, group_gain, forget_bias]).astype(f32)
    vectors = jnp.broadcast_to(vectors.reshape(1, 4 * share), (groups * members, 4 * share))
    vectors = lax.all_to_all(vectors, everywhere, 0, 0, tiled=True)
    mixer_cut, vectors = join(
        jnp.stack([cut_heads(w_forget, w_input), cut_heads(w_query, w_outgate)], axis=1), vectors
    )
    mixer_cut = over_group(mixer_cut)
    zv_all = over_groups(mixer_cut[:, 0])
    qr_all = over_groups(mixer_cut[:, 1])

    vectors = vectors.reshape(groups * members, 4, share).transpose(1, 0, 2).reshape(4, features)
    here = lax.dynamic_index_in_dim(
        vectors.reshape(4, 2, heads, spots, width), own_row, 1, False
    )
    here = lax.dynamic_index_in_dim(here, own_spot, 2, False).reshape(4, wide)
    first_gain, mid_gain = vectors[0:1], vectors[1:2]
    gain_here, bias_here = here[2:3], here[3:4]

    input_float = block_input.astype(f32).reshape(tokens, features)
    first_rate = rms_rate(input_float)
    normed = (input_float * first_rate * first_gain).astype(bf16)
    pair_cut = jnp.concatenate(
        [w_gate.reshape(block, spots, units), w_up.reshape(block, spots, units)], axis=-1
    ).transpose(1, 0, 2)
    down_cut = w_down.T.reshape(block, spots, units).transpose(1, 0, 2)

    normed, held = join(normed, held)
    first, pair_cut, down_cut = join(gather_first(normed), pair_cut, down_cut)
    normed_all = gather_last(gather_second(*first))

    docs = jnp.concatenate([doc_starts, swap_row(doc_starts)], axis=0)
    at = jnp.stack([own_spot, lax.axis_index("z") * (spots * span)]).astype(jnp.int32)
    by_block = (members, row_count, span)
    zv = times(normed_all, zv_all).reshape(by_block + (2 * wide,))
    zv, pair_cut, down_cut = join(zv, pair_cut, down_cut)
    pair_cut = over_plane(pair_cut)

    once = pl.BlockSpec((1, wide), lambda *_: (0, 0))
    packed_block = (row_count, heads, width + PAD, width)
    packed_shape = jax.ShapeDtypeStruct((2 * row_count,) + packed_block[1:], bf16)
    states = pltpu.VMEM((row_count, heads, width, width), f32)
    decays = pltpu.VMEM((row_count, heads, 1, width), f32)

    def slab(columns, index):
        return pl.BlockSpec((1, row_count, span, columns), index)

    def ahead(h, c, at_ref, docs_ref):
        return (h * spots + (c ^ at_ref[0]), 0, 0, 0)

    def behind(h, c, at_ref, docs_ref):
        return (h * spots + ((spots - 1 - c) ^ at_ref[0]), 0, 0, 0)

    by_half = pl.BlockSpec(packed_block, lambda h, c, at_ref, docs_ref: (h, 0, 0, 0))

    packed, logs = local_call(
        state_kernel,
        at,
        docs,
        (zv, bias_here),
        [slab(2 * wide, ahead), once],
        (packed_shape, jax.ShapeDtypeStruct(by_block + (wide,), f32)),
        (by_half, slab(wide, ahead)),
        (2, spots),
        (states, decays),
    )
    grad_low = out_grad.reshape(tokens, features)

    carried = []
    for step in range(groups - 1):
        packed = hop(packed, True)
        if step == 0:
            packed, pair_cut = join(packed, pair_cut.reshape(spots * block, 2 * units))
            grad_sent, down_cut, pair_cut = join(grad_low, down_cut, pair_cut)
            pair_all = lax.all_gather(pair_cut, "z", axis=0, tiled=True)
            near = gather_second(*gather_first(grad_sent))
            down_cut = over_plane(down_cut).reshape(spots * block, units)
        carried.append(packed)
    qr = times(normed_all, qr_all)
    carried, near, qr, down_cut = join(carried, near, qr, down_cut)
    down_all = lax.all_gather(down_cut, "z", axis=0, tiled=True)
    grad_all = gather_last(near)
    qr = qr.reshape(by_block + (2 * wide,))

    def forward_half(side, qr):
        def place(c, at_ref, docs_ref):
            return (side * spots + (c ^ at_ref[0]), 0, 0, 0)

        def local(c, at_ref, docs_ref):
            return (c ^ at_ref[0], 0, 0, 0)

        def kernel(*refs):
            forward_kernel(side, *refs)

        return local_call(
            kernel,
            at,
            docs,
            (qr, zv, logs, bias_here, gain_here, *carried),
            [slab(2 * wide, place), slab(2 * wide, place), slab(wide, place), once, once]
            + [pl.BlockSpec(packed_block, lambda c, at_ref, docs_ref: (side, 0, 0, 0))]
            * len(carried),
            (
                jax.ShapeDtypeStruct((spots,) + by_block[1:] + (wide,), f32),
                jax.ShapeDtypeStruct((spots,) + by_block[1:] + (wide,), bf16),
                jax.ShapeDtypeStruct((spots, row_count, heads, width, width), f32),
                jax.ShapeDtypeStruct((spots, row_count, heads, span, span), f32),
            ),
            (
                slab(wide, local),
                slab(wide, local),
                pl.BlockSpec(
                    (1, row_count, heads, width, width),
                    lambda c, at_ref, docs_ref: (c, 0, 0, 0, 0),
                ),
                pl.BlockSpec(
                    (1, row_count, heads, span, span),
                    lambda c, at_ref, docs_ref: (c, 0, 0, 0, 0),
                ),
            ),
            (spots,),
            (states,),
        )

    if by_chip:
        keep = lax.dynamic_index_in_dim(held, own_row, 0, False)
        give = lax.dynamic_index_in_dim(held, 1 - own_row, 0, False)
        take = swap_row(give)
        out_here = jnp.stack(
            [jnp.where(own_first, keep, take), jnp.where(own_first, take, keep)], axis=1
        ).reshape(wide, features)
    else:
        held = held.reshape(2, heads, spots, width, features)
        held = lax.dynamic_index_in_dim(held, own_row, 0, False)
        out_here = lax.dynamic_index_in_dim(held, own_spot, 1, False).reshape(wide, features)

    far_out, far_mixed, far_starts, far_scores = forward_half(1, qr)
    far_mixed = far_mixed.reshape(half, wide)
    near_out, near_mixed, near_starts, near_scores = forward_half(0, qr)
    near_mixed = near_mixed.reshape(half, wide)
    state = scatter_product(near_mixed, far_mixed, out_here, tokens)
    hidden = input_float + scatter_group(state)[0]

    mid_rate = rms_rate(hidden)
    first, grad_all, mixer_weights = join(
        gather_first((hidden * mid_rate * mid_gain).astype(bf16)),
        grad_all,
        jnp.concatenate([qr_all, zv_all], axis=1),
    )
    mid_all = gather_last(gather_second(*first))
    both, product = feed_up(mid_all, pair_all, tokens)

    def spread(partial):
        return lax.psum_scatter(partial.astype(bf16), "z", scatter_dimension=0, tiled=True)

    down_part = contract_rows(grad_all, product).astype(bf16)
    grad_down = spread(down_part)
    grad_both = feed_back(grad_all, down_all, both, tokens)
    state, mid_late, both_late, product = join(
        scatter_turned(grad_both, pair_all), mid_all, grad_both, product
    )
    pair_part = contract_rows(mid_late, both_late).astype(bf16)
    grad_mid, pair_part, grad_down = scatter_group(state, (pair_part,), (grad_down,))
    grad_pair = spread(pair_part)
    grad_float = out_grad.astype(f32).reshape(tokens, features)
    grad_hidden = grad_float + rms_back(grad_mid * mid_gain, hidden, mid_rate)

    first, sums = join(
        gather_first(grad_hidden.astype(bf16)),
        scatter_turned(product, down_all),
    )
    near_gm = lay(gather_second(*first))
    far_gm = swap_row(near_gm)
    sums = scatter_second(*join(sums, near_gm)[0])
    grad_mixed = jnp.concatenate(
        [times_transpose(near_gm, out_here), times_transpose(far_gm, out_here)], axis=0
    ).reshape(by_block + (wide,))
    mixer_out = jnp.concatenate([near_out, far_out], axis=0)
    starts = jnp.concatenate([near_starts, far_starts], axis=0)
    scores = jnp.concatenate([near_scores, far_scores], axis=0)
    scores_spec = pl.BlockSpec(
        (1, row_count, heads, span, span),
        lambda h, c, at_ref, docs_ref: (h * spots + spots - 1 - c, 0, 0, 0, 0),
    )
    starts_spec = pl.BlockSpec(
        (1, row_count, heads, width, width),
        lambda h, c, at_ref, docs_ref: (h * spots + spots - 1 - c, 0, 0, 0, 0),
    )
    all_grads, lows, parts, packed, slopes = local_call(
        open_kernel,
        at,
        docs,
        (qr, zv, logs, mixer_out, grad_mixed, bias_here, gain_here, starts),
        [
            slab(2 * wide, behind),
            slab(2 * wide, behind),
            slab(wide, behind),
            slab(wide, behind),
            slab(wide, behind),
            once,
            once,
            starts_spec,
        ],
        (
            jax.ShapeDtypeStruct(by_block + (4 * wide,), bf16),
            jax.ShapeDtypeStruct(by_block + (wide,), f32),
            jax.ShapeDtypeStruct(by_block + (wide,), f32),
            packed_shape,
            jax.ShapeDtypeStruct((2 * spots, row_count, heads, span, span), f32),
        ),
        (slab(2 * wide, behind), slab(wide, behind), slab(wide, behind), by_half, scores_spec),
        (2, spots),
        (states, decays),
    )
    packed, sums, near_late, far_late = join(packed, sums, near_gm, far_gm)

    def out_rows():
        rows = contract_rows(near_mixed, near_late) + contract_rows(far_mixed, far_late)
        return rows.astype(bf16)

    def query_part():
        qr_grads = all_grads.reshape(2 * half, 4 * wide)[:, : 2 * wide]
        return contract_rows(normed_all, qr_grads).astype(bf16)

    def turn_units(back):
        return back.transpose(0, 2, 1).reshape(spots * units, block).astype(f32)

    def pair_parts(back):
        return [
            jnp.concatenate(
                [back[spot, :, low : low + units].astype(f32) for spot in range(spots)], axis=1
            )
            for low in (0, units)
        ]

    packed, grad_down = join(packed, grad_down)
    down_back = over_plane(grad_down.reshape(spots, block, units))

    def beside(step):
        if step == 0:
            return (out_rows(), scatter_third(*sums), down_back)
        if step == 1:
            return (query_part(), turn_units(done[2]))
        return ()

    later = []
    done = []
    for step in range(groups - 1):
        packed, extra = join(hop(packed, False), beside(step))
        later.append(packed)
        done += extra
    grad_out_rows, sums, _, qr_part, grad_down = done
    later, grad_pair = join(later, grad_pair)
    pair_back = over_plane(grad_pair.reshape(spots, block, 2 * units))
    block_output = (hidden + scatter_last(*sums)).astype(bf16)
    if by_chip:
        cut = grad_out_rows.reshape(heads, 2, share, features)
        keep = lax.dynamic_index_in_dim(cut, own_row, 1, False)
        give = lax.dynamic_index_in_dim(cut, 1 - own_row, 1, False)
        take = swap_row(give)
        cut = jnp.concatenate(
            [jnp.where(own_first, keep, take), jnp.where(own_first, take, keep)], axis=0
        )
        grad_out = spread(cut.reshape(groups * share, features))
    else:
        placed = jnp.zeros((2, heads, spots, width, features), bf16)
        placed = lax.dynamic_update_slice(
            placed,
            grad_out_rows.reshape(1, heads, 1, width, features),
            (own_row, 0, own_spot, 0, 0),
        )
        grad_out = lax.psum_scatter(
            placed.reshape(features, features), everywhere, scatter_dimension=0, tiled=True
        )
    grad_qr = spread(qr_part)

    def behind_right(h, c, at_ref, docs_ref):
        return behind(h, c, at_ref, docs_ref)[:3] + (1,)

    all_grads, bias_part = local_call(
        close_kernel,
        at,
        docs,
        (all_grads, qr, zv, logs, lows, parts, bias_here, starts, scores, slopes, *later),
        [
            pl.BlockSpec(memory_space=pl.ANY),
            slab(2 * wide, behind),
            slab(2 * wide, behind),
            slab(wide, behind),
            slab(wide, behind),
            slab(wide, behind),
            once,
            starts_spec,
            scores_spec,
            scores_spec,
        ]
        + [by_half] * len(later),
        (
            jax.ShapeDtypeStruct(by_block + (4 * wide,), bf16),
            jax.ShapeDtypeStruct((1, wide), f32),
        ),
        (slab(2 * wide, behind_right), once),
        (2, spots),
        (states,),
        {2: 0},
    )
    all_grads, pair_back, grad_out = join(all_grads, pair_back, grad_out)
    all_grads = all_grads.reshape(2 * half, 4 * wide)
    zv_part = contract_rows(normed_all, all_grads[:, 2 * wide :]).astype(bf16)
    late_grads, zv_part = join(all_grads, zv_part)
    grad_zv = spread(zv_part)
    state = scatter_turned(late_grads, mixer_weights)
    bias_placed = jnp.zeros((2, heads, spots, width), f32)
    bias_placed = lax.dynamic_update_slice(
        bias_placed, bias_part.reshape(1, heads, 1, width), (own_row, 0, own_spot, 0)
    )
    bias_back = lax.all_to_all(
        bias_placed.reshape(groups * members, share), everywhere, 0, 0, tiled=True
    )
    grad_bias = jnp.sum(bias_back, axis=0)

    def join_heads(cut):
        back = cut.reshape(spots, 2, share, 2, heads, width)
        return [
            back[:, :, :, at].transpose(2, 1, 3, 0, 4).reshape(share, features).astype(f32)
            for at in range(2)
        ]

    state, block_output, grad_out, grad_qr = join(
        state, block_output, grad_out, over_group(grad_qr.reshape(members, share, 2 * wide))
    )
    grad_out = grad_out.astype(f32)
    state, grad_out, block_output, (grad_gate, grad_up) = join(
        scatter_second(*state), grad_out, block_output, pair_parts(pair_back)
    )
    state, grad_zv, grad_qr = join(scatter_sums(*state), grad_zv, grad_qr)
    state, (query_back, outgate_back), (forget_back, input_back) = join(
        scatter_fourth(*state),
        join_heads(grad_qr),
        join_heads(over_group(grad_zv.reshape(members, share, 2 * wide))),
    )
    grad_normed = scatter_last(*state)
    input_grad = grad_hidden + rms_back(grad_normed * first_gain, input_float, first_rate)
    input_grad = input_grad.astype(bf16).reshape(block_input.shape)

    own_vectors = (norm_gain.astype(f32), mlp_gain.astype(f32), group_gain.astype(f32))
    grad_head_gain = jnp.sum(grad_out * w_out.astype(f32), axis=1) / own_vectors[2]

    mid_part = jnp.sum(grad_gate * w_gate.astype(f32) + grad_up * w_up.astype(f32), axis=1)
    mid_part = mid_part.reshape(2, share)
    mid_keep = lax.dynamic_index_in_dim(mid_part, own_row, 0, False)
    mid_give = lax.dynamic_index_in_dim(mid_part, 1 - own_row, 0, False)
    grad_mid_gain = (mid_keep + swap_row(mid_give)) / own_vectors[1]

    first_part = query_back * w_query.astype(f32) + outgate_back * w_outgate.astype(f32)
    first_part += forget_back * w_forget.astype(f32) + input_back * w_input.astype(f32)
    grad_first_gain = jnp.sum(first_part, axis=1) / own_vectors[0]

    return (
        block_output.reshape(block_input.shape),
        input_grad,
        query_back,
        forget_back,
        input_back,
        outgate_back,
        grad_out,
        grad_gate,
        grad_up,
        grad_down,
        grad_first_gain,
        grad_mid_gain,
        grad_head_gain,
        grad_bias,
    )


def solution(mesh):
    count, rows = mesh.devices.shape
    folded = Mesh(mesh.devices.reshape(count // 4, 2, 2, rows), everywhere)
    seq = ("z", "y", "x")
    token_spec = P("row", seq, None)
    matrix_spec = P(everywhere, None)
    vector_spec = P(everywhere)
    wide_spec = P(seq, "row")
    tall_spec = P("row", seq)
    in_specs = (
        (token_spec, token_spec, P("row", None))
        + (matrix_spec,) * 5
        + (wide_spec, wide_spec, tall_spec)
        + (vector_spec,) * 4
    )
    out_specs = (
        (token_spec, token_spec)
        + (matrix_spec,) * 5
        + (wide_spec, wide_spec, tall_spec)
        + (vector_spec,) * 4
    )
    return jax.shard_map(
        on_device, mesh=folded, in_specs=in_specs, out_specs=out_specs, check_vma=False
    )
```
